256 devices in a mesh: grp: 32 (over x, z), head: 8 (over y, core).
Axes of the slice: x: 4, y: 4, z: 8, core: 2. Of those that a mesh axis runs over, the one named last changes fastest.
Arguments:
- grid_in: bfloat16 [112, 65536], P(None, ('grp', 'head')), may hold values from -6 to 6
- mesh_embed: bfloat16 [32768, 1024], P(('grp', 'head')), may hold values from -6 to 6
- enc_src: int32 [16, 32768], P(None, ('grp', 'head')), may hold values from 0 to 255
- enc_len: int32 [32768], P(('grp', 'head')), may hold values from 1 to 16
- enc_kv_weight: bfloat16 [112, 2048], replicated, may hold values from -0.5 to 0.5
- proc_gain: float32 [1024], replicated, may hold values from 0.1 to 1.9
- qkv_weight: bfloat16 [1024, 3, 1024], P(None, None, 'head'), may hold values from -0.1875 to 0.1875
- out_weight: bfloat16 [1024, 1024], P('head'), may hold values from -0.1875 to 0.1875
- dec_gain: float32 [1024], replicated, may hold values from 0.1 to 1.9
- unpack_pair_projector: bfloat16 [1024, 2048], replicated, may hold values from -0.1875 to 0.1875
- readout_asking_coefficients: bfloat16 [112, 1024], replicated, may hold values from -0.5 to 0.5
- readout_final_coefficients: bfloat16 [100, 1024], replicated, may hold values from -0.1875 to 0.1875
- dec_send: int32 [8192, 32], P(('grp', 'head')), may hold values from 0 to 127
- dec_src: int32 [3, 65536], P(None, ('grp', 'head')), may hold values from 0 to 1023
- dforecast: bfloat16 [100, 65536], P(None, ('grp', 'head')), may hold values from -6 to 6
Outputs:
- estimated_atmosphere: float32 [100, 65536], P(None, ('grp', 'head'))
- vertex_derivative: float32 [32768, 1024], P(('grp', 'head'))
The draws below stay inside these ranges and needn't reach their ends.
Inputs may be any that keep to these rules, and one draw needn't show every extreme that they name: `enc_src`: each encoder edge of a mesh node names a grid point of the same block. Edges e < enc_len[m] of node m are live. `dec_send`: row (g * 8 + h) * 32 + t lists, slot by slot, the local mesh rows that block g * 8 + h sends to grid block t * 8 + h. `dec_src`: slot r = g * 32 + s of a grid block t * 8 + h is slot s of what block g * 8 + h sends to it.
All inputs are finite; a program needn't handle non-finite values.
Results may differ from the reference program's by a relative error of at most 0.019.
Values may be sent and summed in bfloat16 or wider, within the bound.
A program may use at most 128 MiB of HBM per device.

```python
import jax
import jax.numpy as jnp
from jax import lax

C = 1024
NH = 16
HEAD_WIDTH = 64
V = 112
PROGNOSTIC_FIELDS = 100
MESH_DEV = 128
GP_DEV = 256
ENC_K = 16
DEC_K = 3
DSLOTS = 32
WIN = 256
GRAPH_VERTICES = 32768
LATTICE_SITES = 65536
PAIRS = 8192
N_GRP = 32
N_HEAD = 8


def with_ends(drawn, rng, low, largest):
    dims = drawn.shape
    place = [jax.random.randint(jax.random.fold_in(rng, axis), (), 0, dims[axis]) for axis in range(len(dims))]
    drawn = drawn.at[tuple(place)].set(low)
    longest = dims.index(max(dims))
    place[longest] = (place[longest] + 1) % dims[longest]
    return drawn.at[tuple(place)].set(largest)


def block_scale(own_key, extent, cuts, least, top_value):
    loudness = 1.0
    for axis_at, blocks in cuts:
        heights = jax.random.uniform(jax.random.fold_in(jax.random.fold_in(own_key, 6), axis_at), (blocks,), jnp.float32, least / len(cuts), top_value / len(cuts))
        loudness = loudness * jnp.repeat(jnp.exp(heights), extent[axis_at] // blocks).reshape((-1,) + (1,) * (len(extent) - 1 - axis_at))
    return loudness


def bell_draw(own_key, dims, deviation, limit, shards=(), held_as=jnp.bfloat16):
    level = block_scale(own_key, dims, shards, -0.22, 0.18) if shards else 1.0
    values = jax.random.normal(own_key, dims, jnp.float32) * deviation * level
    return jnp.minimum(jnp.maximum(values, -limit), limit).astype(held_as)


def setup_inputs(seed: int = 0) -> dict:
    key_list = jax.random.split(jax.random.key(seed), 16)
    grid_in = bell_draw(key_list[0], (V, LATTICE_SITES), 1.0, 6.0, ((1, 256),))
    mesh_embed = bell_draw(key_list[1], (GRAPH_VERTICES, C), 1.0, 6.0, ((0, 256),))
    enc_src = with_ends(jax.random.randint(key_list[2], (ENC_K, GRAPH_VERTICES), 0, GP_DEV), jax.random.fold_in(key_list[2], 1), 0, GP_DEV - 1).astype(jnp.int32)
    enc_len = with_ends(jax.random.randint(key_list[3], (GRAPH_VERTICES,), 1, ENC_K + 1), jax.random.fold_in(key_list[3], 1), 1, ENC_K).astype(jnp.int32)
    enc_kv_weight = bell_draw(key_list[4], (V, 2 * C), V ** -0.5, 0.5)
    proc_gain = jnp.clip(1.0 + 0.18 * jax.random.normal(key_list[5], (C,), jnp.float32), 0.1, 1.9)
    qkv_weight = bell_draw(key_list[6], (C, 3, C), C ** -0.5, 0.1875, ((2, 8),))
    out_weight = bell_draw(key_list[7], (C, C), C ** -0.5, 0.1875, ((0, 8),))
    dec_gain = jnp.clip(1.0 + 0.18 * jax.random.normal(key_list[8], (C,), jnp.float32), 0.1, 1.9)
    unpack_pair_projector = bell_draw(key_list[9], (C, 2 * C), C ** -0.5, 0.1875)
    readout_asking_coefficients = bell_draw(key_list[10], (V, C), V ** -0.5, 0.5)
    readout_final_coefficients = bell_draw(key_list[11], (PROGNOSTIC_FIELDS, C), C ** -0.5, 0.1875)
    dec_send = with_ends(jax.random.randint(key_list[12], (PAIRS, DSLOTS), 0, MESH_DEV), jax.random.fold_in(key_list[12], 1), 0, MESH_DEV - 1).astype(jnp.int32)
    dec_src = with_ends(jax.random.randint(key_list[13], (DEC_K, LATTICE_SITES), 0, N_GRP * DSLOTS), jax.random.fold_in(key_list[13], 1), 0, (N_GRP * DSLOTS) - 1).astype(jnp.int32)
    dforecast = bell_draw(key_list[14], (PROGNOSTIC_FIELDS, LATTICE_SITES), 1.0, 6.0, ((1, 256),))
    return {"grid_in": grid_in, "mesh_embed": mesh_embed, "enc_src": enc_src, "enc_len": enc_len, "enc_kv_weight": enc_kv_weight, "proc_gain": proc_gain, "qkv_weight": qkv_weight, "out_weight": out_weight, "dec_gain": dec_gain, "unpack_pair_projector": unpack_pair_projector, "readout_asking_coefficients": readout_asking_coefficients, "readout_final_coefficients": readout_final_coefficients, "dec_send": dec_send, "dec_src": dec_src, "dforecast": dforecast}


EPS = 1e-05

def norm_rows(rows, gain):
    row_mean = lax.optimization_barrier(jnp.mean(rows, axis=-1, keepdims=True))
    centred = rows - row_mean
    spread = lax.optimization_barrier(jnp.mean(centred * centred, axis=-1, keepdims=True))
    inverse = lax.rsqrt(spread + EPS)
    unit_rows = centred * inverse
    return (unit_rows * gain, unit_rows, inverse)

def norm_back(grad_rows, unit_rows, inverse, gain):
    scaled = grad_rows * gain
    first_mean = lax.optimization_barrier(jnp.mean(scaled, axis=-1, keepdims=True))
    second_mean = lax.optimization_barrier(jnp.mean(scaled * unit_rows, axis=-1, keepdims=True))
    return inverse * (scaled - first_mean - unit_rows * second_mean)

def encode_block(lattice_fields, embed_rows, sender_vertices, counts, kv_weight):
    entry_extent = embed_rows.shape[1]
    node_count = embed_rows.shape[0]
    fan_in = sender_vertices.shape[0]
    grid_kv = lax.dot_general(lattice_fields, kv_weight, (((0,), (0,)), ((), ())), preferred_element_type=jnp.float32).astype(jnp.bfloat16)
    edge_rows = grid_kv[sender_vertices]
    key_portion = edge_rows[..., :entry_extent].astype(jnp.float32).reshape(fan_in, node_count, NH, HEAD_WIDTH)
    value_portion = edge_rows[..., entry_extent:].astype(jnp.float32).reshape(fan_in, node_count, NH, HEAD_WIDTH)
    query_rows = embed_rows.astype(jnp.float32).reshape(node_count, NH, HEAD_WIDTH)
    score_matrix = jnp.einsum('tfl,otfl->otf', query_rows, key_portion) * HEAD_WIDTH ** (-0.5)
    is_live = lax.broadcasted_iota(jnp.int32, (fan_in, node_count), 0) < counts[None, :]
    masked_scores = jnp.where(is_live[..., None], score_matrix, -jnp.inf)
    row_top = lax.optimization_barrier(jnp.max(masked_scores, axis=0, keepdims=True))
    exp_terms = jnp.exp(masked_scores - row_top)
    softmax_weight = (exp_terms / lax.optimization_barrier(jnp.sum(exp_terms, axis=0, keepdims=True))).astype(jnp.bfloat16)
    blended_rows = jnp.einsum('xcu,xcut->cut', softmax_weight.astype(jnp.float32), value_portion)
    return embed_rows.astype(jnp.float32) + blended_rows.reshape(node_count, entry_extent)

def window_attention_all(qkv):
    total_rows = qkv.shape[0]
    entry_extent = qkv.shape[2]
    block_rows = min(512, MESH_DEV * N_HEAD)
    query_rows = qkv[:, 0].reshape(total_rows, NH, HEAD_WIDTH)
    key_all = jnp.pad(qkv[:, 1], ((WIN, WIN), (0, 0))).reshape(total_rows + 2 * WIN, NH, HEAD_WIDTH)
    value_all = jnp.pad(qkv[:, 2], ((WIN, WIN), (0, 0))).reshape(total_rows + 2 * WIN, NH, HEAD_WIDTH)

    def attend_block(start_row):
        query_block = lax.dynamic_slice_in_dim(query_rows, start_row, block_rows, 0).astype(jnp.float32)
        key_block = lax.dynamic_slice_in_dim(key_all, start_row, block_rows + 2 * WIN, 0).astype(jnp.float32)
        value_block = lax.dynamic_slice_in_dim(value_all, start_row, block_rows + 2 * WIN, 0).astype(jnp.float32)
        score_matrix = jnp.einsum('qhd,khd->hqk', query_block, key_block) * HEAD_WIDTH ** (-0.5)
        query_pos = start_row + lax.broadcasted_iota(jnp.int32, (block_rows, 1), 0)
        key_pos = start_row - WIN + lax.broadcasted_iota(jnp.int32, (1, block_rows + 2 * WIN), 1)
        pos_gap = query_pos - key_pos
        is_live = (pos_gap <= WIN) & (pos_gap >= -WIN) & (key_pos >= 0) & (key_pos < total_rows)
        masked_scores = jnp.where(is_live[None], score_matrix, -jnp.inf)
        row_top = lax.optimization_barrier(jnp.max(masked_scores, axis=-1, keepdims=True))
        exp_terms = jnp.exp(masked_scores - row_top)
        softmax_weight = (exp_terms / lax.optimization_barrier(jnp.sum(exp_terms, axis=-1, keepdims=True))).astype(jnp.bfloat16)
        blended_rows = jnp.einsum('hqk,khd->qhd', softmax_weight.astype(jnp.float32), value_block)
        return blended_rows.reshape(block_rows, entry_extent).astype(jnp.bfloat16)
    starts = jnp.arange(total_rows // block_rows, dtype=jnp.int32) * block_rows
    return lax.map(attend_block, starts).reshape(total_rows, entry_extent)

def readout_tile(lattice_fields, neighbour_pairing, sender_vertices, q_weight, readout_result, upstream_derivative):
    point_count = lattice_fields.shape[1]
    entry_extent = q_weight.shape[1]
    fan_in = sender_vertices.shape[0]
    score_scale = HEAD_WIDTH ** (-0.5)
    query_rows = lax.dot_general(lattice_fields, q_weight, (((0,), (0,)), ((), ())), preferred_element_type=jnp.float32).astype(jnp.bfloat16)
    query_f = query_rows.astype(jnp.float32).reshape(point_count, NH, HEAD_WIDTH)
    edge_rows = neighbour_pairing[sender_vertices]
    key_portion = edge_rows[..., :entry_extent].astype(jnp.float32).reshape(fan_in, point_count, NH, HEAD_WIDTH)
    value_portion = edge_rows[..., entry_extent:].astype(jnp.float32).reshape(fan_in, point_count, NH, HEAD_WIDTH)
    score_matrix = jnp.einsum('pnd,epnd->epn', query_f, key_portion) * score_scale
    row_top = lax.optimization_barrier(jnp.max(score_matrix, axis=0, keepdims=True))
    exp_terms = jnp.exp(score_matrix - row_top)
    softmax_weight = exp_terms / lax.optimization_barrier(jnp.sum(exp_terms, axis=0, keepdims=True))
    rounded = lax.optimization_barrier(softmax_weight.astype(jnp.bfloat16)).astype(jnp.float32)
    blended_rows = jnp.einsum('epn,epnd->pnd', rounded, value_portion)
    result_lines = blended_rows.reshape(point_count, entry_extent).astype(jnp.bfloat16)
    estimated_atmosphere = lattice_fields[:PROGNOSTIC_FIELDS].astype(jnp.float32) + lax.dot_general(readout_result, result_lines, (((1,), (1,)), ((), ())), preferred_element_type=jnp.float32)
    back_grad = lax.dot_general(upstream_derivative, readout_result, (((0,), (0,)), ((), ())), preferred_element_type=jnp.float32).reshape(point_count, NH, HEAD_WIDTH)
    along_value = jnp.einsum('pnd,epnd->epn', back_grad, value_portion)
    score_grad = softmax_weight * (along_value - lax.optimization_barrier(jnp.sum(softmax_weight * along_value, axis=0, keepdims=True)))
    key_grad = score_grad[..., None] * query_f * score_scale
    value_grad = rounded[..., None] * back_grad
    edge_grad = jnp.concatenate([key_grad.reshape(fan_in, point_count, entry_extent), value_grad.reshape(fan_in, point_count, entry_extent)], axis=-1)
    adjacent_sensitivity = jax.ops.segment_sum(edge_grad.reshape(fan_in * point_count, 2 * entry_extent), sender_vertices.reshape(fan_in * point_count), num_segments=neighbour_pairing.shape[0])
    return (estimated_atmosphere, adjacent_sensitivity)

def reference(grid_in, mesh_embed, enc_src, enc_len, enc_kv_weight, proc_gain, qkv_weight, out_weight, dec_gain, unpack_pair_projector, readout_asking_coefficients, readout_final_coefficients, dec_send, dec_src, dforecast):
    blocks = N_GRP * N_HEAD
    entry_extent = mesh_embed.shape[1]
    lookup_positions = jnp.arange(blocks, dtype=jnp.int32)

    def encode_step(block_index):
        lattice_fields = lax.dynamic_slice_in_dim(grid_in, block_index * GP_DEV, GP_DEV, 1)
        embed_rows = lax.dynamic_slice_in_dim(mesh_embed, block_index * MESH_DEV, MESH_DEV, 0)
        sender_vertices = lax.dynamic_slice_in_dim(enc_src, block_index * MESH_DEV, MESH_DEV, 1)
        counts = lax.dynamic_slice_in_dim(enc_len, block_index * MESH_DEV, MESH_DEV, 0)
        return encode_block(lattice_fields, embed_rows, sender_vertices, counts, enc_kv_weight)
    hidden = lax.map(encode_step, lookup_positions).reshape(GRAPH_VERTICES, entry_extent)
    normed, _, _ = norm_rows(hidden, proc_gain)
    normed_in = normed.astype(jnp.bfloat16)
    qkv = jnp.dot(normed_in, qkv_weight.reshape(entry_extent, 3 * entry_extent), preferred_element_type=jnp.float32).astype(jnp.bfloat16).reshape(GRAPH_VERTICES, 3, entry_extent)
    attended = window_attention_all(qkv)
    part_width = entry_extent // N_HEAD
    projected = jnp.zeros((GRAPH_VERTICES, entry_extent), jnp.float32)
    for head_group in range(N_HEAD):
        part_term = jnp.dot(attended[:, head_group * part_width:(head_group + 1) * part_width], out_weight[head_group * part_width:(head_group + 1) * part_width], preferred_element_type=jnp.float32)
        projected = projected + lax.optimization_barrier(part_term.astype(jnp.bfloat16)).astype(jnp.float32)
    state_rows = hidden + projected
    dec_norm, unit_rows, inverse = norm_rows(state_rows, dec_gain)
    dec_in = dec_norm.astype(jnp.bfloat16)
    mesh_kv = jnp.dot(dec_in, unpack_pair_projector, preferred_element_type=jnp.float32).astype(jnp.bfloat16)
    slot_count = N_GRP * DSLOTS
    slot_index = jnp.arange(slot_count, dtype=jnp.int32)

    def readout_update(running_carried_tuple, block_index):
        home_grp = block_index // N_HEAD
        home_head = block_index % N_HEAD
        source_block = slot_index // DSLOTS * N_HEAD + home_head
        send_table = dec_send[source_block * N_GRP + home_grp, slot_index % DSLOTS]
        corner_elements = source_block * MESH_DEV + send_table
        neighbour_pairing = mesh_kv[corner_elements]
        lattice_fields = lax.dynamic_slice_in_dim(grid_in, block_index * GP_DEV, GP_DEV, 1)
        sender_vertices = lax.dynamic_slice_in_dim(dec_src, block_index * GP_DEV, GP_DEV, 1)
        upstream_derivative = lax.dynamic_slice_in_dim(dforecast, block_index * GP_DEV, GP_DEV, 1)
        estimated_atmosphere, adjacent_sensitivity = readout_tile(lattice_fields, neighbour_pairing, sender_vertices, readout_asking_coefficients, readout_final_coefficients, upstream_derivative)
        element_terms_list = lax.dot_general(adjacent_sensitivity.astype(jnp.bfloat16), unpack_pair_projector, (((1,), (1,)), ((), ())), preferred_element_type=jnp.float32)
        return (running_carried_tuple.at[corner_elements].add(element_terms_list), estimated_atmosphere)
    entry_derivative, prediction_lines = lax.scan(readout_update, jnp.zeros((GRAPH_VERTICES, entry_extent), jnp.float32), lookup_positions)
    estimated_atmosphere = jnp.transpose(prediction_lines, (1, 0, 2)).reshape(PROGNOSTIC_FIELDS, LATTICE_SITES)
    vertex_derivative = norm_back(entry_derivative, unit_rows, inverse, dec_gain)
    return (estimated_atmosphere, vertex_derivative)
```

```python
import jax
import jax.numpy as jnp
from jax import lax
from jax.experimental import pallas as pl
from jax.experimental.pallas import tpu as pltpu
from jax.sharding import PartitionSpec as P

F32 = jnp.float32
BF = jnp.bfloat16
EPS = 1e-05
SCALE = 0.125


def nn(a, b):
    return lax.dot_general(a, b, (((1,), (0,)), ((), ())), preferred_element_type=F32)


def nt(a, b):
    return lax.dot_general(a, b, (((1,), (1,)), ((), ())), preferred_element_type=F32)


def tn(a, b):
    return lax.dot_general(a, b, (((0,), (0,)), ((), ())), preferred_element_type=F32)


def half_masks():
    lane = lax.broadcasted_iota(jnp.int32, (1, 128), 1)
    return [(lane < 64).astype(F32).astype(BF), (lane >= 64).astype(F32).astype(BF)]


def norm_rows(rows):
    row_mean = jnp.mean(rows, axis=-1, keepdims=True)
    centred = rows - row_mean
    spread = jnp.mean(centred * centred, axis=-1, keepdims=True)
    inverse = lax.rsqrt(spread + EPS)
    return centred * inverse, inverse


def encode(grid_ref, emb_ref, src_ref, len_ref, wkv_ref, hid_ref):
    points = grid_ref.shape[1]
    nodes = emb_ref.shape[0]
    pid = lax.broadcasted_iota(jnp.int32, (points, nodes), 0)
    count = jnp.zeros((points, nodes), F32)
    lens = len_ref[...]
    for e in range(src_ref.shape[0]):
        row = jnp.where(e < lens, src_ref[e : e + 1, :], -1)
        count += (pid == row).astype(F32)
    dead = jnp.where(count > 0, 0.0, -jnp.inf)
    grid_t = grid_ref[...].T
    masks = half_masks()

    def pair(j, _):
        cols = pl.ds(pl.multiple_of(j * 128, 128), 128)
        vcols = pl.ds(pl.multiple_of(j * 128 + 1024, 128), 128)
        keys = nn(grid_t, wkv_ref[:, cols]).astype(BF)
        values = nn(grid_t, wkv_ref[:, vcols]).astype(BF)
        emb = emb_ref[:, cols]
        weights = []
        for n in range(2):
            score = nt(keys, emb * masks[n]) * SCALE + dead
            top = jnp.max(score, axis=0, keepdims=True)
            term = jnp.exp(score - top) * count
            weights.append((term / jnp.sum(term, axis=0, keepdims=True)).astype(BF))
        mixed = tn(weights[0], values * masks[0]) + tn(weights[1], values * masks[1])
        hid_ref[:, cols] = emb.astype(F32) + mixed
        return 0

    lax.fori_loop(0, emb_ref.shape[1] // 128, pair, 0)


def attend(q_ref, k_ref, v_ref, out_ref, blk, low, high):
    masks = half_masks()
    rows = pl.ds(blk * 256, 256)
    span = pl.ds(blk * 256, 768)
    q = q_ref[rows, :]
    k = k_ref[span, :]
    v = v_ref[span, :]
    gap = lax.broadcasted_iota(jnp.int32, (256, 768), 1) - lax.broadcasted_iota(
        jnp.int32, (256, 768), 0
    )
    col = lax.broadcasted_iota(jnp.int32, (256, 768), 1)
    live = (gap >= 0) & (gap <= 512) & (col >= low) & (col < high)
    total = None
    for n in range(2):
        score = jnp.where(live, nt(q * masks[n], k), -jnp.inf)
        top = jnp.max(score, axis=1, keepdims=True)
        term = jnp.exp(score - top)
        part = nn(term.astype(BF), v * masks[n]) / jnp.sum(term, axis=1, keepdims=True)
        total = part if total is None else total + part
    out_ref[rows, :] = total.astype(BF)


def encode_kernel(grid_ref, emb_ref, src_ref, len_ref, wkv_ref, gain_ref, hid_ref, norm_ref):
    encode(grid_ref, emb_ref, src_ref, len_ref, wkv_ref, hid_ref)
    unit, _ = norm_rows(hid_ref[...])
    norm_ref[...] = (unit * gain_ref[...]).astype(BF)


def attend_kernel(q_ref, k_ref, v_ref, out_ref):
    g = lax.axis_index("grp")
    for blk in range(4):
        low = jnp.where(g == 0, 256, 0) if blk == 0 else 0
        high = jnp.where(g == lax.axis_size("grp") - 1, 512, 768) if blk == 3 else 768
        attend(q_ref, k_ref, v_ref, out_ref, blk, low, high)


def head_sum():
    row = lax.broadcasted_iota(jnp.int32, (1024, 128), 0) // 64
    col = lax.broadcasted_iota(jnp.int32, (1024, 128), 1)
    return (row == col).astype(F32).astype(BF)


def head_spread():
    row = lax.broadcasted_iota(jnp.int32, (128, 1024), 0)
    col = lax.broadcasted_iota(jnp.int32, (128, 1024), 1) // 64
    return (row == col).astype(F32).astype(BF)


def decode(grid_ref, dfc_ref, srct_ref, src_ref, wq_ref, wf_ref, u_ref, slot_ref, est_ref, back_ref, xe, kv, bg, rg):
    pts = 256
    lane = lax.broadcasted_iota(jnp.int32, (pts, 1024), 1)
    for e in range(3):
        pick = (srct_ref[:, e : e + 1] == lane).astype(F32).astype(BF)

        def gather(j, _):
            cols = pl.ds(pl.multiple_of(j * 256, 256), 256)
            xe[e * pts : (e + 1) * pts, cols] = nn(pick, slot_ref[:, cols]).astype(BF)
            return 0

        lax.fori_loop(0, 4, gather, 0)

    def project(j, _):
        cols = pl.ds(pl.multiple_of(j * 256, 256), 256)
        kv[:, cols] = nn(xe[...], u_ref[:, cols]).astype(BF)
        return 0

    lax.fori_loop(0, 8, project, 0)
    query = tn(grid_ref[...], wq_ref[...]).astype(BF)
    bg[...] = tn(dfc_ref[...], wf_ref[...])
    hsum = head_sum()
    spread = head_spread()
    qf = query.astype(F32)
    score, along = [], []
    for e in range(3):
        rows = slice(e * pts, (e + 1) * pts)
        score.append(nn((qf * kv[rows, :1024].astype(F32)).astype(BF), hsum) * SCALE)
        along.append(nn((bg[...] * kv[rows, 1024:].astype(F32)).astype(BF), hsum))
    top = jnp.maximum(jnp.maximum(score[0], score[1]), score[2])
    term = [jnp.exp(s - top) for s in score]
    total = term[0] + term[1] + term[2]
    weight = [t / total for t in term]
    mean = weight[0] * along[0] + weight[1] * along[1] + weight[2] * along[2]
    mix = jnp.zeros((pts, 1024), F32)
    for e in range(3):
        rows = slice(e * pts, (e + 1) * pts)
        wide = nn(weight[e].astype(BF), spread)
        mix += wide * kv[rows, 1024:].astype(F32)
        grad = nn((weight[e] * (along[e] - mean) * SCALE).astype(BF), spread)
        kv[rows, :1024] = (grad * qf).astype(BF)
        kv[rows, 1024:] = (wide * bg[...]).astype(BF)
    est_ref[...] = grid_ref[0:100, :].astype(F32) + nt(wf_ref[...], mix.astype(BF))

    def unproject(j, _):
        cols = pl.ds(pl.multiple_of(j * 256, 256), 256)
        rg[:, cols] = nt(kv[...], u_ref[cols, :]).astype(BF)
        return 0

    lax.fori_loop(0, 4, unproject, 0)

    def scatter(j, _):
        rows = pl.ds(pl.multiple_of(j * 128, 128), 128)
        sub = lax.broadcasted_iota(jnp.int32, (128, pts), 0) + j * 128
        pick = jnp.concatenate(
            [(src_ref[e : e + 1, :] == sub).astype(F32).astype(BF) for e in range(3)], axis=1
        )
        back_ref[rows, :] = nn(pick, rg[...]).astype(BF)
        return 0

    lax.fori_loop(0, 8, scatter, 0)


def with_halo(cells, width):
    count = lax.axis_size("grp")
    head = cells[:width]
    tail = cells[-width:]
    return jnp.concatenate(
        [
            lax.ppermute(tail, "grp", [(i, (i + 1) % count) for i in range(count - 1)]),
            cells,
            lax.ppermute(head, "grp", [((i + 1) % count, i) for i in range(count - 1)]),
        ],
        axis=0,
    )


VM = pl.BlockSpec(memory_space=pltpu.VMEM)


def body(
    grid_in, mesh_embed, enc_src, enc_len, enc_kv_weight, proc_gain, qkv_weight, out_weight,
    dec_gain, unpack, wq, wf, dec_send, dec_src, dforecast,
):
    params = pltpu.CompilerParams(vmem_limit_bytes=50 * 2**20)
    hidden, normed_in = pl.pallas_call(
        encode_kernel,
        out_shape=(
            jax.ShapeDtypeStruct((128, 1024), F32),
            jax.ShapeDtypeStruct((128, 1024), BF),
        ),
        in_specs=[VM] * 6,
        out_specs=(VM, VM),
        compiler_params=params,
    )(grid_in, mesh_embed, enc_src, enc_len.reshape(1, -1), enc_kv_weight, proc_gain.reshape(1, -1))
    triple = jnp.dot(
        lax.all_gather(normed_in, "head", axis=0, tiled=True),
        qkv_weight.reshape(1024, 384),
        preferred_element_type=F32,
    ).astype(BF)
    query = triple[:, :128] * SCALE
    extended = with_halo(triple[:, 128:], 256)
    attended = pl.pallas_call(
        attend_kernel,
        out_shape=jax.ShapeDtypeStruct((1024, 128), BF),
        in_specs=[VM] * 3,
        out_specs=VM,
        compiler_params=params,
    )(query, extended[:, :128], extended[:, 128:])
    projected = lax.psum_scatter(
        jnp.dot(attended, out_weight, preferred_element_type=F32).astype(BF),
        "head", scatter_dimension=0, tiled=True,
    ).astype(F32)
    unit, inverse = norm_rows(hidden + projected)
    dec_in = (unit * dec_gain).astype(BF)
    flat = dec_send.reshape(-1)
    pick = (flat[:, None] == jnp.arange(128)[None, :]).astype(BF)
    sent = jnp.dot(pick, dec_in, preferred_element_type=F32).astype(BF)
    arrived = lax.all_to_all(sent.reshape(32, 32, 1024), "grp", 0, 0, tiled=True).reshape(1024, 1024)
    estimated, back = pl.pallas_call(
        decode,
        out_shape=(
            jax.ShapeDtypeStruct((100, 256), F32),
            jax.ShapeDtypeStruct((1024, 1024), BF),
        ),
        in_specs=[VM] * 8,
        out_specs=(VM, VM),
        scratch_shapes=[
            pltpu.VMEM((768, 1024), BF),
            pltpu.VMEM((768, 2048), BF),
            pltpu.VMEM((256, 1024), F32),
            pltpu.VMEM((768, 1024), BF),
        ],
        compiler_params=params,
    )(grid_in, dforecast, dec_src.T, dec_src, wq, wf, unpack, arrived)
    returned = lax.all_to_all(back.reshape(32, 32, 1024), "grp", 0, 0, tiled=True).reshape(1024, 1024)
    place = (jnp.arange(128)[:, None] == flat[None, :]).astype(BF)
    entry = jnp.dot(place, returned, preferred_element_type=F32)
    scaled = entry * dec_gain
    first = jnp.mean(scaled, axis=-1, keepdims=True)
    second = jnp.mean(scaled * unit, axis=-1, keepdims=True)
    return estimated, inverse * (scaled - first - unit * second)


def solution(mesh):
    return jax.shard_map(
        body,
        mesh=mesh,
        in_specs=(
            P(None, ("grp", "head")), P(("grp", "head"), None), P(None, ("grp", "head")),
            P(("grp", "head")), P(), P(), P(None, None, "head"), P("head", None), P(), P(), P(), P(),
            P(("grp", "head"), None), P(None, ("grp", "head")), P(None, ("grp", "head")),
        ),
        out_specs=(P(None, ("grp", "head")), P(("grp", "head"), None)),
        check_vma=False,
    )
```

```python
import jax
import jax.numpy as jnp
from jax import lax
from jax.experimental import pallas as pl
from jax.experimental.pallas import tpu as pltpu
from jax.sharding import PartitionSpec as P

F32 = jnp.float32
BF = jnp.bfloat16
EPS = 1e-05
SCALE = 0.125


def nn(a, b):
    return lax.dot_general(a, b, (((1,), (0,)), ((), ())), preferred_element_type=F32)


def nt(a, b):
    return lax.dot_general(a, b, (((1,), (1,)), ((), ())), preferred_element_type=F32)


def tn(a, b):
    return lax.dot_general(a, b, (((0,), (0,)), ((), ())), preferred_element_type=F32)


def half_masks():
    lane = lax.broadcasted_iota(jnp.int32, (1, 128), 1)
    return [(lane < 64).astype(F32).astype(BF), (lane >= 64).astype(F32).astype(BF)]


def norm_rows(rows):
    row_mean = jnp.mean(rows, axis=-1, keepdims=True)
    centred = rows - row_mean
    spread = jnp.mean(centred * centred, axis=-1, keepdims=True)
    inverse = lax.rsqrt(spread + EPS)
    return centred * inverse, inverse


def encode(grid_ref, emb_ref, src_ref, len_ref, wkv_ref, hid_ref):
    points = grid_ref.shape[1]
    nodes = emb_ref.shape[0]
    pid = lax.broadcasted_iota(jnp.int32, (points, nodes), 0)
    count = jnp.zeros((points, nodes), F32)
    lens = len_ref[...]
    for e in range(src_ref.shape[0]):
        row = jnp.where(e < lens, src_ref[e : e + 1, :], -1)
        count += (pid == row).astype(F32)
    dead = jnp.where(count > 0, 0.0, -jnp.inf)
    grid_t = grid_ref[...].T
    masks = half_masks()

    def pair(j, _):
        cols = pl.ds(pl.multiple_of(j * 128, 128), 128)
        vcols = pl.ds(pl.multiple_of(j * 128 + 1024, 128), 128)
        keys = nn(grid_t, wkv_ref[:, cols]).astype(BF)
        values = nn(grid_t, wkv_ref[:, vcols]).astype(BF)
        emb = emb_ref[:, cols]
        weights = []
        for n in range(2):
            score = nt(keys, emb * masks[n]) * SCALE + dead
            top = jnp.max(score, axis=0, keepdims=True)
            term = jnp.exp(score - top) * count
            weights.append((term / jnp.sum(term, axis=0, keepdims=True)).astype(BF))
        mixed = tn(weights[0], values * masks[0]) + tn(weights[1], values * masks[1])
        hid_ref[:, cols] = emb.astype(F32) + mixed
        return 0

    lax.fori_loop(0, emb_ref.shape[1] // 128, pair, 0)


def attend(q_ref, k_ref, v_ref, out_ref, blk, low, high):
    masks = half_masks()
    rows = pl.ds(blk * 256, 256)
    span = pl.ds(blk * 256, 768)
    q = q_ref[rows, :]
    k = k_ref[span, :]
    v = v_ref[span, :]
    gap = lax.broadcasted_iota(jnp.int32, (256, 768), 1) - lax.broadcasted_iota(
        jnp.int32, (256, 768), 0
    )
    col = lax.broadcasted_iota(jnp.int32, (256, 768), 1)
    live = (gap >= 0) & (gap <= 512) & (col >= low) & (col < high)
    total = None
    for n in range(2):
        score = jnp.where(live, nt(q * masks[n], k), -jnp.inf)
        top = jnp.max(score, axis=1, keepdims=True)
        term = jnp.exp(score - top)
        part = nn(term.astype(BF), v * masks[n]) / jnp.sum(term, axis=1, keepdims=True)
        total = part if total is None else total + part
    out_ref[rows, :] = total.astype(BF)


MESH = pl.DeviceIdType.MESH


class Ring:
    def __init__(self, full, send, recv):
        h = lax.axis_index("head")
        y, c = h // 2, h % 2
        self.full, self.send, self.recv, self.used = full, send, recv, []
        self.own = h
        self.up = ((y + 1) % 4) * 2 + c
        self.dn = ((y + 3) % 4) * 2 + c
        self.op = ((y + 2) % 4) * 2 + c
        self.flip = 1 - 2 * c
        self.sib = h + self.flip

    def copy(self, block, start, size, to, sem, land):
        view = self.full.at[pl.ds(block * 128 + start, size), :]
        copy = pltpu.make_async_remote_copy(
            src_ref=view, dst_ref=view, send_sem=self.send.at[sem], recv_sem=self.recv.at[land],
            device_id={"head": to}, device_id_type=MESH,
        )
        copy.start()
        self.used.append(copy)
        return copy

    def begin(self):
        own = self.own
        self.dn_a = self.copy(own, 0, 64, self.up, 0, 0)
        self.up_b = self.copy(own, 64, 64, self.dn, 1, 3)
        self.side = self.copy(own, 0, 128, self.sib, 4, 6)
        self.dn_b = self.copy(own, 64, 64, self.up, 2, 1)
        self.up_a = self.copy(own, 0, 64, self.dn, 3, 2)

    def forward(self):
        self.dn_a.wait_recv()
        self.op_a = self.copy(self.dn, 0, 64, self.up, 5, 4)
        self.side_dn_a = self.copy(self.dn, 0, 64, self.sib, 6, 7)
        self.up_b.wait_recv()
        self.op_b = self.copy(self.up, 64, 64, self.dn, 7, 5)
        self.side_up_b = self.copy(self.up, 64, 64, self.sib, 8, 8)

    def near(self):
        self.dn_b.wait_recv()
        self.side_dn_b = self.copy(self.dn, 64, 64, self.sib, 9, 9)
        self.up_a.wait_recv()
        self.side_up_a = self.copy(self.up, 0, 64, self.sib, 10, 10)

    def far(self):
        self.op_a.wait_recv()
        self.side_op_a = self.copy(self.op, 0, 64, self.sib, 11, 11)
        self.op_b.wait_recv()
        self.side_op_b = self.copy(self.op, 64, 64, self.sib, 12, 12)

    def finish(self):
        for copy in self.used:
            copy.wait_send()


def front_kernel(
    grid_h, emb_h, src_h, len_h, wkv_h, pgain_h, wqkv_h, wout_h, dgain_h,
    unit_o, inv_o, din_o,
    grid_v, emb_v, src_v, len_v, wkv_v, pgain_v, wqkv_v, dgain_v, hid, full, wfull, q, kx, vx, att, afull,
    load, nsend, nrecv, wsend, wrecv, hsend, hrecv, asend, arecv,
):
    g = lax.axis_index("grp")
    h = lax.axis_index("head")
    groups = lax.axis_size("grp")
    right, left = (g + 1) % groups, (g + groups - 1) % groups
    pairs = [
        (wout_h, wfull.at[pl.ds(h * 128, 128), :]), (grid_h, grid_v), (emb_h, emb_v), (src_h, src_v),
        (len_h, len_v), (wkv_h, wkv_v), (pgain_h, pgain_v), (wqkv_h, wqkv_v), (dgain_h, dgain_v),
    ]
    loads = [pltpu.make_async_copy(s, d, load.at[i]) for i, (s, d) in enumerate(pairs)]
    for copy in loads:
        copy.start()
    barrier = pltpu.get_barrier_semaphore()
    for i in range(1, 8):
        pl.semaphore_signal(barrier, inc=1, device_id={"head": (h + i) % 8}, device_id_type=MESH)
    for other in (right, left):
        pl.semaphore_signal(barrier, inc=1, device_id={"grp": other}, device_id_type=MESH)
    pl.semaphore_wait(barrier, 9)
    loads[0].wait()
    weights = Ring(wfull, wsend, wrecv)
    weights.begin()
    for copy in loads[1:]:
        copy.wait()

    encode(grid_v, emb_v, src_v, len_v, wkv_v, hid)
    unit, _ = norm_rows(hid[...])
    full[pl.ds(h * 128, 128), :] = (unit * pgain_v[...]).astype(BF)
    rows = Ring(full, nsend, nrecv)
    rows.begin()

    def project(block):
        at = pl.multiple_of(block * 128, 128)
        triple = nn(full[pl.ds(at, 128), :], wqkv_v[...]).astype(BF)
        q[pl.ds(at, 128), :] = (triple[:, :128].astype(F32) * SCALE).astype(BF)
        kx[pl.ds(at + 256, 128), :] = triple[:, 128:256]
        vx[pl.ds(at + 256, 128), :] = triple[:, 256:]

    flip = rows.flip
    project(h)
    rows.side.wait_recv()
    project(rows.sib)
    rows.forward()
    rows.near()
    project(rows.dn)
    project(rows.up)
    rows.side_dn_a.wait_recv()
    rows.side_dn_b.wait_recv()
    project(rows.dn + flip)
    rows.side_up_a.wait_recv()
    rows.side_up_b.wait_recv()
    project(rows.up + flip)
    rows.far()
    project(rows.op)
    rows.side_op_a.wait_recv()
    rows.side_op_b.wait_recv()
    project(rows.op + flip)

    halos = []
    for i, ref in enumerate((kx, vx)):
        for j, (start, land, to) in enumerate(((1024, 0, right), (256, 1280, left))):
            copy = pltpu.make_async_remote_copy(
                src_ref=ref.at[pl.ds(start, 256), :], dst_ref=ref.at[pl.ds(land, 256), :],
                send_sem=hsend.at[i * 2 + j], recv_sem=hrecv.at[i * 2 + j],
                device_id={"grp": to}, device_id_type=MESH,
            )
            copy.start()
            halos.append(copy)
    weights.forward()
    weights.near()

    def give(to):
        return pltpu.make_async_remote_copy(
            src_ref=att.at[pl.ds(to * 128, 128), :],
            dst_ref=afull.at[:, pl.ds(pl.multiple_of(h * 128, 128), 128)],
            send_sem=asend.at[to], recv_sem=arecv.at[h],
            device_id={"head": to}, device_id_type=MESH,
        )

    for blk in (1, 2, 0, 3):
        if blk == 0:
            for copy in halos:
                copy.wait_recv()
        low = jnp.where(g == 0, 256, 0) if blk == 0 else 0
        high = jnp.where(g == groups - 1, 512, 768) if blk == 3 else 768
        attend(q, kx, vx, att, blk, low, high)
        for to in (2 * blk, 2 * blk + 1):

            @pl.when(to != h)
            def _():
                give(to).start()

    weights.far()
    mine = pl.multiple_of(h * 128, 128)
    afull[:, pl.ds(mine, 128)] = att[pl.ds(mine, 128), :]
    for copy in (
        weights.side, weights.side_dn_a, weights.side_dn_b, weights.side_up_a, weights.side_up_b,
        weights.side_op_a, weights.side_op_b,
    ):
        copy.wait_recv()
    for other in range(8):

        @pl.when(other != h)
        def _():
            pltpu.make_async_remote_copy(
                src_ref=att.at[pl.ds(0, 128), :],
                dst_ref=afull.at[:, pl.ds(other * 128, 128)],
                send_sem=asend.at[other], recv_sem=arecv.at[other],
                device_id={"head": other}, device_id_type=MESH,
            ).wait()

    state = hid[...] + nn(afull[...], wfull[...])
    unit, inverse = norm_rows(state)
    unit_o[...] = unit
    inv_o[...] = jnp.broadcast_to(inverse, (128, 128))
    din_o[...] = (unit * dgain_v[...]).astype(BF)
    rows.finish()
    weights.finish()
    for copy in halos:
        copy.wait_send()


def front(grid_in, mesh_embed, enc_src, enc_len, wkv, pgain, wqkv, wout, dgain):
    ops = (grid_in, mesh_embed, enc_src, enc_len, wkv, pgain, wqkv)
    stage = [pltpu.VMEM(a.shape, a.dtype) for a in ops] + [pltpu.VMEM(dgain.shape, F32)]
    dma = pltpu.SemaphoreType.DMA
    return pl.pallas_call(
        front_kernel,
        out_shape=(
            jax.ShapeDtypeStruct((128, 1024), F32),
            jax.ShapeDtypeStruct((128, 128), F32),
            jax.ShapeDtypeStruct((128, 1024), BF),
        ),
        in_specs=[pl.BlockSpec(memory_space=pl.ANY)] * 9,
        out_specs=(VM, VM, VM),
        scratch_shapes=stage
        + [
            pltpu.VMEM((128, 1024), F32),
            pltpu.VMEM((1024, 1024), BF),
            pltpu.VMEM((1024, 1024), BF),
            pltpu.VMEM((1024, 128), BF),
            pltpu.VMEM((1536, 128), BF),
            pltpu.VMEM((1536, 128), BF),
            pltpu.VMEM((1024, 128), BF),
            pltpu.VMEM((128, 1024), BF),
            dma((9,)), dma((13,)), dma((13,)), dma((13,)), dma((13,)), dma((4,)), dma((4,)), dma((8,)), dma((8,)),
        ],
        compiler_params=pltpu.CompilerParams(
            vmem_limit_bytes=60 * 2**20, collective_id=0, has_side_effects=True
        ),
    )(*ops, wout, dgain)


def head_sum():
    row = lax.broadcasted_iota(jnp.int32, (1024, 128), 0) // 64
    col = lax.broadcasted_iota(jnp.int32, (1024, 128), 1)
    return (row == col).astype(F32).astype(BF)


def head_spread():
    row = lax.broadcasted_iota(jnp.int32, (128, 1024), 0)
    col = lax.broadcasted_iota(jnp.int32, (128, 1024), 1) // 64
    return (row == col).astype(F32).astype(BF)


def decode(grid_ref, dfc_ref, srct_ref, src_ref, wq_ref, wf_ref, u_ref, slot_ref, est_ref, back_ref, xe, kv, bg, rg):
    pts = 256
    lane = lax.broadcasted_iota(jnp.int32, (pts, 1024), 1)
    for e in range(3):
        pick = (srct_ref[:, e : e + 1] == lane).astype(F32).astype(BF)

        def gather(j, _):
            cols = pl.ds(pl.multiple_of(j * 256, 256), 256)
            xe[e * pts : (e + 1) * pts, cols] = nn(pick, slot_ref[:, cols]).astype(BF)
            return 0

        lax.fori_loop(0, 4, gather, 0)

    def project(j, _):
        cols = pl.ds(pl.multiple_of(j * 256, 256), 256)
        kv[:, cols] = nn(xe[...], u_ref[:, cols]).astype(BF)
        return 0

    lax.fori_loop(0, 8, project, 0)
    query = tn(grid_ref[...], wq_ref[...]).astype(BF)
    bg[...] = tn(dfc_ref[...], wf_ref[...])
    hsum = head_sum()
    spread = head_spread()
    qf = query.astype(F32)
    score, along = [], []
    for e in range(3):
        rows = slice(e * pts, (e + 1) * pts)
        score.append(nn((qf * kv[rows, :1024].astype(F32)).astype(BF), hsum) * SCALE)
        along.append(nn((bg[...] * kv[rows, 1024:].astype(F32)).astype(BF), hsum))
    top = jnp.maximum(jnp.maximum(score[0], score[1]), score[2])
    term = [jnp.exp(s - top) for s in score]
    total = term[0] + term[1] + term[2]
    weight = [t / total for t in term]
    mean = weight[0] * along[0] + weight[1] * along[1] + weight[2] * along[2]
    mix = jnp.zeros((pts, 1024), F32)
    for e in range(3):
        rows = slice(e * pts, (e + 1) * pts)
        wide = nn(weight[e].astype(BF), spread)
        mix += wide * kv[rows, 1024:].astype(F32)
        grad = nn((weight[e] * (along[e] - mean) * SCALE).astype(BF), spread)
        kv[rows, :1024] = (grad * qf).astype(BF)
        kv[rows, 1024:] = (wide * bg[...]).astype(BF)
    est_ref[...] = grid_ref[0:100, :].astype(F32) + nt(wf_ref[...], mix.astype(BF))

    def unproject(j, _):
        cols = pl.ds(pl.multiple_of(j * 256, 256), 256)
        rg[:, cols] = nt(kv[...], u_ref[cols, :]).astype(BF)
        return 0

    lax.fori_loop(0, 4, unproject, 0)

    def scatter(j, _):
        rows = pl.ds(pl.multiple_of(j * 128, 128), 128)
        sub = lax.broadcasted_iota(jnp.int32, (128, pts), 0) + j * 128
        pick = jnp.concatenate(
            [(src_ref[e : e + 1, :] == sub).astype(F32).astype(BF) for e in range(3)], axis=1
        )
        back_ref[rows, :] = nn(pick, rg[...]).astype(BF)
        return 0

    lax.fori_loop(0, 8, scatter, 0)


VM = pl.BlockSpec(memory_space=pltpu.VMEM)


def body(
    grid_in, mesh_embed, enc_src, enc_len, enc_kv_weight, proc_gain, qkv_weight, out_weight,
    dec_gain, unpack, wq, wf, dec_send, dec_src, dforecast,
):
    params = pltpu.CompilerParams(vmem_limit_bytes=50 * 2**20)
    unit, inverse, dec_in = front(
        grid_in, mesh_embed, enc_src, enc_len.reshape(1, -1), enc_kv_weight, proc_gain.reshape(1, -1),
        qkv_weight.reshape(1024, 384), out_weight, dec_gain.reshape(1, -1),
    )
    inverse = inverse[:, :1]
    flat = dec_send.reshape(-1)
    pick = (flat[:, None] == jnp.arange(128)[None, :]).astype(BF)
    sent = jnp.dot(pick, dec_in, preferred_element_type=F32).astype(BF)
    arrived = lax.all_to_all(sent.reshape(32, 32, 1024), "grp", 0, 0, tiled=True).reshape(1024, 1024)
    estimated, back = pl.pallas_call(
        decode,
        out_shape=(
            jax.ShapeDtypeStruct((100, 256), F32),
            jax.ShapeDtypeStruct((1024, 1024), BF),
        ),
        in_specs=[VM] * 8,
        out_specs=(VM, VM),
        scratch_shapes=[
            pltpu.VMEM((768, 1024), BF),
            pltpu.VMEM((768, 2048), BF),
            pltpu.VMEM((256, 1024), F32),
            pltpu.VMEM((768, 1024), BF),
        ],
        compiler_params=params,
    )(grid_in, dforecast, dec_src.T, dec_src, wq, wf, unpack, arrived)
    returned = lax.all_to_all(back.reshape(32, 32, 1024), "grp", 0, 0, tiled=True).reshape(1024, 1024)
    place = (jnp.arange(128)[:, None] == flat[None, :]).astype(BF)
    entry = jnp.dot(place, returned, preferred_element_type=F32)
    scaled = entry * dec_gain
    first = jnp.mean(scaled, axis=-1, keepdims=True)
    second = jnp.mean(scaled * unit, axis=-1, keepdims=True)
    return estimated, inverse * (scaled - first - unit * second)


def solution(mesh):
    return jax.shard_map(
        body,
        mesh=mesh,
        in_specs=(
            P(None, ("grp", "head")), P(("grp", "head"), None), P(None, ("grp", "head")),
            P(("grp", "head")), P(), P(), P(None, None, "head"), P("head", None), P(), P(), P(), P(),
            P(("grp", "head"), None), P(None, ("grp", "head")), P(None, ("grp", "head")),
        ),
        out_specs=(P(None, ("grp", "head")), P(("grp", "head"), None)),
        check_vma=False,
    )
```

```python
import jax
import jax.numpy as jnp
from jax import lax
from jax.experimental import pallas as pl
from jax.experimental.pallas import tpu as pltpu
from jax.sharding import PartitionSpec as P

F32 = jnp.float32
BF = jnp.bfloat16
EPS = 1e-05
SCALE = 0.125


def nn(a, b):
    return lax.dot_general(a, b, (((1,), (0,)), ((), ())), preferred_element_type=F32)


def nt(a, b):
    return lax.dot_general(a, b, (((1,), (1,)), ((), ())), preferred_element_type=F32)


def tn(a, b):
    return lax.dot_general(a, b, (((0,), (0,)), ((), ())), preferred_element_type=F32)


def half_masks():
    lane = lax.broadcasted_iota(jnp.int32, (1, 128), 1)
    return [(lane < 64).astype(F32).astype(BF), (lane >= 64).astype(F32).astype(BF)]


def norm_rows(rows):
    row_mean = jnp.mean(rows, axis=-1, keepdims=True)
    centred = rows - row_mean
    spread = jnp.mean(centred * centred, axis=-1, keepdims=True)
    inverse = lax.rsqrt(spread + EPS)
    return centred * inverse, inverse


def encode(grid_ref, emb_ref, src_ref, len_ref, wkv_ref, hid_ref):
    points = grid_ref.shape[1]
    nodes = emb_ref.shape[0]
    pid = lax.broadcasted_iota(jnp.int32, (points, nodes), 0)
    count = jnp.zeros((points, nodes), F32)
    lens = len_ref[...]
    for e in range(src_ref.shape[0]):
        row = jnp.where(e < lens, src_ref[e : e + 1, :], -1)
        count += (pid == row).astype(F32)
    dead = jnp.where(count > 0, 0.0, -jnp.inf)
    grid_t = grid_ref[...].T
    masks = half_masks()

    def pair(j, _):
        cols = pl.ds(pl.multiple_of(j * 128, 128), 128)
        vcols = pl.ds(pl.multiple_of(j * 128 + 1024, 128), 128)
        keys = nn(grid_t, wkv_ref[:, cols]).astype(BF)
        values = nn(grid_t, wkv_ref[:, vcols]).astype(BF)
        emb = emb_ref[:, cols]
        weights = []
        for n in range(2):
            score = nt(keys, emb * masks[n]) * SCALE + dead
            top = jnp.max(score, axis=0, keepdims=True)
            term = jnp.exp(score - top) * count
            weights.append((term / jnp.sum(term, axis=0, keepdims=True)).astype(BF))
        mixed = tn(weights[0], values * masks[0]) + tn(weights[1], values * masks[1])
        hid_ref[:, cols] = emb.astype(F32) + mixed
        return 0

    lax.fori_loop(0, emb_ref.shape[1] // 128, pair, 0)


def attend(q_ref, k_ref, v_ref, out_ref, blk, low, high):
    masks = half_masks()
    rows = pl.ds(blk * 256, 256)
    span = pl.ds(blk * 256, 768)
    q = q_ref[rows, :]
    k = k_ref[span, :]
    v = v_ref[span, :]
    gap = lax.broadcasted_iota(jnp.int32, (256, 768), 1) - lax.broadcasted_iota(
        jnp.int32, (256, 768), 0
    )
    col = lax.broadcasted_iota(jnp.int32, (256, 768), 1)
    live = (gap >= 0) & (gap <= 512) & (col >= low) & (col < high)
    total = None
    for n in range(2):
        score = jnp.where(live, nt(q * masks[n], k), -jnp.inf)
        top = jnp.max(score, axis=1, keepdims=True)
        term = jnp.exp(score - top)
        part = nn(term.astype(BF), v * masks[n]) / jnp.sum(term, axis=1, keepdims=True)
        total = part if total is None else total + part
    out_ref[rows, :] = total.astype(BF)


MESH = pl.DeviceIdType.MESH


class Ring:
    def __init__(self, full, send, recv):
        h = lax.axis_index("head")
        y, c = h // 2, h % 2
        self.full, self.send, self.recv, self.used = full, send, recv, []
        self.own = h
        self.up = ((y + 1) % 4) * 2 + c
        self.dn = ((y + 3) % 4) * 2 + c
        self.op = ((y + 2) % 4) * 2 + c
        self.flip = 1 - 2 * c
        self.sib = h + self.flip

    def copy(self, block, start, size, to, sem, land):
        view = self.full.at[pl.ds(block * 128 + start, size), :]
        copy = pltpu.make_async_remote_copy(
            src_ref=view, dst_ref=view, send_sem=self.send.at[sem], recv_sem=self.recv.at[land],
            device_id={"head": to}, device_id_type=MESH,
        )
        copy.start()
        self.used.append(copy)
        return copy

    def begin(self):
        own = self.own
        self.dn_a = self.copy(own, 0, 64, self.up, 0, 0)
        self.up_b = self.copy(own, 64, 64, self.dn, 1, 3)
        self.side = self.copy(own, 0, 128, self.sib, 4, 6)
        self.dn_b = self.copy(own, 64, 64, self.up, 2, 1)
        self.up_a = self.copy(own, 0, 64, self.dn, 3, 2)

    def forward(self):
        self.dn_a.wait_recv()
        self.op_a = self.copy(self.dn, 0, 64, self.up, 5, 4)
        self.side_dn_a = self.copy(self.dn, 0, 64, self.sib, 6, 7)
        self.up_b.wait_recv()
        self.op_b = self.copy(self.up, 64, 64, self.dn, 7, 5)
        self.side_up_b = self.copy(self.up, 64, 64, self.sib, 8, 8)

    def near(self):
        self.dn_b.wait_recv()
        self.side_dn_b = self.copy(self.dn, 64, 64, self.sib, 9, 9)
        self.up_a.wait_recv()
        self.side_up_a = self.copy(self.up, 0, 64, self.sib, 10, 10)

    def far(self):
        self.op_a.wait_recv()
        self.side_op_a = self.copy(self.op, 0, 64, self.sib, 11, 11)
        self.op_b.wait_recv()
        self.side_op_b = self.copy(self.op, 64, 64, self.sib, 12, 12)

    def finish(self):
        for copy in self.used:
            copy.wait_send()


def front_kernel(
    grid_h, emb_h, src_h, len_h, wkv_h, pgain_h, wqkv_h, wout_h, dgain_h,
    unit_o, inv_o, din_o,
    grid_v, emb_v, src_v, len_v, wkv_v, pgain_v, wqkv_v, dgain_v, hid, full, wfull, q, kx, vx, att, afull,
    load, nsend, nrecv, wsend, wrecv, hsend, hrecv, asend, arecv,
):
    g = lax.axis_index("grp")
    h = lax.axis_index("head")
    groups = lax.axis_size("grp")
    right, left = (g + 1) % groups, (g + groups - 1) % groups
    pairs = [
        (wout_h, wfull.at[pl.ds(h * 128, 128), :]), (grid_h, grid_v), (emb_h, emb_v), (src_h, src_v),
        (len_h, len_v), (wkv_h, wkv_v), (pgain_h, pgain_v), (wqkv_h, wqkv_v), (dgain_h, dgain_v),
    ]
    loads = [pltpu.make_async_copy(s, d, load.at[i]) for i, (s, d) in enumerate(pairs)]
    for copy in loads:
        copy.start()
    barrier = pltpu.get_barrier_semaphore()
    for i in range(1, 8):
        pl.semaphore_signal(barrier, inc=1, device_id={"head": (h + i) % 8}, device_id_type=MESH)
    for other in (right, left):
        pl.semaphore_signal(barrier, inc=1, device_id={"grp": other}, device_id_type=MESH)
    pl.semaphore_wait(barrier, 9)
    loads[0].wait()
    weights = Ring(wfull, wsend, wrecv)
    weights.begin()
    for copy in loads[1:]:
        copy.wait()

    encode(grid_v, emb_v, src_v, len_v, wkv_v, hid)
    unit, _ = norm_rows(hid[...])
    full[pl.ds(h * 128, 128), :] = (unit * pgain_v[...]).astype(BF)
    rows = Ring(full, nsend, nrecv)
    rows.begin()

    def project(block):
        at = pl.multiple_of(block * 128, 128)
        triple = nn(full[pl.ds(at, 128), :], wqkv_v[...]).astype(BF)
        q[pl.ds(at, 128), :] = (triple[:, :128].astype(F32) * SCALE).astype(BF)
        kx[pl.ds(at + 256, 128), :] = triple[:, 128:256]
        vx[pl.ds(at + 256, 128), :] = triple[:, 256:]

    flip = rows.flip
    project(h)
    rows.side.wait_recv()
    project(rows.sib)
    rows.forward()
    rows.near()
    project(rows.dn)
    project(rows.up)
    rows.side_dn_a.wait_recv()
    rows.side_dn_b.wait_recv()
    project(rows.dn + flip)
    rows.side_up_a.wait_recv()
    rows.side_up_b.wait_recv()
    project(rows.up + flip)
    rows.far()
    project(rows.op)
    rows.side_op_a.wait_recv()
    rows.side_op_b.wait_recv()
    project(rows.op + flip)

    halos = []
    for i, ref in enumerate((kx, vx)):
        for j, (start, land, to) in enumerate(((1024, 0, right), (256, 1280, left))):
            copy = pltpu.make_async_remote_copy(
                src_ref=ref.at[pl.ds(start, 256), :], dst_ref=ref.at[pl.ds(land, 256), :],
                send_sem=hsend.at[i * 2 + j], recv_sem=hrecv.at[i * 2 + j],
                device_id={"grp": to}, device_id_type=MESH,
            )
            copy.start()
            halos.append(copy)
    weights.forward()
    weights.near()

    def give(to):
        return pltpu.make_async_remote_copy(
            src_ref=att.at[pl.ds(to * 128, 128), :],
            dst_ref=afull.at[:, pl.ds(pl.multiple_of(h * 128, 128), 128)],
            send_sem=asend.at[to], recv_sem=arecv.at[h],
            device_id={"head": to}, device_id_type=MESH,
        )

    for blk in (1, 2, 0, 3):
        if blk == 0:
            for copy in halos:
                copy.wait_recv()
        low = jnp.where(g == 0, 256, 0) if blk == 0 else 0
        high = jnp.where(g == groups - 1, 512, 768) if blk == 3 else 768
        attend(q, kx, vx, att, blk, low, high)
        for to in (2 * blk, 2 * blk + 1):

            @pl.when(to != h)
            def _():
                give(to).start()

    weights.far()
    mine = pl.multiple_of(h * 128, 128)
    afull[:, pl.ds(mine, 128)] = att[pl.ds(mine, 128), :]
    for copy in (
        weights.side, weights.side_dn_a, weights.side_dn_b, weights.side_up_a, weights.side_up_b,
        weights.side_op_a, weights.side_op_b,
    ):
        copy.wait_recv()
    for other in range(8):

        @pl.when(other != h)
        def _():
            pltpu.make_async_remote_copy(
                src_ref=att.at[pl.ds(0, 128), :],
                dst_ref=afull.at[:, pl.ds(other * 128, 128)],
                send_sem=asend.at[other], recv_sem=arecv.at[other],
                device_id={"head": other}, device_id_type=MESH,
            ).wait()

    state = hid[...] + nn(afull[...], wfull[...])
    unit, inverse = norm_rows(state)
    unit_o[...] = unit
    inv_o[...] = jnp.broadcast_to(inverse, (128, 128))
    din_o[...] = (unit * dgain_v[...]).astype(BF)
    rows.finish()
    weights.finish()
    for copy in halos:
        copy.wait_send()


def front(grid_in, mesh_embed, enc_src, enc_len, wkv, pgain, wqkv, wout, dgain):
    ops = (grid_in, mesh_embed, enc_src, enc_len, wkv, pgain, wqkv)
    stage = [pltpu.VMEM(a.shape, a.dtype) for a in ops] + [pltpu.VMEM(dgain.shape, F32)]
    dma = pltpu.SemaphoreType.DMA
    return pl.pallas_call(
        front_kernel,
        out_shape=(
            jax.ShapeDtypeStruct((128, 1024), F32),
            jax.ShapeDtypeStruct((128, 128), F32),
            jax.ShapeDtypeStruct((128, 1024), BF),
        ),
        in_specs=[pl.BlockSpec(memory_space=pl.ANY)] * 9,
        out_specs=(VM, VM, VM),
        scratch_shapes=stage
        + [
            pltpu.VMEM((128, 1024), F32),
            pltpu.VMEM((1024, 1024), BF),
            pltpu.VMEM((1024, 1024), BF),
            pltpu.VMEM((1024, 128), BF),
            pltpu.VMEM((1536, 128), BF),
            pltpu.VMEM((1536, 128), BF),
            pltpu.VMEM((1024, 128), BF),
            pltpu.VMEM((128, 1024), BF),
            dma((9,)), dma((13,)), dma((13,)), dma((13,)), dma((13,)), dma((4,)), dma((4,)), dma((8,)), dma((8,)),
        ],
        compiler_params=pltpu.CompilerParams(
            vmem_limit_bytes=60 * 2**20, collective_id=0, has_side_effects=True
        ),
    )(*ops, wout, dgain)


def head_sum():
    row = lax.broadcasted_iota(jnp.int32, (1024, 128), 0) // 64
    col = lax.broadcasted_iota(jnp.int32, (1024, 128), 1)
    return (row == col).astype(F32).astype(BF)


def head_spread():
    row = lax.broadcasted_iota(jnp.int32, (128, 1024), 0)
    col = lax.broadcasted_iota(jnp.int32, (128, 1024), 1) // 64
    return (row == col).astype(F32).astype(BF)


def decode_ready(grid_ref, dfc_ref, wq_ref, wf_ref, query, bg):
    query[...] = tn(grid_ref[...], wq_ref[...]).astype(BF)
    bg[...] = tn(dfc_ref[...], wf_ref[...])


def decode(grid_ref, srct_ref, wf_ref, u_ref, slot_ref, est_ref, xe, kv, query, bg, rg):
    pts = 256
    lane = lax.broadcasted_iota(jnp.int32, (pts, 1024), 1)
    for e in range(3):
        pick = (srct_ref[:, e : e + 1] == lane).astype(F32).astype(BF)

        def gather(j, _):
            cols = pl.ds(pl.multiple_of(j * 256, 256), 256)
            xe[e * pts : (e + 1) * pts, cols] = nn(pick, slot_ref[:, cols]).astype(BF)
            return 0

        lax.fori_loop(0, 4, gather, 0)

    def project(j, _):
        cols = pl.ds(pl.multiple_of(j * 256, 256), 256)
        kv[:, cols] = nn(xe[...], u_ref[:, cols]).astype(BF)
        return 0

    lax.fori_loop(0, 8, project, 0)
    hsum = head_sum()
    spread = head_spread()
    qf = query[...].astype(F32)
    score, along = [], []
    for e in range(3):
        rows = slice(e * pts, (e + 1) * pts)
        score.append(nn((qf * kv[rows, :1024].astype(F32)).astype(BF), hsum) * SCALE)
        along.append(nn((bg[...] * kv[rows, 1024:].astype(F32)).astype(BF), hsum))
    top = jnp.maximum(jnp.maximum(score[0], score[1]), score[2])
    term = [jnp.exp(s - top) for s in score]
    total = term[0] + term[1] + term[2]
    weight = [t / total for t in term]
    mean = weight[0] * along[0] + weight[1] * along[1] + weight[2] * along[2]
    mix = jnp.zeros((pts, 1024), F32)
    for e in range(3):
        rows = slice(e * pts, (e + 1) * pts)
        wide = nn(weight[e].astype(BF), spread)
        mix += wide * kv[rows, 1024:].astype(F32)
        grad = nn((weight[e] * (along[e] - mean) * SCALE).astype(BF), spread)
        kv[rows, :1024] = (grad * qf).astype(BF)
        kv[rows, 1024:] = (wide * bg[...]).astype(BF)
    est_ref[...] = grid_ref[0:100, :].astype(F32) + nt(wf_ref[...], mix.astype(BF))

    def unproject(j, _):
        cols = pl.ds(pl.multiple_of(j * 256, 256), 256)
        rg[:, cols] = nt(kv[...], u_ref[cols, :]).astype(BF)
        return 0

    lax.fori_loop(0, 4, unproject, 0)


NX, NZ = 4, 8
A, B = slice(0, 64), slice(64, 128)


def back_kernel(
    din_h, unit_h, inv_h, gain_h, tab_h, grid_h, dfc_h, srct_h, src_h, wq_h, wf_h, u_h,
    est_o, vert_o,
    unit_v, inv_v, gain_v, tab_v, grid_v, dfc_v, srct_v, src_v, wq_v, wf_v, u_v,
    zbuf, tab, xs, arrived, xe, kv, query, bg, rg, bs, rback, outs, ins,
    load, tsend, trecv, zsend, zrecv, xsend, xrecv, bsend, brecv, qsend, qrecv,
):
    g = lax.axis_index("grp")
    x, z = g // NZ, g % NZ
    nexts = [(z + 1) % NZ, (z + NZ - 1) % NZ]
    pairs = [
        (din_h, zbuf.at[z]), (tab_h, tab_v), (grid_h, grid_v), (dfc_h, dfc_v), (wq_h, wq_v), (wf_h, wf_v),
        (srct_h, srct_v), (src_h, src_v), (u_h, u_v), (unit_h, unit_v), (inv_h, inv_v), (gain_h, gain_v),
    ]
    loads = [pltpu.make_async_copy(s, d, load.at[i]) for i, (s, d) in enumerate(pairs)]
    for copy in loads:
        copy.start()

    def remote(source, target, send, recv, xx, zz):
        copy = pltpu.make_async_remote_copy(
            src_ref=source, dst_ref=target, send_sem=send, recv_sem=recv,
            device_id={"grp": xx * NZ + zz}, device_id_type=MESH,
        )
        copy.start()
        return copy

    barrier = pltpu.get_barrier_semaphore()
    for k in range(1, NZ):
        pl.semaphore_signal(barrier, inc=1, device_id={"grp": x * NZ + (z + k) % NZ}, device_id_type=MESH)
    for k in range(1, NX):
        pl.semaphore_signal(barrier, inc=1, device_id={"grp": (x + k) % NX * NZ + z}, device_id_type=MESH)
    pl.semaphore_wait(barrier, NX + NZ - 2)
    loads[0].wait()
    sent = []
    ring = {}

    def pass_on(way, d, chunk):
        block = (z + d) % NZ if way else (z + NZ - d) % NZ
        view = zbuf.at[block, pl.ds(64 * chunk, 64), :]
        sem = way * 8 + d * 2 + chunk
        ring[way, d, chunk] = remote(view, view, zsend.at[sem], zrecv.at[sem], x, nexts[way])
        sent.append(ring[way, d, chunk])

    hops = ((0, 0), (1, 1), (0, 1), (1, 0))
    for way, chunk in hops:
        pass_on(way, 0, chunk)
    loads[1].wait()
    tab[pl.ds(z, 1)] = tab_v[pl.ds(z, 1)]
    tables = [
        remote(tab_v.at[(z + k) % NZ], tab.at[z], tsend.at[k], trecv.at[k], x, (z + k) % NZ)
        for k in range(1, NZ)
    ]
    sent.extend(tables)

    def chosen(zz):
        node = lax.broadcasted_iota(jnp.int32, (128, 128), 0)
        return (node == tab[zz][0:1, :]).astype(F32).astype(BF)

    crossing = []

    def select(index, zz):
        xs[index] = tn(chosen(zz), zbuf[zz]).astype(BF)
        land = pl.ds(pl.multiple_of((x * NZ + zz) * 32, 32), 32)
        for k in range(1, NX):
            xx = (x + k) % NX
            sem = index * NX + k
            crossing.append(remote(
                xs.at[index, pl.ds(pl.multiple_of(xx * 32, 32), 32), :], arrived.at[land, :],
                xsend.at[sem], xrecv.at[sem], xx, z,
            ))
        arrived[land, :] = xs[index, pl.ds(pl.multiple_of(x * 32, 32), 32), :]

    select(0, z)
    for copy in loads[2:6]:
        copy.wait()
    decode_ready(grid_v, dfc_v, wq_v, wf_v, query, bg)
    for copy in loads[6:]:
        copy.wait()
    for copy in tables:
        copy.wait_recv()
    for d in range(1, 5):
        for way, chunk in hops:
            last = way == chunk
            if d < 4 or last:
                ring[way, d - 1, chunk].wait_recv()
            if d < 3 or (d == 3 and last):
                pass_on(way, d, chunk)
        if d < 4:
            select(2 * d - 1, (z + NZ - d) % NZ)
            select(2 * d, (z + d) % NZ)
        else:
            select(7, (z + 4) % NZ)
    for copy in crossing:
        copy.wait_recv()
    decode(grid_v, srct_v, wf_v, u_v, arrived, est_o, xe, kv, query, bg, rg)

    order = [(7, (z + 4) % NZ)]
    for d in (3, 2, 1):
        order += [(2 * d, (z + d) % NZ), (2 * d - 1, (z + NZ - d) % NZ)]
    order.append((0, z))
    returning = {}
    for index, zz in order:
        row = lax.broadcasted_iota(jnp.int32, (128, 256), 0)
        slot = (row // 32 * NZ + zz) * 32 + row % 32
        pick = jnp.concatenate(
            [(src_v[e : e + 1, :] == slot).astype(F32).astype(BF) for e in range(3)], axis=1
        )
        bs[index] = nn(pick, rg[...]).astype(BF)
        land = pl.ds(pl.multiple_of(x * 32, 32), 32)
        for k in range(1, NX):
            xx = (x + k) % NX
            sem = index * NX + k
            returning[index, k] = remote(
                bs.at[index, pl.ds(pl.multiple_of(xx * 32, 32), 32), :], rback.at[index, land, :],
                bsend.at[sem], brecv.at[sem], xx, z,
            )
        rback[index, land, :] = bs[index, land, :]

    def partial(index, zz):
        for k in range(1, NX):
            returning[index, k].wait_recv()
        return nn(chosen(zz), rback[index])

    flow = {}

    def push(way, i, chunk):
        rows = pl.ds(64 * chunk, 64)
        sem = way * 8 + i * 2 + chunk
        flow[way, i, chunk] = remote(
            outs.at[way, i, rows, :], ins.at[way, i, rows, :], qsend.at[sem], qrecv.at[sem], x, nexts[way]
        )

    part = partial(7, (z + 4) % NZ)
    outs[0, 3, A] = part[A].astype(BF)
    push(0, 3, 0)
    outs[1, 3, B] = part[B].astype(BF)
    push(1, 3, 1)
    for d in (3, 2, 1):
        for way in range(2):
            index = 2 * d - way
            part = partial(index, (z + NZ - d) % NZ if way else (z + d) % NZ)
            for chunk in (way, 1 - way):
                rows = B if chunk else A
                value = part[rows]
                if d < 3 or chunk == way:
                    flow[way, d, chunk].wait_recv()
                    value = value + ins[way, d, rows].astype(F32)
                outs[way, d - 1, rows] = value.astype(BF)
                push(way, d - 1, chunk)
    part = partial(0, z)
    for way in range(2):
        for chunk in range(2):
            flow[way, 0, chunk].wait_recv()
    grad = part + ins[0, 0].astype(F32) + ins[1, 0].astype(F32)
    unit = unit_v[...]
    scaled = grad * gain_v[...]
    first = jnp.mean(scaled, axis=-1, keepdims=True)
    second = jnp.mean(scaled * unit, axis=-1, keepdims=True)
    vert_o[...] = inv_v[:, 0:1] * (scaled - first - unit * second)
    for copy in sent + crossing + list(returning.values()) + list(flow.values()):
        copy.wait_send()


def back(din, unit, inv, gain, send, grid_in, dforecast, dec_src, wq, wf, u):
    table = jnp.broadcast_to(
        send.reshape(NX, NZ, 32).transpose(1, 0, 2).reshape(NZ, 1, 128), (NZ, 8, 128)
    )
    ops = (din, unit, inv, gain, table, grid_in, dforecast, dec_src.T, dec_src, wq, wf, u)
    dma = pltpu.SemaphoreType.DMA
    vm = pltpu.VMEM
    return pl.pallas_call(
        back_kernel,
        out_shape=(
            jax.ShapeDtypeStruct((100, 256), F32),
            jax.ShapeDtypeStruct((128, 1024), F32),
        ),
        in_specs=[pl.BlockSpec(memory_space=pl.ANY)] * len(ops),
        out_specs=(VM, VM),
        scratch_shapes=[vm(a.shape, a.dtype) for a in ops[1:]]
        + [
            vm((NZ, 128, 1024), BF),
            vm((NZ, 8, 128), jnp.int32),
            vm((8, 128, 1024), BF),
            vm((1024, 1024), BF),
            vm((768, 1024), BF),
            vm((768, 2048), BF),
            vm((256, 1024), BF),
            vm((256, 1024), F32),
            vm((768, 1024), BF),
            vm((8, 128, 1024), BF),
            vm((8, 128, 1024), BF),
            vm((2, 4, 128, 1024), BF),
            vm((2, 4, 128, 1024), BF),
            dma((12,)), dma((8,)), dma((8,)), dma((16,)), dma((16,)), dma((32,)), dma((32,)), dma((32,)), dma((32,)),
            dma((16,)), dma((16,)),
        ],
        compiler_params=pltpu.CompilerParams(
            vmem_limit_bytes=60 * 2**20, collective_id=1, has_side_effects=True
        ),
    )(*ops)


VM = pl.BlockSpec(memory_space=pltpu.VMEM)


def body(
    grid_in, mesh_embed, enc_src, enc_len, enc_kv_weight, proc_gain, qkv_weight, out_weight,
    dec_gain, unpack, wq, wf, dec_send, dec_src, dforecast,
):
    unit, inverse, dec_in = front(
        grid_in, mesh_embed, enc_src, enc_len.reshape(1, -1), enc_kv_weight, proc_gain.reshape(1, -1),
        qkv_weight.reshape(1024, 384), out_weight, dec_gain.reshape(1, -1),
    )
    return back(
        dec_in, unit, inverse, dec_gain.reshape(1, -1), dec_send, grid_in, dforecast, dec_src, wq, wf, unpack
    )


def solution(mesh):
    return jax.shard_map(
        body,
        mesh=mesh,
        in_specs=(
            P(None, ("grp", "head")), P(("grp", "head"), None), P(None, ("grp", "head")),
            P(("grp", "head")), P(), P(), P(None, None, "head"), P("head", None), P(), P(), P(), P(),
            P(("grp", "head"), None), P(None, ("grp", "head")), P(None, ("grp", "head")),
        ),
        out_specs=(P(None, ("grp", "head")), P(("grp", "head"), None)),
        check_vma=False,
    )
```

```python
import jax
import jax.numpy as jnp
from jax import lax
from jax.experimental import pallas as pl
from jax.experimental.pallas import tpu as pltpu
from jax.sharding import PartitionSpec as P

F32 = jnp.float32
BF = jnp.bfloat16
EPS = 1e-05
SCALE = 0.125


def nn(a, b):
    return lax.dot_general(a, b, (((1,), (0,)), ((), ())), preferred_element_type=F32)


def nt(a, b):
    return lax.dot_general(a, b, (((1,), (1,)), ((), ())), preferred_element_type=F32)


def tn(a, b):
    return lax.dot_general(a, b, (((0,), (0,)), ((), ())), preferred_element_type=F32)


def half_masks():
    lane = lax.broadcasted_iota(jnp.int32, (1, 128), 1)
    return [(lane < 64).astype(F32).astype(BF), (lane >= 64).astype(F32).astype(BF)]


def norm_rows(rows):
    row_mean = jnp.mean(rows, axis=-1, keepdims=True)
    centred = rows - row_mean
    spread = jnp.mean(centred * centred, axis=-1, keepdims=True)
    inverse = lax.rsqrt(spread + EPS)
    return centred * inverse, inverse


def encode(grid_ref, emb_ref, src_ref, len_ref, wkv_ref, hid_ref):
    points = grid_ref.shape[1]
    nodes = emb_ref.shape[0]
    pid = lax.broadcasted_iota(jnp.int32, (points, nodes), 0)
    count = jnp.zeros((points, nodes), F32)
    lens = len_ref[...]
    for e in range(src_ref.shape[0]):
        row = jnp.where(e < lens, src_ref[e : e + 1, :], -1)
        count += (pid == row).astype(F32)
    dead = jnp.where(count > 0, 0.0, -jnp.inf)
    grid_t = grid_ref[...].T
    masks = half_masks()

    def pair(j, _):
        cols = pl.ds(pl.multiple_of(j * 128, 128), 128)
        vcols = pl.ds(pl.multiple_of(j * 128 + 1024, 128), 128)
        keys = nn(grid_t, wkv_ref[:, cols]).astype(BF)
        values = nn(grid_t, wkv_ref[:, vcols]).astype(BF)
        emb = emb_ref[:, cols]
        weights = []
        for n in range(2):
            score = nt(keys, emb * masks[n]) * SCALE + dead
            top = jnp.max(score, axis=0, keepdims=True)
            term = jnp.exp(score - top) * count
            weights.append((term / jnp.sum(term, axis=0, keepdims=True)).astype(BF))
        mixed = tn(weights[0], values * masks[0]) + tn(weights[1], values * masks[1])
        hid_ref[:, cols] = emb.astype(F32) + mixed
        return 0

    lax.fori_loop(0, emb_ref.shape[1] // 128, pair, 0)


def attend(q_ref, k_ref, v_ref, out_ref, blk, low, high):
    masks = half_masks()
    rows = pl.ds(blk * 256, 256)
    span = pl.ds(blk * 256, 768)
    q = q_ref[rows, :]
    k = k_ref[span, :]
    v = v_ref[span, :]
    gap = lax.broadcasted_iota(jnp.int32, (256, 768), 1) - lax.broadcasted_iota(
        jnp.int32, (256, 768), 0
    )
    col = lax.broadcasted_iota(jnp.int32, (256, 768), 1)
    live = (gap >= 0) & (gap <= 512) & (col >= low) & (col < high)
    total = None
    for n in range(2):
        score = jnp.where(live, nt(q * masks[n], k), -jnp.inf)
        top = jnp.max(score, axis=1, keepdims=True)
        term = jnp.exp(score - top)
        part = nn(term.astype(BF), v * masks[n]) / jnp.sum(term, axis=1, keepdims=True)
        total = part if total is None else total + part
    out_ref[rows, :] = total.astype(BF)


MESH = pl.DeviceIdType.MESH


class Ring:
    def __init__(self, full, send, recv):
        h = lax.axis_index("head")
        y, c = h // 2, h % 2
        self.full, self.send, self.recv, self.used = full, send, recv, []
        self.own = h
        self.up = ((y + 1) % 4) * 2 + c
        self.dn = ((y + 3) % 4) * 2 + c
        self.op = ((y + 2) % 4) * 2 + c
        self.flip = 1 - 2 * c
        self.sib = h + self.flip

    def copy(self, block, start, size, to, sem, land):
        view = self.full.at[pl.ds(block * 128 + start, size), :]
        copy = pltpu.make_async_remote_copy(
            src_ref=view, dst_ref=view, send_sem=self.send.at[sem], recv_sem=self.recv.at[land],
            device_id={"head": to}, device_id_type=MESH,
        )
        copy.start()
        self.used.append(copy)
        return copy

    def begin(self):
        own = self.own
        self.dn_a = self.copy(own, 0, 64, self.up, 0, 0)
        self.up_b = self.copy(own, 64, 64, self.dn, 1, 3)
        self.side = self.copy(own, 0, 128, self.sib, 4, 6)
        self.dn_b = self.copy(own, 64, 64, self.up, 2, 1)
        self.up_a = self.copy(own, 0, 64, self.dn, 3, 2)

    def forward(self):
        self.dn_a.wait_recv()
        self.op_a = self.copy(self.dn, 0, 64, self.up, 5, 4)
        self.side_dn_a = self.copy(self.dn, 0, 64, self.sib, 6, 7)
        self.up_b.wait_recv()
        self.op_b = self.copy(self.up, 64, 64, self.dn, 7, 5)
        self.side_up_b = self.copy(self.up, 64, 64, self.sib, 8, 8)

    def near(self):
        self.dn_b.wait_recv()
        self.side_dn_b = self.copy(self.dn, 64, 64, self.sib, 9, 9)
        self.up_a.wait_recv()
        self.side_up_a = self.copy(self.up, 0, 64, self.sib, 10, 10)

    def far(self):
        self.op_a.wait_recv()
        self.side_op_a = self.copy(self.op, 0, 64, self.sib, 11, 11)
        self.op_b.wait_recv()
        self.side_op_b = self.copy(self.op, 64, 64, self.sib, 12, 12)

    def finish(self):
        for copy in self.used:
            copy.wait_send()


def head_sum():
    row = lax.broadcasted_iota(jnp.int32, (1024, 128), 0) // 64
    col = lax.broadcasted_iota(jnp.int32, (1024, 128), 1)
    return (row == col).astype(F32).astype(BF)


def head_spread():
    row = lax.broadcasted_iota(jnp.int32, (128, 1024), 0)
    col = lax.broadcasted_iota(jnp.int32, (128, 1024), 1) // 64
    return (row == col).astype(F32).astype(BF)


NX, NZ = 4, 8
A, B = slice(0, 64), slice(64, 128)


def middle(grid_ref, wf_ref, est_ref, kv, query, bg, mix):
    hsum = head_sum()
    spread = head_spread()

    def part(i, _):
        at = pl.multiple_of(i * 128, 128)
        rows = [pl.ds(at + e * 256, 128) for e in range(3)]
        qf = query[pl.ds(at, 128), :].astype(F32)
        back = bg[pl.ds(at, 128), :]
        products = [(qf * kv[r, :1024].astype(F32)).astype(BF) for r in rows]
        products += [(back * kv[r, 1024:].astype(F32)).astype(BF) for r in rows]
        sums = nn(jnp.concatenate(products, axis=0), hsum)
        score = [sums[e * 128 : e * 128 + 128] * SCALE for e in range(3)]
        along = [sums[e * 128 + 384 : e * 128 + 512] for e in range(3)]
        top = jnp.maximum(jnp.maximum(score[0], score[1]), score[2])
        term = [jnp.exp(s - top) for s in score]
        total = term[0] + term[1] + term[2]
        weight = [t / total for t in term]
        mean = weight[0] * along[0] + weight[1] * along[1] + weight[2] * along[2]
        heads = [w.astype(BF) for w in weight]
        heads += [(w * (s - mean) * SCALE).astype(BF) for w, s in zip(weight, along)]
        mixed = jnp.zeros((128, 1024), F32)
        for e in range(3):
            wide = nn(heads[e], spread)
            mixed += wide * kv[rows[e], 1024:].astype(F32)
            grad = nn(heads[3 + e], spread)
            kv[rows[e], :1024] = (grad * qf).astype(BF)
            kv[rows[e], 1024:] = (wide * back).astype(BF)
        mix[pl.ds(at, 128), :] = mixed.astype(BF)
        return 0

    lax.fori_loop(0, 2, part, 0)
    est_ref[...] = grid_ref[0:100, :].astype(F32) + nt(wf_ref[...], mix[...])


DMA = pltpu.SemaphoreType.DMA
SCRATCH = {
    "grid_v": ((112, 256), BF), "emb_v": ((128, 1024), BF), "src_v": ((16, 128), jnp.int32),
    "len_v": ((1, 128), jnp.int32), "wkv_v": ((112, 2048), BF), "pgain_v": ((1, 1024), F32),
    "wqkv_v": ((1024, 384), BF), "dgain_v": ((1, 1024), F32), "hid": ((128, 1024), F32),
    "full": ((1024, 1024), BF), "wfull": ((1024, 1024), BF), "q": ((1024, 128), BF),
    "kx": ((1536, 128), BF), "vx": ((1536, 128), BF), "att": ((1024, 128), BF), "afull": ((128, 1024), BF),
    "unit": ((128, 1024), F32), "inv": ((128, 128), F32), "send_v": ((32, 32), jnp.int32),
    "mine": ((NZ, 8, 128), jnp.int32), "dfc_v": ((100, 256), BF), "dsrc_v": ((3, 256), jnp.int32),
    "wq_v": ((112, 1024), BF), "wf_v": ((100, 1024), BF), "u_v": ((1024, 2048), BF),
    "zbuf": ((NZ, 128, 1024), BF), "tab": ((NZ, 8, 128), jnp.int32), "xs": ((8, 128, 1024), BF),
    "arrived": ((8, 128, 1024), BF), "kv": ((768, 2048), BF), "query": ((256, 1024), BF),
    "bg": ((256, 1024), F32), "mix": ((256, 1024), BF), "rg": ((768, 1024), BF),
    "bs": ((8, 128, 1024), BF), "rback": ((8, 128, 1024), BF), "outs": ((2, 4, 128, 1024), BF),
    "ins": ((2, 4, 128, 1024), BF),
}
SEMS = {
    "load": 18, "nsend": 13, "nrecv": 13, "wsend": 13, "wrecv": 13, "hsend": 4, "hrecv": 4, "asend": 8,
    "arecv": 8, "tsend": 8, "trecv": 8, "zsend": 16, "zrecv": 16, "xsend": 32, "xrecv": 32, "bsend": 32,
    "brecv": 32, "qsend": 16, "qrecv": 16,
}
INPUTS = (
    "grid_h", "emb_h", "src_h", "len_h", "wkv_h", "pgain_h", "wqkv_h", "wout_h", "dgain_h", "u_h", "wq_h",
    "wf_h", "send_h", "dsrc_h", "dfc_h",
)


class Refs:
    def __init__(self, refs):
        for name, ref in zip(INPUTS + ("est_o", "vert_o") + tuple(SCRATCH) + tuple(SEMS), refs):
            setattr(self, name, ref)


def start_loads(r, h):
    own = pl.ds(pl.multiple_of(h * 128, 128), 128)
    pairs = [
        (r.wout_h, r.wfull.at[own, :]), (r.send_h, r.send_v), (r.grid_h, r.grid_v), (r.emb_h, r.emb_v),
        (r.src_h, r.src_v), (r.len_h, r.len_v), (r.wkv_h, r.wkv_v), (r.pgain_h, r.pgain_v),
        (r.wqkv_h.at[0], r.wqkv_v.at[:, 0:128]), (r.wqkv_h.at[1], r.wqkv_v.at[:, 128:256]),
        (r.wqkv_h.at[2], r.wqkv_v.at[:, 256:384]), (r.dgain_h, r.dgain_v), (r.dfc_h, r.dfc_v),
        (r.dsrc_h, r.dsrc_v), (r.wq_h, r.wq_v), (r.wf_h, r.wf_v), (r.u_h, r.u_v),
    ]
    loads = [pltpu.make_async_copy(s, d, r.load.at[i]) for i, (s, d) in enumerate(pairs)]
    for copy in loads:
        copy.start()
    return loads


def kernel(*refs):
    r = Refs(refs)
    g = lax.axis_index("grp")
    h = lax.axis_index("head")
    groups = lax.axis_size("grp")
    right, left = (g + 1) % groups, (g + groups - 1) % groups
    x, z = g // NZ, g % NZ
    nexts = [(z + 1) % NZ, (z + NZ - 1) % NZ]
    loads = start_loads(r, h)
    barrier = pltpu.get_barrier_semaphore()
    for i in range(1, 8):
        pl.semaphore_signal(barrier, inc=1, device_id={"head": (h + i) % 8}, device_id_type=MESH)
    for k in range(1, NZ):
        pl.semaphore_signal(barrier, inc=1, device_id={"grp": x * NZ + (z + k) % NZ}, device_id_type=MESH)
    for k in range(1, NX):
        pl.semaphore_signal(barrier, inc=1, device_id={"grp": (x + k) % NX * NZ + z}, device_id_type=MESH)
    for other in (right, left):
        pl.semaphore_signal(barrier, inc=1, device_id={"grp": other}, device_id_type=MESH)
    loads[1].wait()
    table = jnp.concatenate([r.send_v[8 * k : 8 * k + 8, :] for k in range(NX)], axis=1)
    for k in range(NZ):
        r.mine[k] = jnp.broadcast_to(table[k : k + 1, :], (8, 128))
    pl.semaphore_wait(barrier, 7 + NZ + NX - 2 + 2)
    loads[0].wait()
    weights = Ring(r.wfull, r.wsend, r.wrecv)
    weights.begin()

    def remote(source, target, send, recv, xx, zz):
        copy = pltpu.make_async_remote_copy(
            src_ref=source, dst_ref=target, send_sem=send, recv_sem=recv,
            device_id={"grp": xx * NZ + zz}, device_id_type=MESH,
        )
        copy.start()
        return copy

    r.tab[pl.ds(z, 1)] = r.mine[pl.ds(z, 1)]
    tables = [
        remote(r.mine.at[(z + k) % NZ], r.tab.at[z], r.tsend.at[k], r.trecv.at[k], x, (z + k) % NZ)
        for k in range(1, NZ)
    ]
    for copy in loads[2:8]:
        copy.wait()
    encode(r.grid_v, r.emb_v, r.src_v, r.len_v, r.wkv_v, r.hid)
    unit, _ = norm_rows(r.hid[...])
    r.full[pl.ds(pl.multiple_of(h * 128, 128), 128), :] = (unit * r.pgain_v[...]).astype(BF)
    rows = Ring(r.full, r.nsend, r.nrecv)
    rows.begin()
    for copy in loads[8:16]:
        copy.wait()

    def project(block):
        at = pl.multiple_of(block * 128, 128)
        triple = nn(r.full[pl.ds(at, 128), :], r.wqkv_v[...]).astype(BF)
        r.q[pl.ds(at, 128), :] = (triple[:, :128].astype(F32) * SCALE).astype(BF)
        r.kx[pl.ds(at + 256, 128), :] = triple[:, 128:256]
        r.vx[pl.ds(at + 256, 128), :] = triple[:, 256:]

    flip = rows.flip
    project(h)
    rows.side.wait_recv()
    rows.forward()
    project(rows.sib)
    rows.near()
    project(rows.dn)
    project(rows.up)
    rows.side_dn_a.wait_recv()
    rows.side_dn_b.wait_recv()
    project(rows.dn + flip)
    rows.side_up_a.wait_recv()
    rows.side_up_b.wait_recv()
    project(rows.up + flip)
    rows.far()
    project(rows.op)
    rows.side_op_a.wait_recv()
    rows.side_op_b.wait_recv()
    project(rows.op + flip)

    halos = []
    for i, ref in enumerate((r.kx, r.vx)):
        for j, (start, land, to) in enumerate(((1024, 0, right), (256, 1280, left))):
            copy = pltpu.make_async_remote_copy(
                src_ref=ref.at[pl.ds(start, 256), :], dst_ref=ref.at[pl.ds(land, 256), :],
                send_sem=r.hsend.at[i * 2 + j], recv_sem=r.hrecv.at[i * 2 + j],
                device_id={"grp": to}, device_id_type=MESH,
            )
            copy.start()
            halos.append(copy)
    weights.forward()
    weights.near()

    def give(start, column, to, land):
        return pltpu.make_async_remote_copy(
            src_ref=r.att.at[pl.ds(start, 128), :], dst_ref=r.afull.at[:, pl.ds(column, 128)],
            send_sem=r.asend.at[to], recv_sem=r.arecv.at[land],
            device_id={"head": to}, device_id_type=MESH,
        )

    mine = pl.multiple_of(h * 128, 128)
    for blk in (1, 2, 0, 3):
        if blk == 0:
            weights.far()
            for copy in halos:
                copy.wait_recv()
        low = jnp.where(g == 0, 256, 0) if blk == 0 else 0
        high = jnp.where(g == groups - 1, 512, 768) if blk == 3 else 768
        attend(r.q, r.kx, r.vx, r.att, blk, low, high)
        for to in (2 * blk, 2 * blk + 1):

            @pl.when(to != h)
            def _():
                give(to * 128, mine, to, h).start()

    r.afull[:, pl.ds(mine, 128)] = r.att[pl.ds(mine, 128), :]
    r.query[...] = tn(r.grid_v[...], r.wq_v[...]).astype(BF)
    r.bg[...] = tn(r.dfc_v[...], r.wf_v[...])
    three = jnp.concatenate([r.dsrc_v[...], jnp.zeros((5, 256), jnp.int32)], axis=0)
    edges = three.astype(F32).T.astype(jnp.int32)
    for copy in (
        weights.side, weights.side_dn_a, weights.side_dn_b, weights.side_up_a, weights.side_up_b,
        weights.side_op_a, weights.side_op_b,
    ):
        copy.wait_recv()
    for other in range(8):

        @pl.when(other != h)
        def _():
            give(0, other * 128, other, other).wait()

    unit, inverse = norm_rows(r.hid[...] + nn(r.afull[...], r.wfull[...]))
    r.zbuf[z] = (unit * r.dgain_v[...]).astype(BF)
    sent = list(tables) + halos
    ring = {}

    def pass_on(way, d, chunk):
        block = (z + d) % NZ if way else (z + NZ - d) % NZ
        view = r.zbuf.at[block, pl.ds(64 * chunk, 64), :]
        sem = way * 8 + d * 2 + chunk
        ring[way, d, chunk] = remote(view, view, r.zsend.at[sem], r.zrecv.at[sem], x, nexts[way])
        sent.append(ring[way, d, chunk])

    hops = ((0, 0), (1, 1), (0, 1), (1, 0))
    for way, chunk in hops:
        pass_on(way, 0, chunk)
    r.unit[...] = unit
    r.inv[...] = jnp.broadcast_to(inverse, (128, 128))

    def where(index):
        if index == 0:
            return z
        return (z + (NZ - (index + 1) // 2 if index % 2 else index // 2)) % NZ

    def chosen(zz):
        node = lax.broadcasted_iota(jnp.int32, (128, 128), 0)
        return (node == r.tab[zz][0:1, :]).astype(F32).astype(BF)

    crossing = {}
    land = pl.ds(pl.multiple_of(x * 32, 32), 32)

    def select(index):
        zz = where(index)
        r.xs[index] = tn(chosen(zz), r.zbuf[zz]).astype(BF)
        for k in range(1, NX):
            xx = (x + k) % NX
            sem = index * NX + k
            crossing[index, k] = remote(
                r.xs.at[index, pl.ds(pl.multiple_of(xx * 32, 32), 32), :], r.arrived.at[index, land, :],
                r.xsend.at[sem], r.xrecv.at[sem], xx, z,
            )
        r.arrived[index, land, :] = r.xs[index, land, :]

    def absorb(first, count, tiles):
        if tiles[0] == 0:
            for index in range(first, first + count):
                for k in range(1, NX):
                    crossing[index, k].wait_recv()
        lane = lax.broadcasted_iota(jnp.int32, (1, 128), 1)
        slots = jnp.concatenate(
            [(lane // 32 * NZ + where(first + j)) * 32 + lane % 32 for j in range(count)], axis=1
        )
        picks = jnp.concatenate(
            [(edges[:, e : e + 1] == slots).astype(F32).astype(BF) for e in range(3)], axis=0
        )

        def tile(j, _):
            cols = pl.ds(pl.multiple_of(j * 256, 256), 256)
            block = r.arrived[first : first + count].reshape(count * 128, 1024)
            value = nn(picks, nn(block, r.u_v[:, cols]).astype(BF)).astype(BF)
            r.kv[:, cols] = value if first == 0 else r.kv[:, cols] + value
            return 0

        lax.fori_loop(*tiles, tile, 0)

    for copy in tables:
        copy.wait_recv()
    loads[16].wait()
    select(0)
    for d in range(1, 5):
        for way, chunk in hops:
            if d == 3 and (way, chunk) == (0, 1):
                absorb(0, 3, (4, 8))
            last = way == chunk
            if d < 4 or last:
                ring[way, d - 1, chunk].wait_recv()
            if d < 3 or (d == 3 and last):
                pass_on(way, d, chunk)
        if d < 4:
            select(2 * d - 1)
            select(2 * d)
        else:
            select(7)
        if d == 2:
            absorb(0, 3, (0, 4))
    absorb(3, 2, (0, 8))
    absorb(5, 2, (0, 8))
    absorb(7, 1, (0, 8))
    middle(r.grid_v, r.wf_v, r.est_o, r.kv, r.query, r.bg, r.mix)

    def unproject(j, _):
        cols = pl.ds(pl.multiple_of(j * 256, 256), 256)
        r.rg[:, cols] = nt(r.kv[...], r.u_v[cols, :]).astype(BF)
        return 0

    lax.fori_loop(0, 4, unproject, 0)
    returning = {}

    def scatter(index):
        zz = where(index)
        row = lax.broadcasted_iota(jnp.int32, (128, 256), 0)
        slot = (row // 32 * NZ + zz) * 32 + row % 32
        pick = jnp.concatenate(
            [(r.dsrc_v[e : e + 1, :] == slot).astype(F32).astype(BF) for e in range(3)], axis=1
        )
        r.bs[index] = nn(pick, r.rg[...]).astype(BF)
        for k in range(1, NX):
            xx = (x + k) % NX
            sem = index * NX + k
            returning[index, k] = remote(
                r.bs.at[index, pl.ds(pl.multiple_of(xx * 32, 32), 32), :], r.rback.at[index, land, :],
                r.bsend.at[sem], r.brecv.at[sem], xx, z,
            )
        r.rback[index, land, :] = r.bs[index, land, :]

    def partial(index):
        for k in range(1, NX):
            returning[index, k].wait_recv()
        return nn(chosen(where(index)), r.rback[index])

    flow = {}

    def push(way, i, chunk):
        rows = pl.ds(64 * chunk, 64)
        sem = way * 8 + i * 2 + chunk
        flow[way, i, chunk] = remote(
            r.outs.at[way, i, rows, :], r.ins.at[way, i, rows, :], r.qsend.at[sem], r.qrecv.at[sem],
            x, nexts[way],
        )

    def step(d):
        for way in range(2):
            part = partial(2 * d - way)
            for chunk in (way, 1 - way):
                rows = B if chunk else A
                value = part[rows]
                if d < 3 or chunk == way:
                    flow[way, d, chunk].wait_recv()
                    value = value + r.ins[way, d, rows].astype(F32)
                r.outs[way, d - 1, rows] = value.astype(BF)
                push(way, d - 1, chunk)

    scatter(7)
    scatter(6)
    scatter(5)
    part = partial(7)
    r.outs[0, 3, A] = part[A].astype(BF)
    push(0, 3, 0)
    r.outs[1, 3, B] = part[B].astype(BF)
    push(1, 3, 1)
    scatter(4)
    scatter(3)
    step(3)
    scatter(2)
    scatter(1)
    scatter(0)
    step(2)
    step(1)
    part = partial(0)
    for way in range(2):
        for chunk in range(2):
            flow[way, 0, chunk].wait_recv()
    grad = part + r.ins[0, 0].astype(F32) + r.ins[1, 0].astype(F32)
    unit = r.unit[...]
    scaled = grad * r.dgain_v[...]
    first = jnp.mean(scaled, axis=-1, keepdims=True)
    second = jnp.mean(scaled * unit, axis=-1, keepdims=True)
    r.vert_o[...] = r.inv[:, 0:1] * (scaled - first - unit * second)
    rows.finish()
    weights.finish()
    for copy in sent + list(crossing.values()) + list(returning.values()) + list(flow.values()):
        copy.wait_send()


VM = pl.BlockSpec(memory_space=pltpu.VMEM)
OUT = (jax.ShapeDtypeStruct((100, 256), F32), jax.ShapeDtypeStruct((128, 1024), F32))


def hand_over(a_ref, b_ref, c_ref, d_ref):
    c_ref[...] = a_ref[...]
    d_ref[...] = b_ref[...]


def body(
    grid_in, mesh_embed, enc_src, enc_len, enc_kv_weight, proc_gain, qkv_weight, out_weight,
    dec_gain, unpack, wq, wf, dec_send, dec_src, dforecast,
):
    est, vert = pl.pallas_call(
        kernel,
        out_shape=OUT,
        in_specs=[pl.BlockSpec(memory_space=pl.ANY)] * 15,
        out_specs=(VM, VM),
        scratch_shapes=[pltpu.VMEM(*s) for s in SCRATCH.values()] + [DMA((n,)) for n in SEMS.values()],
        compiler_params=pltpu.CompilerParams(
            vmem_limit_bytes=60 * 2**20, collective_id=0, has_side_effects=True
        ),
    )(
        grid_in, mesh_embed, enc_src, enc_len.reshape(1, -1), enc_kv_weight, proc_gain.reshape(1, -1),
        qkv_weight.transpose(1, 0, 2), out_weight, dec_gain.reshape(1, -1), unpack, wq, wf, dec_send,
        dec_src, dforecast,
    )
    return pl.pallas_call(
        hand_over, out_shape=OUT, in_specs=[VM, VM], out_specs=(VM, VM)
    )(est, vert)


def solution(mesh):
    return jax.shard_map(
        body,
        mesh=mesh,
        in_specs=(
            P(None, ("grp", "head")), P(("grp", "head"), None), P(None, ("grp", "head")),
            P(("grp", "head")), P(), P(), P(None, None, "head"), P("head", None), P(), P(), P(), P(),
            P(("grp", "head"), None), P(None, ("grp", "head")), P(None, ("grp", "head")),
        ),
        out_specs=(P(None, ("grp", "head")), P(("grp", "head"), None)),
        check_vma=False,
    )
```

```python
import jax
import jax.numpy as jnp
from jax import lax
from jax.experimental import pallas as pl
from jax.experimental.pallas import tpu as pltpu
from jax.sharding import PartitionSpec as P

F32 = jnp.float32
BF = jnp.bfloat16
EPS = 1e-05
SCALE = 0.125


def nn(a, b):
    return lax.dot_general(a, b, (((1,), (0,)), ((), ())), preferred_element_type=F32)


def nt(a, b):
    return lax.dot_general(a, b, (((1,), (1,)), ((), ())), preferred_element_type=F32)


def tn(a, b):
    return lax.dot_general(a, b, (((0,), (0,)), ((), ())), preferred_element_type=F32)


def half_masks():
    lane = lax.broadcasted_iota(jnp.int32, (1, 128), 1)
    return [(lane < 64).astype(F32).astype(BF), (lane >= 64).astype(F32).astype(BF)]


def norm_rows(rows):
    row_mean = jnp.mean(rows, axis=-1, keepdims=True)
    centred = rows - row_mean
    spread = jnp.mean(centred * centred, axis=-1, keepdims=True)
    inverse = lax.rsqrt(spread + EPS)
    return centred * inverse, inverse


def encode(grid_ref, emb_ref, src_ref, len_ref, wkv_ref, hid_ref):
    points = grid_ref.shape[1]
    nodes = emb_ref.shape[0]
    pid = lax.broadcasted_iota(jnp.int32, (points, nodes), 0)
    count = jnp.zeros((points, nodes), F32)
    lens = len_ref[...]
    for e in range(src_ref.shape[0]):
        row = jnp.where(e < lens, src_ref[e : e + 1, :], -1)
        count += (pid == row).astype(F32)
    dead = jnp.where(count > 0, 0.0, -jnp.inf)
    grid_t = grid_ref[...].T
    masks = half_masks()

    def pair(j, _):
        cols = pl.ds(j * 128, 128)
        vcols = pl.ds(j * 128 + 1024, 128)
        keys = nn(grid_t, wkv_ref[:, cols]).astype(BF)
        values = nn(grid_t, wkv_ref[:, vcols]).astype(BF)
        emb = emb_ref[:, cols]
        weights = []
        for n in range(2):
            score = nt(keys, emb * masks[n]) * SCALE + dead
            top = jnp.max(score, axis=0, keepdims=True)
            term = jnp.exp(score - top) * count
            weights.append((term / jnp.sum(term, axis=0, keepdims=True)).astype(BF))
        mixed = tn(weights[0], values * masks[0]) + tn(weights[1], values * masks[1])
        hid_ref[:, cols] = emb.astype(F32) + mixed
        return 0

    for j in range(emb_ref.shape[1] // 128):
        pair(j, 0)


def attend(q_ref, kv_ref, out_ref, blk, low, high):
    masks = half_masks()
    rows = pl.ds(blk * 256, 256)
    span = pl.ds(blk * 256, 768)
    q = q_ref[rows, :]
    k = kv_ref[span, 0:128]
    v = kv_ref[span, 128:256]
    gap = lax.broadcasted_iota(jnp.int32, (256, 768), 1) - lax.broadcasted_iota(
        jnp.int32, (256, 768), 0
    )
    col = lax.broadcasted_iota(jnp.int32, (256, 768), 1)
    live = (gap >= 0) & (gap <= 512) & (col >= low) & (col < high)
    total = None
    for n in range(2):
        score = jnp.where(live, nt(q * masks[n], k), -jnp.inf)
        top = jnp.max(score, axis=1, keepdims=True)
        term = jnp.exp(score - top)
        part = nn(term.astype(BF), v * masks[n]) / jnp.sum(term, axis=1, keepdims=True)
        total = part if total is None else total + part
    out_ref[rows, :] = total.astype(BF)


MESH = pl.DeviceIdType.MESH


class Ring:
    def __init__(self, full, send, recv):
        h = lax.axis_index("head")
        y, c = h // 2, h % 2
        self.full, self.send, self.recv, self.used = full, send, recv, []
        self.own = h
        self.up = ((y + 1) % 4) * 2 + c
        self.dn = ((y + 3) % 4) * 2 + c
        self.op = ((y + 2) % 4) * 2 + c
        self.flip = 1 - 2 * c
        self.sib = h + self.flip

    def copy(self, block, start, size, to, sem, land):
        view = self.full.at[pl.ds(block * 128 + start, size), :]
        copy = pltpu.make_async_remote_copy(
            src_ref=view, dst_ref=view, send_sem=self.send.at[sem], recv_sem=self.recv.at[land],
            device_id={"head": to}, device_id_type=MESH,
        )
        copy.start()
        self.used.append(copy)
        return copy

    def begin(self):
        own = self.own
        self.dn_a = self.copy(own, 0, 64, self.up, 0, 0)
        self.up_b = self.copy(own, 64, 64, self.dn, 1, 3)
        self.side = self.copy(own, 0, 128, self.sib, 4, 6)
        self.dn_b = self.copy(own, 64, 64, self.up, 2, 1)
        self.up_a = self.copy(own, 0, 64, self.dn, 3, 2)

    def forward(self):
        self.dn_a.wait_recv()
        self.op_a = self.copy(self.dn, 0, 64, self.up, 5, 4)
        self.side_dn_a = self.copy(self.dn, 0, 64, self.sib, 6, 7)
        self.up_b.wait_recv()
        self.op_b = self.copy(self.up, 64, 64, self.dn, 7, 5)
        self.side_up_b = self.copy(self.up, 64, 64, self.sib, 8, 8)

    def near(self):
        self.dn_b.wait_recv()
        self.side_dn_b = self.copy(self.dn, 64, 64, self.sib, 9, 9)
        self.up_a.wait_recv()
        self.side_up_a = self.copy(self.up, 0, 64, self.sib, 10, 10)

    def far(self):
        self.op_a.wait_recv()
        self.side_op_a = self.copy(self.op, 0, 64, self.sib, 11, 11)
        self.op_b.wait_recv()
        self.side_op_b = self.copy(self.op, 64, 64, self.sib, 12, 12)

    def finish(self):
        for copy in self.used:
            copy.wait_send()


def head_sum():
    row = lax.broadcasted_iota(jnp.int32, (1024, 128), 0) // 64
    col = lax.broadcasted_iota(jnp.int32, (1024, 128), 1)
    return (row == col).astype(F32).astype(BF)


def head_spread():
    row = lax.broadcasted_iota(jnp.int32, (128, 1024), 0)
    col = lax.broadcasted_iota(jnp.int32, (128, 1024), 1) // 64
    return (row == col).astype(F32).astype(BF)


NX, NZ = 4, 8
HALF = (slice(0, 512), slice(512, 1024))


def middle(kv, query, bg, mix):
    hsum = head_sum()
    spread = head_spread()

    def part(i, _):
        at = pl.multiple_of(i * 128, 128)
        rows = [pl.ds(at + e * 256, 128) for e in range(3)]
        qf = query[pl.ds(at, 128), :].astype(F32)
        back = bg[pl.ds(at, 128), :]
        products = [(qf * kv[r, :1024].astype(F32)).astype(BF) for r in rows]
        products += [(back * kv[r, 1024:].astype(F32)).astype(BF) for r in rows]
        sums = nn(jnp.concatenate(products, axis=0), hsum)
        score = [sums[e * 128 : e * 128 + 128] * SCALE for e in range(3)]
        along = [sums[e * 128 + 384 : e * 128 + 512] for e in range(3)]
        top = jnp.maximum(jnp.maximum(score[0], score[1]), score[2])
        term = [jnp.exp(s - top) for s in score]
        total = term[0] + term[1] + term[2]
        weight = [t / total for t in term]
        mean = weight[0] * along[0] + weight[1] * along[1] + weight[2] * along[2]
        heads = [w.astype(BF) for w in weight]
        heads += [(w * (s - mean) * SCALE).astype(BF) for w, s in zip(weight, along)]
        mixed = jnp.zeros((128, 1024), F32)
        for e in range(3):
            wide = nn(heads[e], spread)
            mixed += wide * kv[rows[e], 1024:].astype(F32)
            grad = nn(heads[3 + e], spread)
            kv[rows[e], :1024] = (grad * qf).astype(BF)
            kv[rows[e], 1024:] = (wide * back).astype(BF)
        mix[pl.ds(at, 128), :] = mixed.astype(BF)
        return 0

    lax.fori_loop(0, 2, part, 0)


DMA = pltpu.SemaphoreType.DMA
SCRATCH = {
    "grid_v": ((112, 256), BF), "emb_v": ((128, 1024), BF), "src_v": ((16, 128), jnp.int32),
    "len_v": ((1, 128), jnp.int32), "wkv_v": ((112, 2048), BF), "pgain_v": ((1, 1024), F32),
    "wqkv_v": ((1024, 384), BF), "dgain_v": ((1, 1024), F32), "hid": ((128, 1024), F32),
    "full": ((1024, 1024), BF), "wfull": ((1024, 1024), BF), "q": ((1024, 128), BF),
    "kvx": ((1536, 256), BF), "att": ((1024, 128), BF), "afull": ((128, 1024), BF),
    "unit": ((128, 1024), F32), "inv": ((128, 128), F32), "send_v": ((32, 32), jnp.int32),
    "mine": ((NZ, 8, 128), jnp.int32), "dfc_v": ((100, 256), BF), "dsrc_v": ((3, 256), jnp.int32),
    "wq_v": ((112, 1024), BF), "wf_v": ((100, 1024), BF), "u_v": ((1024, 2048), BF),
    "zbuf": ((NZ, 128, 1024), BF), "tab": ((NZ, 8, 128), jnp.int32), "xs": ((8, 128, 1024), BF),
    "arrived": ((8, 128, 1024), BF), "xe": ((768, 1024), BF), "kv": ((768, 2048), BF), "query": ((256, 1024), BF),
    "bg": ((256, 1024), F32), "mix": ((256, 1024), BF), "rg": ((768, 1024), BF),
    "bs": ((8, 128, 1024), BF), "rback": ((8, 128, 1024), BF), "outs": ((2, 4, 128, 1024), BF),
    "ins": ((2, 4, 128, 1024), BF),
}
SEMS = {
    "load": 18, "nsend": 13, "nrecv": 13, "wsend": 13, "wrecv": 13, "hsend": 4, "hrecv": 4, "asend": 8,
    "arecv": 8, "tsend": 8, "trecv": 8, "zsend": 16, "zrecv": 16, "xsend": 64, "xrecv": 64, "bsend": 64,
    "brecv": 64, "qsend": 16, "qrecv": 16,
}
INPUTS = (
    "grid_h", "emb_h", "src_h", "len_h", "wkv_h", "pgain_h", "wqkv_h", "wout_h", "dgain_h", "u_h", "wq_h",
    "wf_h", "send_h", "dsrc_h", "dfc_h",
)


class Refs:
    def __init__(self, refs):
        for name, ref in zip(INPUTS + ("est_o", "vert_o") + tuple(SCRATCH) + tuple(SEMS), refs):
            setattr(self, name, ref)


def start_loads(r, h):
    own = pl.ds(pl.multiple_of(h * 128, 128), 128)
    pairs = [
        (r.wout_h, r.wfull.at[own, :]), (r.send_h, r.send_v), (r.grid_h, r.grid_v), (r.emb_h, r.emb_v),
        (r.src_h, r.src_v), (r.len_h, r.len_v), (r.wkv_h, r.wkv_v), (r.pgain_h, r.pgain_v),
        (r.wqkv_h.at[0], r.wqkv_v.at[:, 0:128]), (r.wqkv_h.at[1], r.wqkv_v.at[:, 128:256]),
        (r.wqkv_h.at[2], r.wqkv_v.at[:, 256:384]), (r.dgain_h, r.dgain_v), (r.dfc_h, r.dfc_v),
        (r.dsrc_h, r.dsrc_v), (r.wq_h, r.wq_v), (r.wf_h, r.wf_v), (r.u_h, r.u_v),
    ]
    loads = [pltpu.make_async_copy(s, d, r.load.at[i]) for i, (s, d) in enumerate(pairs)]
    for copy in loads:
        copy.start()
    return loads


def kernel(*refs):
    r = Refs(refs)
    g = lax.axis_index("grp")
    h = lax.axis_index("head")
    groups = lax.axis_size("grp")
    right, left = (g + 1) % groups, (g + groups - 1) % groups
    x, z = g // NZ, g % NZ
    nexts = [(z + 1) % NZ, (z + NZ - 1) % NZ]
    loads = start_loads(r, h)
    barrier = pltpu.get_barrier_semaphore()
    for i in range(1, 8):
        pl.semaphore_signal(barrier, inc=1, device_id={"head": (h + i) % 8}, device_id_type=MESH)
    for k in range(1, NZ):
        pl.semaphore_signal(barrier, inc=1, device_id={"grp": x * NZ + (z + k) % NZ}, device_id_type=MESH)
    for k in range(1, NX):
        pl.semaphore_signal(barrier, inc=1, device_id={"grp": (x + k) % NX * NZ + z}, device_id_type=MESH)
    for other in (right, left):
        pl.semaphore_signal(barrier, inc=1, device_id={"grp": other}, device_id_type=MESH)
    loads[1].wait()
    table = jnp.concatenate([r.send_v[8 * k : 8 * k + 8, :] for k in range(NX)], axis=1)
    for k in range(NZ):
        r.mine[k] = jnp.broadcast_to(table[k : k + 1, :], (8, 128))
    pl.semaphore_wait(barrier, 7 + NZ + NX - 2 + 2)
    loads[0].wait()
    weights = Ring(r.wfull, r.wsend, r.wrecv)
    weights.begin()

    def remote(source, target, send, recv, xx, zz):
        copy = pltpu.make_async_remote_copy(
            src_ref=source, dst_ref=target, send_sem=send, recv_sem=recv,
            device_id={"grp": xx * NZ + zz}, device_id_type=MESH,
        )
        copy.start()
        return copy

    r.tab[pl.ds(z, 1)] = r.mine[pl.ds(z, 1)]
    tables = [
        remote(r.mine.at[(z + k) % NZ], r.tab.at[z], r.tsend.at[k], r.trecv.at[k], x, (z + k) % NZ)
        for k in range(1, NZ)
    ]
    for copy in loads[2:8]:
        copy.wait()
    encode(r.grid_v, r.emb_v, r.src_v, r.len_v, r.wkv_v, r.hid)
    unit, _ = norm_rows(r.hid[...])
    r.full[pl.ds(pl.multiple_of(h * 128, 128), 128), :] = (unit * r.pgain_v[...]).astype(BF)
    rows = Ring(r.full, r.nsend, r.nrecv)
    rows.begin()
    for copy in loads[8:16]:
        copy.wait()

    def halo(start, land, sem, to):
        return pltpu.make_async_remote_copy(
            src_ref=r.kvx.at[pl.ds(start, 128), :], dst_ref=r.kvx.at[pl.ds(land, 128), :],
            send_sem=r.hsend.at[sem], recv_sem=r.hrecv.at[sem],
            device_id={"grp": to}, device_id_type=MESH,
        )

    def project(block):
        at = pl.multiple_of(block * 128, 128)
        triple = nn(r.full[pl.ds(at, 128), :], r.wqkv_v[...]).astype(BF)
        r.q[pl.ds(at, 128), :] = (triple[:, :128].astype(F32) * SCALE).astype(BF)
        r.kvx[pl.ds(at + 256, 128), :] = triple[:, 128:]

        @pl.when(block >= 6)
        def _():
            halo(at + 256, at - 768, block - 6, right).start()

        @pl.when(block < 2)
        def _():
            halo(at + 256, at + 1280, block + 2, left).start()

    flip = rows.flip
    project(h)
    rows.side.wait_recv()
    rows.forward()
    project(rows.sib)
    rows.near()
    project(rows.dn)
    project(rows.up)
    rows.side_dn_a.wait_recv()
    rows.side_dn_b.wait_recv()
    project(rows.dn + flip)
    rows.side_up_a.wait_recv()
    rows.side_up_b.wait_recv()
    project(rows.up + flip)
    rows.far()
    project(rows.op)
    rows.side_op_a.wait_recv()
    rows.side_op_b.wait_recv()
    project(rows.op + flip)

    halos = [
        halo(1024, 0, 0, right), halo(1152, 128, 1, right), halo(256, 1280, 2, left), halo(384, 1408, 3, left),
    ]
    weights.forward()
    weights.near()

    def give(start, column, to, land):
        return pltpu.make_async_remote_copy(
            src_ref=r.att.at[pl.ds(start, 128), :], dst_ref=r.afull.at[:, pl.ds(column, 128)],
            send_sem=r.asend.at[to], recv_sem=r.arecv.at[land],
            device_id={"head": to}, device_id_type=MESH,
        )

    mine = pl.multiple_of(h * 128, 128)
    for blk in (1, 2, 0, 3):
        if blk == 0:
            weights.far()
            for copy in halos:
                copy.wait_recv()
        low = jnp.where(g == 0, 256, 0) if blk == 0 else 0
        high = jnp.where(g == groups - 1, 512, 768) if blk == 3 else 768
        attend(r.q, r.kvx, r.att, blk, low, high)
        for to in (2 * blk, 2 * blk + 1):

            @pl.when(to != h)
            def _():
                give(to * 128, mine, to, h).start()

    r.afull[:, pl.ds(mine, 128)] = r.att[pl.ds(mine, 128), :]
    r.query[...] = tn(r.grid_v[...], r.wq_v[...]).astype(BF)
    r.bg[...] = tn(r.dfc_v[...], r.wf_v[...])
    three = jnp.concatenate([r.dsrc_v[...], jnp.zeros((5, 256), jnp.int32)], axis=0)
    edges = three.astype(F32).T.astype(jnp.int32)
    for copy in (
        weights.side, weights.side_dn_a, weights.side_dn_b, weights.side_up_a, weights.side_up_b,
        weights.side_op_a, weights.side_op_b,
    ):
        copy.wait_recv()
    for other in range(8):

        @pl.when(other != h)
        def _():
            give(0, other * 128, other, other).wait()

    unit, inverse = norm_rows(r.hid[...] + nn(r.afull[...], r.wfull[...]))
    r.zbuf[z] = (unit * r.dgain_v[...]).astype(BF)
    sent = list(tables) + halos
    ring = {}

    def pass_on(way, d, chunk):
        block = (z + d) % NZ if way else (z + NZ - d) % NZ
        view = r.zbuf.at[block, :, pl.ds(512 * chunk, 512)]
        sem = way * 8 + d * 2 + chunk
        ring[way, d, chunk] = remote(view, view, r.zsend.at[sem], r.zrecv.at[sem], x, nexts[way])
        sent.append(ring[way, d, chunk])

    hops = ((0, 0), (1, 1), (0, 1), (1, 0))
    for way, chunk in hops:
        pass_on(way, 0, chunk)
    r.unit[...] = unit
    r.inv[...] = jnp.broadcast_to(inverse, (128, 128))

    def where(index):
        if index == 0:
            return z
        return (z + (NZ - (index + 1) // 2 if index % 2 else index // 2)) % NZ

    def chosen(zz):
        node = lax.broadcasted_iota(jnp.int32, (128, 128), 0)
        return (node == r.tab[zz][0:1, :]).astype(F32).astype(BF)

    crossing = {}
    land = pl.ds(pl.multiple_of(x * 32, 32), 32)

    def select(index, half):
        zz = where(index)
        cols = pl.ds(512 * half, 512)
        r.xs[index, :, HALF[half]] = tn(chosen(zz), r.zbuf[zz, :, HALF[half]]).astype(BF)
        for k in range(1, NX):
            xx = (x + k) % NX
            sem = index * 8 + half * NX + k
            crossing[index, half, k] = remote(
                r.xs.at[index, pl.ds(pl.multiple_of(xx * 32, 32), 32), cols], r.arrived.at[index, land, cols],
                r.xsend.at[sem], r.xrecv.at[sem], xx, z,
            )
        r.arrived[index, land, HALF[half]] = r.xs[index, land, HALF[half]]

    def absorb(first, count):
        for index in range(first, first + count):
            for half in range(2):
                for k in range(1, NX):
                    crossing[index, half, k].wait_recv()
        lane = lax.broadcasted_iota(jnp.int32, (1, 128), 1)
        slots = jnp.concatenate(
            [(lane // 32 * NZ + where(first + j)) * 32 + lane % 32 for j in range(count)], axis=1
        )
        picks = jnp.concatenate(
            [(edges[:, e : e + 1] == slots).astype(F32).astype(BF) for e in range(3)], axis=0
        )

        def tile(j, _):
            cols = pl.ds(pl.multiple_of(j * 256, 256), 256)
            block = r.arrived[first : first + count, :, cols].reshape(count * 128, 256)
            value = nn(picks, block).astype(BF)
            r.xe[:, cols] = value if first == 0 else r.xe[:, cols] + value
            return 0

        lax.fori_loop(0, 4, tile, 0)

    for copy in tables:
        copy.wait_recv()
    loads[16].wait()
    select(0, 0)
    select(0, 1)
    for d in range(1, 5):
        for phase in range(2):
            if d == 4 and phase == 1:
                continue
            for way in range(2):
                chunk = way ^ phase
                ring[way, d - 1, chunk].wait_recv()
                if d < 3 or (d == 3 and phase == 0):
                    pass_on(way, d, chunk)
            for way in range(2):
                select(7 if d == 4 else 2 * d - 1 + way, way ^ phase)
            if d == 2 and phase == 1:
                absorb(0, 3)
        if d == 3:
            absorb(3, 2)
    absorb(5, 3)

    def unpack(j, _):
        cols = pl.ds(pl.multiple_of(j * 256, 256), 256)
        r.kv[:, cols] = nn(r.xe[...], r.u_v[:, cols]).astype(BF)
        return 0

    lax.fori_loop(0, 8, unpack, 0)
    middle(r.kv, r.query, r.bg, r.mix)

    def unproject(j, _):
        cols = pl.ds(pl.multiple_of(j * 256, 256), 256)
        r.rg[:, cols] = nt(r.kv[...], r.u_v[cols, :]).astype(BF)
        return 0

    returning = {}

    def scatter(half, *indices):
        for index in indices:
            zz = where(index)
            row = lax.broadcasted_iota(jnp.int32, (128, 256), 0)
            slot = (row // 32 * NZ + zz) * 32 + row % 32
            pick = jnp.concatenate(
                [(r.dsrc_v[e : e + 1, :] == slot).astype(F32).astype(BF) for e in range(3)], axis=1
            )
            r.bs[index, :, HALF[half]] = nn(pick, r.rg[:, HALF[half]]).astype(BF)
            cols = pl.ds(512 * half, 512)
            for k in range(1, NX):
                xx = (x + k) % NX
                sem = index * 8 + half * NX + k
                returning[index, half, k] = remote(
                    r.bs.at[index, pl.ds(pl.multiple_of(xx * 32, 32), 32), cols],
                    r.rback.at[index, land, cols], r.bsend.at[sem], r.brecv.at[sem], xx, z,
                )
            r.rback[index, land, HALF[half]] = r.bs[index, land, HALF[half]]

    def partial(index, half):
        for k in range(1, NX):
            returning[index, half, k].wait_recv()
        return nn(chosen(where(index)), r.rback[index, :, HALF[half]])

    flow = {}

    def push(way, i, chunk, value):
        r.outs[way, i, :, HALF[chunk]] = value.astype(BF)
        cols = pl.ds(512 * chunk, 512)
        sem = way * 8 + i * 2 + chunk
        flow[way, i, chunk] = remote(
            r.outs.at[way, i, :, cols], r.ins.at[way, i, :, cols], r.qsend.at[sem], r.qrecv.at[sem],
            x, nexts[way],
        )

    def step(d):
        for phase in range(2):
            for way in range(2):
                chunk = way ^ phase
                value = partial(2 * d - way, chunk)
                if d < 3 or phase == 0:
                    flow[way, d, chunk].wait_recv()
                    value = value + r.ins[way, d, :, HALF[chunk]].astype(F32)
                push(way, d - 1, chunk, value)

    lax.fori_loop(0, 2, unproject, 0)
    scatter(0, 7, 6, 5)
    lax.fori_loop(2, 4, unproject, 0)
    scatter(1, 7, 6, 5)
    push(0, 3, 0, partial(7, 0))
    push(1, 3, 1, partial(7, 1))
    scatter(0, 4, 3)
    scatter(1, 4, 3)
    r.est_o[...] = r.grid_v[0:100, :].astype(F32) + nt(r.wf_v[...], r.mix[...])
    step(3)
    scatter(0, 2, 1, 0)
    scatter(1, 2, 1, 0)
    step(2)
    step(1)
    part = jnp.concatenate([partial(0, 0), partial(0, 1)], axis=1)
    for way in range(2):
        for chunk in range(2):
            flow[way, 0, chunk].wait_recv()
    grad = part + r.ins[0, 0].astype(F32) + r.ins[1, 0].astype(F32)
    unit = r.unit[...]
    scaled = grad * r.dgain_v[...]
    first = jnp.mean(scaled, axis=-1, keepdims=True)
    second = jnp.mean(scaled * unit, axis=-1, keepdims=True)
    r.vert_o[...] = r.inv[:, 0:1] * (scaled - first - unit * second)
    rows.finish()
    weights.finish()
    for copy in sent + list(crossing.values()) + list(returning.values()) + list(flow.values()):
        copy.wait_send()


VM = pl.BlockSpec(memory_space=pltpu.VMEM)
OUT = (jax.ShapeDtypeStruct((100, 256), F32), jax.ShapeDtypeStruct((128, 1024), F32))


def hand_over(a_ref, b_ref, c_ref, d_ref):
    c_ref[...] = a_ref[...]
    d_ref[...] = b_ref[...]


def body(
    grid_in, mesh_embed, enc_src, enc_len, enc_kv_weight, proc_gain, qkv_weight, out_weight,
    dec_gain, unpack, wq, wf, dec_send, dec_src, dforecast,
):
    est, vert = pl.pallas_call(
        kernel,
        out_shape=OUT,
        in_specs=[pl.BlockSpec(memory_space=pl.ANY)] * 15,
        out_specs=(VM, VM),
        scratch_shapes=[pltpu.VMEM(*s) for s in SCRATCH.values()] + [DMA((n,)) for n in SEMS.values()],
        compiler_params=pltpu.CompilerParams(
            vmem_limit_bytes=60 * 2**20, collective_id=0, has_side_effects=True
        ),
    )(
        grid_in, mesh_embed, enc_src, enc_len.reshape(1, -1), enc_kv_weight, proc_gain.reshape(1, -1),
        qkv_weight.transpose(1, 0, 2), out_weight, dec_gain.reshape(1, -1), unpack, wq, wf, dec_send,
        dec_src, dforecast,
    )
    return pl.pallas_call(
        hand_over, out_shape=OUT, in_specs=[VM, VM], out_specs=(VM, VM)
    )(est, vert)


def solution(mesh):
    return jax.shard_map(
        body,
        mesh=mesh,
        in_specs=(
            P(None, ("grp", "head")), P(("grp", "head"), None), P(None, ("grp", "head")),
            P(("grp", "head")), P(), P(), P(None, None, "head"), P("head", None), P(), P(), P(), P(),
            P(("grp", "head"), None), P(None, ("grp", "head")), P(None, ("grp", "head")),
        ),
        out_specs=(P(None, ("grp", "head")), P(("grp", "head"), None)),
        check_vma=False,
    )
```

```python
import jax
import jax.numpy as jnp
from jax import lax
from jax.experimental import pallas as pl
from jax.experimental.pallas import tpu as pltpu
from jax.sharding import PartitionSpec as P

F32 = jnp.float32
BF = jnp.bfloat16
EPS = 1e-05
SCALE = 0.125


def nn(a, b):
    return lax.dot_general(a, b, (((1,), (0,)), ((), ())), preferred_element_type=F32)


def nt(a, b):
    return lax.dot_general(a, b, (((1,), (1,)), ((), ())), preferred_element_type=F32)


def tn(a, b):
    return lax.dot_general(a, b, (((0,), (0,)), ((), ())), preferred_element_type=F32)


def half_masks():
    lane = lax.broadcasted_iota(jnp.int32, (1, 128), 1)
    return [(lane < 64).astype(F32).astype(BF), (lane >= 64).astype(F32).astype(BF)]


def norm_rows(rows):
    row_mean = jnp.mean(rows, axis=-1, keepdims=True)
    centred = rows - row_mean
    spread = jnp.mean(centred * centred, axis=-1, keepdims=True)
    inverse = lax.rsqrt(spread + EPS)
    return centred * inverse, inverse


def encode(grid_ref, emb_ref, src_ref, len_ref, wkv_ref, hid_ref):
    points = grid_ref.shape[1]
    nodes = emb_ref.shape[0]
    pid = lax.broadcasted_iota(jnp.int32, (points, nodes), 0)
    count = jnp.zeros((points, nodes), F32)
    lens = len_ref[...]
    for e in range(src_ref.shape[0]):
        row = jnp.where(e < lens, src_ref[e : e + 1, :], -1)
        count += (pid == row).astype(F32)
    dead = jnp.where(count > 0, 0.0, -jnp.inf)
    grid_t = grid_ref[...].T
    masks = half_masks()

    def pair(j, _):
        cols = pl.ds(j * 128, 128)
        vcols = pl.ds(j * 128 + 1024, 128)
        keys = nn(grid_t, wkv_ref[:, cols]).astype(BF)
        values = nn(grid_t, wkv_ref[:, vcols]).astype(BF)
        emb = emb_ref[:, cols]
        weights = []
        for n in range(2):
            score = nt(keys, emb * masks[n]) * SCALE + dead
            top = jnp.max(score, axis=0, keepdims=True)
            term = jnp.exp(score - top) * count
            weights.append((term / jnp.sum(term, axis=0, keepdims=True)).astype(BF))
        mixed = tn(weights[0], values * masks[0]) + tn(weights[1], values * masks[1])
        hid_ref[:, cols] = emb.astype(F32) + mixed
        return 0

    for j in range(emb_ref.shape[1] // 128):
        pair(j, 0)


def attend(q_ref, kv_ref, out_ref, blk, low, high):
    masks = half_masks()
    rows = pl.ds(blk * 256, 256)
    span = pl.ds(blk * 256, 768)
    q = q_ref[rows, :]
    k = kv_ref[span, 0:128]
    v = kv_ref[span, 128:256]
    gap = lax.broadcasted_iota(jnp.int32, (256, 768), 1) - lax.broadcasted_iota(
        jnp.int32, (256, 768), 0
    )
    col = lax.broadcasted_iota(jnp.int32, (256, 768), 1)
    live = (gap >= 0) & (gap <= 512) & (col >= low) & (col < high)
    total = None
    for n in range(2):
        score = jnp.where(live, nt(q * masks[n], k), -jnp.inf)
        top = jnp.max(score, axis=1, keepdims=True)
        term = jnp.exp(score - top)
        part = nn(term.astype(BF), v * masks[n]) / jnp.sum(term, axis=1, keepdims=True)
        total = part if total is None else total + part
    out_ref[rows, :] = total.astype(BF)


MESH = pl.DeviceIdType.MESH


class Ring:
    def __init__(self, full, send, recv):
        h = lax.axis_index("head")
        y, c = h // 2, h % 2
        self.full, self.send, self.recv, self.used = full, send, recv, []
        self.own = h
        self.up = ((y + 1) % 4) * 2 + c
        self.dn = ((y + 3) % 4) * 2 + c
        self.op = ((y + 2) % 4) * 2 + c
        self.flip = 1 - 2 * c
        self.sib = h + self.flip

    def copy(self, block, start, size, to, sem, land):
        view = self.full.at[pl.ds(block * 128 + start, size), :]
        copy = pltpu.make_async_remote_copy(
            src_ref=view, dst_ref=view, send_sem=self.send.at[sem], recv_sem=self.recv.at[land],
            device_id={"head": to}, device_id_type=MESH,
        )
        copy.start()
        self.used.append(copy)
        return copy

    def begin(self):
        own = self.own
        self.dn_a = self.copy(own, 0, 64, self.up, 0, 0)
        self.up_b = self.copy(own, 64, 64, self.dn, 1, 3)
        self.side = self.copy(own, 0, 128, self.sib, 4, 6)
        self.dn_b = self.copy(own, 64, 64, self.up, 2, 1)
        self.up_a = self.copy(own, 0, 64, self.dn, 3, 2)

    def forward(self):
        self.dn_a.wait_recv()
        self.op_a = self.copy(self.dn, 0, 64, self.up, 5, 4)
        self.side_dn_a = self.copy(self.dn, 0, 64, self.sib, 6, 7)
        self.up_b.wait_recv()
        self.op_b = self.copy(self.up, 64, 64, self.dn, 7, 5)
        self.side_up_b = self.copy(self.up, 64, 64, self.sib, 8, 8)

    def near(self):
        self.dn_b.wait_recv()
        self.side_dn_b = self.copy(self.dn, 64, 64, self.sib, 9, 9)
        self.up_a.wait_recv()
        self.side_up_a = self.copy(self.up, 0, 64, self.sib, 10, 10)

    def far(self):
        self.op_a.wait_recv()
        self.side_op_a = self.copy(self.op, 0, 64, self.sib, 11, 11)
        self.op_b.wait_recv()
        self.side_op_b = self.copy(self.op, 64, 64, self.sib, 12, 12)

    def finish(self):
        for copy in self.used:
            copy.wait_send()


def head_sum():
    row = lax.broadcasted_iota(jnp.int32, (1024, 128), 0) // 64
    col = lax.broadcasted_iota(jnp.int32, (1024, 128), 1)
    return (row == col).astype(F32).astype(BF)


def head_spread():
    row = lax.broadcasted_iota(jnp.int32, (128, 1024), 0)
    col = lax.broadcasted_iota(jnp.int32, (128, 1024), 1) // 64
    return (row == col).astype(F32).astype(BF)


NX, NZ = 4, 8
HALF = (slice(0, 512), slice(512, 1024))


def middle(kv, query, bg, mix):
    hsum = head_sum()
    spread = head_spread()

    def part(i, _):
        at = pl.multiple_of(i * 128, 128)
        rows = [pl.ds(at + e * 256, 128) for e in range(3)]
        qf = query[pl.ds(at, 128), :].astype(F32)
        back = bg[pl.ds(at, 128), :]
        products = [(qf * kv[r, :1024].astype(F32)).astype(BF) for r in rows]
        products += [(back * kv[r, 1024:].astype(F32)).astype(BF) for r in rows]
        sums = nn(jnp.concatenate(products, axis=0), hsum)
        score = [sums[e * 128 : e * 128 + 128] * SCALE for e in range(3)]
        along = [sums[e * 128 + 384 : e * 128 + 512] for e in range(3)]
        top = jnp.maximum(jnp.maximum(score[0], score[1]), score[2])
        term = [jnp.exp(s - top) for s in score]
        total = term[0] + term[1] + term[2]
        weight = [t / total for t in term]
        mean = weight[0] * along[0] + weight[1] * along[1] + weight[2] * along[2]
        heads = [w.astype(BF) for w in weight]
        heads += [(w * (s - mean) * SCALE).astype(BF) for w, s in zip(weight, along)]
        mixed = jnp.zeros((128, 1024), F32)
        for e in range(3):
            wide = nn(heads[e], spread)
            mixed += wide * kv[rows[e], 1024:].astype(F32)
            grad = nn(heads[3 + e], spread)
            kv[rows[e], :1024] = (grad * qf).astype(BF)
            kv[rows[e], 1024:] = (wide * back).astype(BF)
        mix[pl.ds(at, 128), :] = mixed.astype(BF)
        return 0

    lax.fori_loop(0, 2, part, 0)


DMA = pltpu.SemaphoreType.DMA
SCRATCH = {
    "grid_v": ((112, 256), BF), "emb_v": ((128, 1024), BF), "src_v": ((16, 128), jnp.int32),
    "len_v": ((1, 128), jnp.int32), "wkv_v": ((112, 2048), BF), "pgain_v": ((1, 1024), F32),
    "wqkv_v": ((1024, 384), BF), "dgain_v": ((1, 1024), F32), "hid": ((128, 1024), F32),
    "full": ((1024, 1024), BF), "wfull": ((1024, 1024), BF), "q": ((1024, 128), BF),
    "kvx": ((1536, 256), BF), "att": ((1024, 128), BF), "afull": ((128, 1024), BF),
    "unit": ((128, 1024), F32), "inv": ((128, 128), F32), "send_v": ((32, 32), jnp.int32),
    "mine": ((NZ, 8, 128), jnp.int32), "dfc_v": ((100, 256), BF), "dsrc_v": ((3, 256), jnp.int32),
    "wq_v": ((112, 1024), BF), "wf_v": ((100, 1024), BF), "u_v": ((1024, 2048), BF),
    "zbuf": ((NZ, 128, 1024), BF), "tab": ((NZ, 8, 128), jnp.int32), "xs": ((8, 128, 1024), BF),
    "arrived": ((8, 128, 1024), BF), "xe": ((768, 1024), BF), "kv": ((768, 2048), BF), "query": ((256, 1024), BF),
    "bg": ((256, 1024), F32), "mix": ((256, 1024), BF), "rg": ((768, 1024), BF),
    "bs": ((8, 128, 1024), BF), "rback": ((8, 128, 1024), BF), "outs": ((2, 4, 128, 1024), BF),
    "ins": ((2, 4, 128, 1024), BF),
}
SEMS = {
    "load": 18, "nsend": 13, "nrecv": 13, "wsend": 13, "wrecv": 13, "hsend": 4, "hrecv": 4, "asend": 8,
    "arecv": 8, "tsend": 8, "trecv": 8, "zsend": 16, "zrecv": 16, "xsend": 64, "xrecv": 64, "bsend": 64,
    "brecv": 64, "qsend": 16, "qrecv": 16,
}
INPUTS = (
    "grid_h", "emb_h", "src_h", "len_h", "wkv_h", "pgain_h", "wqkv_h", "wout_h", "dgain_h", "u_h", "wq_h",
    "wf_h", "send_h", "dsrc_h", "dfc_h",
)


class Refs:
    def __init__(self, refs):
        for name, ref in zip(INPUTS + ("est_o", "vert_o") + tuple(SCRATCH) + tuple(SEMS), refs):
            setattr(self, name, ref)


def start_loads(r, h):
    own = pl.ds(pl.multiple_of(h * 128, 128), 128)
    pairs = [
        (r.wout_h, r.wfull.at[own, :]), (r.send_h, r.send_v), (r.grid_h, r.grid_v), (r.emb_h, r.emb_v),
        (r.src_h, r.src_v), (r.len_h, r.len_v), (r.wkv_h, r.wkv_v), (r.pgain_h, r.pgain_v),
        (r.wqkv_h.at[0], r.wqkv_v.at[:, 0:128]), (r.wqkv_h.at[1], r.wqkv_v.at[:, 128:256]),
        (r.wqkv_h.at[2], r.wqkv_v.at[:, 256:384]), (r.dgain_h, r.dgain_v), (r.dfc_h, r.dfc_v),
        (r.dsrc_h, r.dsrc_v), (r.wq_h, r.wq_v), (r.wf_h, r.wf_v), (r.u_h, r.u_v),
    ]
    loads = [pltpu.make_async_copy(s, d, r.load.at[i]) for i, (s, d) in enumerate(pairs)]
    for copy in loads:
        copy.start()
    return loads


def kernel(*refs):
    r = Refs(refs)
    g = lax.axis_index("grp")
    h = lax.axis_index("head")
    groups = lax.axis_size("grp")
    right, left = (g + 1) % groups, (g + groups - 1) % groups
    x, z = g // NZ, g % NZ
    nexts = [(z + 1) % NZ, (z + NZ - 1) % NZ]
    loads = start_loads(r, h)
    barrier = pltpu.get_barrier_semaphore()
    for i in range(1, 8):
        pl.semaphore_signal(barrier, inc=1, device_id={"head": (h + i) % 8}, device_id_type=MESH)
    for k in range(1, NZ):
        pl.semaphore_signal(barrier, inc=1, device_id={"grp": x * NZ + (z + k) % NZ}, device_id_type=MESH)
    for k in range(1, NX):
        pl.semaphore_signal(barrier, inc=1, device_id={"grp": (x + k) % NX * NZ + z}, device_id_type=MESH)
    for other in (right, left):
        pl.semaphore_signal(barrier, inc=1, device_id={"grp": other}, device_id_type=MESH)
    loads[1].wait()
    table = jnp.concatenate([r.send_v[8 * k : 8 * k + 8, :] for k in range(NX)], axis=1)
    for k in range(NZ):
        r.mine[k] = jnp.broadcast_to(table[k : k + 1, :], (8, 128))

    def remote(source, target, send, recv, xx, zz):
        copy = pltpu.make_async_remote_copy(
            src_ref=source, dst_ref=target, send_sem=send, recv_sem=recv,
            device_id={"grp": xx * NZ + zz}, device_id_type=MESH,
        )
        copy.start()
        return copy

    for copy in loads[2:8]:
        copy.wait()
    encode(r.grid_v, r.emb_v, r.src_v, r.len_v, r.wkv_v, r.hid)
    unit, _ = norm_rows(r.hid[...])
    r.full[pl.ds(pl.multiple_of(h * 128, 128), 128), :] = (unit * r.pgain_v[...]).astype(BF)
    pl.semaphore_wait(barrier, 7 + NZ + NX - 2 + 2)
    rows = Ring(r.full, r.nsend, r.nrecv)
    rows.begin()
    r.tab[pl.ds(z, 1)] = r.mine[pl.ds(z, 1)]
    tables = [
        remote(r.mine.at[(z + k) % NZ], r.tab.at[z], r.tsend.at[k], r.trecv.at[k], x, (z + k) % NZ)
        for k in range(1, NZ)
    ]
    loads[0].wait()
    weights = Ring(r.wfull, r.wsend, r.wrecv)
    for copy in loads[8:16]:
        copy.wait()

    def halo(start, land, sem, to):
        return pltpu.make_async_remote_copy(
            src_ref=r.kvx.at[pl.ds(start, 128), :], dst_ref=r.kvx.at[pl.ds(land, 128), :],
            send_sem=r.hsend.at[sem], recv_sem=r.hrecv.at[sem],
            device_id={"grp": to}, device_id_type=MESH,
        )

    def project(block):
        at = pl.multiple_of(block * 128, 128)
        triple = nn(r.full[pl.ds(at, 128), :], r.wqkv_v[...]).astype(BF)
        r.q[pl.ds(at, 128), :] = (triple[:, :128].astype(F32) * SCALE).astype(BF)
        r.kvx[pl.ds(at + 256, 128), :] = triple[:, 128:]

        @pl.when(block >= 6)
        def _():
            halo(at + 256, at - 768, block - 6, right).start()

        @pl.when(block < 2)
        def _():
            halo(at + 256, at + 1280, block + 2, left).start()

    flip = rows.flip
    project(h)
    rows.side.wait_recv()
    rows.forward()
    project(rows.sib)
    rows.near()
    weights.begin()
    project(rows.dn)
    project(rows.up)
    rows.side_dn_a.wait_recv()
    rows.side_dn_b.wait_recv()
    project(rows.dn + flip)
    rows.side_up_a.wait_recv()
    rows.side_up_b.wait_recv()
    project(rows.up + flip)
    rows.far()
    project(rows.op)
    rows.side_op_a.wait_recv()
    rows.side_op_b.wait_recv()
    project(rows.op + flip)

    halos = [
        halo(1024, 0, 0, right), halo(1152, 128, 1, right), halo(256, 1280, 2, left), halo(384, 1408, 3, left),
    ]
    weights.forward()
    weights.near()

    def give(start, column, to, land):
        return pltpu.make_async_remote_copy(
            src_ref=r.att.at[pl.ds(start, 128), :], dst_ref=r.afull.at[:, pl.ds(column, 128)],
            send_sem=r.asend.at[to], recv_sem=r.arecv.at[land],
            device_id={"head": to}, device_id_type=MESH,
        )

    mine = pl.multiple_of(h * 128, 128)
    for blk in (1, 2, 0, 3):
        if blk == 0:
            weights.far()
            for copy in halos:
                copy.wait_recv()
        low = jnp.where(g == 0, 256, 0) if blk == 0 else 0
        high = jnp.where(g == groups - 1, 512, 768) if blk == 3 else 768
        attend(r.q, r.kvx, r.att, blk, low, high)
        for to in (2 * blk, 2 * blk + 1):

            @pl.when(to != h)
            def _():
                give(to * 128, mine, to, h).start()

    r.afull[:, pl.ds(mine, 128)] = r.att[pl.ds(mine, 128), :]
    r.query[...] = tn(r.grid_v[...], r.wq_v[...]).astype(BF)
    r.bg[...] = tn(r.dfc_v[...], r.wf_v[...])
    three = jnp.concatenate([r.dsrc_v[...], jnp.zeros((5, 256), jnp.int32)], axis=0)
    edges = three.astype(F32).T.astype(jnp.int32)
    for copy in (
        weights.side, weights.side_dn_a, weights.side_dn_b, weights.side_up_a, weights.side_up_b,
        weights.side_op_a, weights.side_op_b,
    ):
        copy.wait_recv()
    for other in range(8):

        @pl.when(other != h)
        def _():
            give(0, other * 128, other, other).wait()

    unit, inverse = norm_rows(r.hid[...] + nn(r.afull[...], r.wfull[...]))
    r.zbuf[z] = (unit * r.dgain_v[...]).astype(BF)
    sent = list(tables) + halos
    ring = {}

    def pass_on(way, d, chunk):
        block = (z + d) % NZ if way else (z + NZ - d) % NZ
        view = r.zbuf.at[block, :, pl.ds(512 * chunk, 512)]
        sem = way * 8 + d * 2 + chunk
        ring[way, d, chunk] = remote(view, view, r.zsend.at[sem], r.zrecv.at[sem], x, nexts[way])
        sent.append(ring[way, d, chunk])

    hops = ((0, 0), (1, 1), (0, 1), (1, 0))
    for way, chunk in hops:
        pass_on(way, 0, chunk)
    r.unit[...] = unit
    r.inv[...] = jnp.broadcast_to(inverse, (128, 128))

    def where(index):
        if index == 0:
            return z
        return (z + (NZ - (index + 1) // 2 if index % 2 else index // 2)) % NZ

    def chosen(zz):
        node = lax.broadcasted_iota(jnp.int32, (128, 128), 0)
        return (node == r.tab[zz][0:1, :]).astype(F32).astype(BF)

    crossing = {}
    land = pl.ds(pl.multiple_of(x * 32, 32), 32)

    def select(index, half):
        zz = where(index)
        cols = pl.ds(512 * half, 512)
        r.xs[index, :, HALF[half]] = tn(chosen(zz), r.zbuf[zz, :, HALF[half]]).astype(BF)
        for k in range(1, NX):
            xx = (x + k) % NX
            sem = index * 8 + half * NX + k
            crossing[index, half, k] = remote(
                r.xs.at[index, pl.ds(pl.multiple_of(xx * 32, 32), 32), cols], r.arrived.at[index, land, cols],
                r.xsend.at[sem], r.xrecv.at[sem], xx, z,
            )
        r.arrived[index, land, HALF[half]] = r.xs[index, land, HALF[half]]

    def absorb(first, count):
        for index in range(first, first + count):
            for half in range(2):
                for k in range(1, NX):
                    crossing[index, half, k].wait_recv()
        lane = lax.broadcasted_iota(jnp.int32, (1, 128), 1)
        slots = jnp.concatenate(
            [(lane // 32 * NZ + where(first + j)) * 32 + lane % 32 for j in range(count)], axis=1
        )
        picks = jnp.concatenate(
            [(edges[:, e : e + 1] == slots).astype(F32).astype(BF) for e in range(3)], axis=0
        )

        def tile(j, _):
            cols = pl.ds(pl.multiple_of(j * 256, 256), 256)
            block = r.arrived[first : first + count, :, cols].reshape(count * 128, 256)
            value = nn(picks, block).astype(BF)
            r.xe[:, cols] = value if first == 0 else r.xe[:, cols] + value
            return 0

        lax.fori_loop(0, 4, tile, 0)

    for copy in tables:
        copy.wait_recv()
    loads[16].wait()
    select(0, 0)
    select(0, 1)
    for d in range(1, 5):
        for phase in range(2):
            if d == 4 and phase == 1:
                continue
            for way in range(2):
                chunk = way ^ phase
                ring[way, d - 1, chunk].wait_recv()
                if d < 3 or (d == 3 and phase == 0):
                    pass_on(way, d, chunk)
            for way in range(2):
                select(7 if d == 4 else 2 * d - 1 + way, way ^ phase)
            if d == 2 and phase == 1:
                absorb(0, 3)
        if d == 3:
            absorb(3, 2)
    absorb(5, 3)

    def unpack(j, _):
        cols = pl.ds(pl.multiple_of(j * 256, 256), 256)
        r.kv[:, cols] = nn(r.xe[...], r.u_v[:, cols]).astype(BF)
        return 0

    lax.fori_loop(0, 8, unpack, 0)
    middle(r.kv, r.query, r.bg, r.mix)

    def unproject(j, _):
        cols = pl.ds(pl.multiple_of(j * 256, 256), 256)
        r.rg[:, cols] = nt(r.kv[...], r.u_v[cols, :]).astype(BF)
        return 0

    returning = {}

    def scatter(half, *indices):
        for index in indices:
            zz = where(index)
            row = lax.broadcasted_iota(jnp.int32, (128, 256), 0)
            slot = (row // 32 * NZ + zz) * 32 + row % 32
            pick = jnp.concatenate(
                [(r.dsrc_v[e : e + 1, :] == slot).astype(F32).astype(BF) for e in range(3)], axis=1
            )
            r.bs[index, :, HALF[half]] = nn(pick, r.rg[:, HALF[half]]).astype(BF)
            cols = pl.ds(512 * half, 512)
            for k in range(1, NX):
                xx = (x + k) % NX
                sem = index * 8 + half * NX + k
                returning[index, half, k] = remote(
                    r.bs.at[index, pl.ds(pl.multiple_of(xx * 32, 32), 32), cols],
                    r.rback.at[index, land, cols], r.bsend.at[sem], r.brecv.at[sem], xx, z,
                )
            r.rback[index, land, HALF[half]] = r.bs[index, land, HALF[half]]

    def partial(index, half):
        for k in range(1, NX):
            returning[index, half, k].wait_recv()
        return nn(chosen(where(index)), r.rback[index, :, HALF[half]])

    flow = {}

    def push(way, i, chunk, value):
        r.outs[way, i, :, HALF[chunk]] = value.astype(BF)
        cols = pl.ds(512 * chunk, 512)
        sem = way * 8 + i * 2 + chunk
        flow[way, i, chunk] = remote(
            r.outs.at[way, i, :, cols], r.ins.at[way, i, :, cols], r.qsend.at[sem], r.qrecv.at[sem],
            x, nexts[way],
        )

    def step(d, phase):
        for way in range(2):
            chunk = way ^ phase
            value = partial(2 * d - way, chunk)
            if d < 3 or phase == 0:
                flow[way, d, chunk].wait_recv()
                value = value + r.ins[way, d, :, HALF[chunk]].astype(F32)
            push(way, d - 1, chunk, value)

    lax.fori_loop(0, 2, unproject, 0)
    scatter(0, 7)
    lax.fori_loop(2, 4, unproject, 0)
    scatter(1, 7)
    scatter(1, 6)
    scatter(0, 5)
    push(0, 3, 0, partial(7, 0))
    push(1, 3, 1, partial(7, 1))
    scatter(0, 6)
    scatter(1, 5)
    scatter(1, 4)
    step(3, 1)
    scatter(0, 3)
    scatter(0, 4)
    scatter(1, 3)
    r.est_o[...] = r.grid_v[0:100, :].astype(F32) + nt(r.wf_v[...], r.mix[...])
    step(3, 0)
    scatter(1, 2)
    scatter(0, 1)
    scatter(0, 2)
    scatter(1, 1)
    step(2, 1)
    scatter(0, 0)
    scatter(1, 0)
    step(2, 0)
    step(1, 1)
    step(1, 0)
    part = jnp.concatenate([partial(0, 0), partial(0, 1)], axis=1)
    for way in range(2):
        for chunk in range(2):
            flow[way, 0, chunk].wait_recv()
    grad = part + r.ins[0, 0].astype(F32) + r.ins[1, 0].astype(F32)
    unit = r.unit[...]
    scaled = grad * r.dgain_v[...]
    first = jnp.mean(scaled, axis=-1, keepdims=True)
    second = jnp.mean(scaled * unit, axis=-1, keepdims=True)
    r.vert_o[...] = r.inv[:, 0:1] * (scaled - first - unit * second)
    rows.finish()
    weights.finish()
    for copy in sent + list(crossing.values()) + list(returning.values()) + list(flow.values()):
        copy.wait_send()


VM = pl.BlockSpec(memory_space=pltpu.VMEM)
OUT = (jax.ShapeDtypeStruct((100, 256), F32), jax.ShapeDtypeStruct((128, 1024), F32))


def hand_over(a_ref, b_ref, c_ref, d_ref):
    c_ref[...] = a_ref[...]
    d_ref[...] = b_ref[...]


def body(
    grid_in, mesh_embed, enc_src, enc_len, enc_kv_weight, proc_gain, qkv_weight, out_weight,
    dec_gain, unpack, wq, wf, dec_send, dec_src, dforecast,
):
    est, vert = pl.pallas_call(
        kernel,
        out_shape=OUT,
        in_specs=[pl.BlockSpec(memory_space=pl.ANY)] * 15,
        out_specs=(VM, VM),
        scratch_shapes=[pltpu.VMEM(*s) for s in SCRATCH.values()] + [DMA((n,)) for n in SEMS.values()],
        compiler_params=pltpu.CompilerParams(
            vmem_limit_bytes=60 * 2**20, collective_id=0, has_side_effects=True
        ),
    )(
        grid_in, mesh_embed, enc_src, enc_len.reshape(1, -1), enc_kv_weight, proc_gain.reshape(1, -1),
        qkv_weight.transpose(1, 0, 2), out_weight, dec_gain.reshape(1, -1), unpack, wq, wf, dec_send,
        dec_src, dforecast,
    )
    return pl.pallas_call(
        hand_over, out_shape=OUT, in_specs=[VM, VM], out_specs=(VM, VM)
    )(est, vert)


def solution(mesh):
    return jax.shard_map(
        body,
        mesh=mesh,
        in_specs=(
            P(None, ("grp", "head")), P(("grp", "head"), None), P(None, ("grp", "head")),
            P(("grp", "head")), P(), P(), P(None, None, "head"), P("head", None), P(), P(), P(), P(),
            P(("grp", "head"), None), P(None, ("grp", "head")), P(None, ("grp", "head")),
        ),
        out_specs=(P(None, ("grp", "head")), P(("grp", "head"), None)),
        check_vma=False,
    )
```

```python
import jax
import jax.numpy as jnp
from jax import lax
from jax.experimental import pallas as pl
from jax.experimental.pallas import tpu as pltpu
from jax.sharding import PartitionSpec as P

F32 = jnp.float32
BF = jnp.bfloat16
EPS = 1e-05
SCALE = 0.125


def nn(a, b):
    return lax.dot_general(a, b, (((1,), (0,)), ((), ())), preferred_element_type=F32)


def nt(a, b):
    return lax.dot_general(a, b, (((1,), (1,)), ((), ())), preferred_element_type=F32)


def tn(a, b):
    return lax.dot_general(a, b, (((0,), (0,)), ((), ())), preferred_element_type=F32)


def half_masks():
    lane = lax.broadcasted_iota(jnp.int32, (1, 128), 1)
    return [(lane < 64).astype(F32).astype(BF), (lane >= 64).astype(F32).astype(BF)]


def norm_rows(rows):
    row_mean = jnp.mean(rows, axis=-1, keepdims=True)
    centred = rows - row_mean
    spread = jnp.mean(centred * centred, axis=-1, keepdims=True)
    inverse = lax.rsqrt(spread + EPS)
    return centred * inverse, inverse


def encode(grid_ref, emb_ref, src_ref, len_ref, wkv_ref, hid_ref):
    points = grid_ref.shape[1]
    nodes = emb_ref.shape[0]
    pid = lax.broadcasted_iota(jnp.int32, (points, nodes), 0)
    count = jnp.zeros((points, nodes), F32)
    lens = len_ref[...]
    for e in range(src_ref.shape[0]):
        row = jnp.where(e < lens, src_ref[e : e + 1, :], -1)
        count += (pid == row).astype(F32)
    dead = jnp.where(count > 0, 0.0, -jnp.inf)
    grid_t = grid_ref[...].T
    masks = half_masks()

    def pair(j, _):
        cols = pl.ds(j * 128, 128)
        vcols = pl.ds(j * 128 + 1024, 128)
        keys = nn(grid_t, wkv_ref[:, cols]).astype(BF)
        values = nn(grid_t, wkv_ref[:, vcols]).astype(BF)
        emb = emb_ref[:, cols]
        weights = []
        for n in range(2):
            score = nt(keys, emb * masks[n]) * SCALE + dead
            top = jnp.max(score, axis=0, keepdims=True)
            term = jnp.exp(score - top) * count
            weights.append((term / jnp.sum(term, axis=0, keepdims=True)).astype(BF))
        mixed = tn(weights[0], values * masks[0]) + tn(weights[1], values * masks[1])
        hid_ref[:, cols] = emb.astype(F32) + mixed
        return 0

    for j in range(emb_ref.shape[1] // 128):
        pair(j, 0)


def attend(q_ref, kv_ref, out_ref, blk, low, high):
    masks = half_masks()
    rows = pl.ds(blk * 256, 256)
    span = pl.ds(blk * 256, 768)
    q = q_ref[rows, :]
    k = kv_ref[span, 0:128]
    v = kv_ref[span, 128:256]
    gap = lax.broadcasted_iota(jnp.int32, (256, 768), 1) - lax.broadcasted_iota(
        jnp.int32, (256, 768), 0
    )
    col = lax.broadcasted_iota(jnp.int32, (256, 768), 1)
    live = (gap >= 0) & (gap <= 512) & (col >= low) & (col < high)
    total = None
    for n in range(2):
        score = jnp.where(live, nt(q * masks[n], k), -jnp.inf)
        top = jnp.max(score, axis=1, keepdims=True)
        term = jnp.exp(score - top)
        part = nn(term.astype(BF), v * masks[n]) / jnp.sum(term, axis=1, keepdims=True)
        total = part if total is None else total + part
    out_ref[rows, :] = total.astype(BF)


MESH = pl.DeviceIdType.MESH


class Ring:
    def __init__(self, full, send, recv):
        h = lax.axis_index("head")
        y, c = h // 2, h % 2
        self.full, self.send, self.recv, self.used = full, send, recv, []
        self.own = h
        self.up = ((y + 1) % 4) * 2 + c
        self.dn = ((y + 3) % 4) * 2 + c
        self.op = ((y + 2) % 4) * 2 + c
        self.flip = 1 - 2 * c
        self.sib = h + self.flip

    def copy(self, block, start, size, to, sem, land):
        view = self.full.at[pl.ds(block * 128 + start, size), :]
        copy = pltpu.make_async_remote_copy(
            src_ref=view, dst_ref=view, send_sem=self.send.at[sem], recv_sem=self.recv.at[land],
            device_id={"head": to}, device_id_type=MESH,
        )
        copy.start()
        self.used.append(copy)
        return copy

    def begin(self):
        own = self.own
        self.dn_a = self.copy(own, 0, 64, self.up, 0, 0)
        self.up_b = self.copy(own, 64, 64, self.dn, 1, 3)
        self.side = self.copy(own, 0, 128, self.sib, 4, 6)
        self.dn_b = self.copy(own, 64, 64, self.up, 2, 1)
        self.up_a = self.copy(own, 0, 64, self.dn, 3, 2)

    def forward(self):
        self.dn_a.wait_recv()
        self.op_a = self.copy(self.dn, 0, 64, self.up, 5, 4)
        self.side_dn_a = self.copy(self.dn, 0, 64, self.sib, 6, 7)
        self.up_b.wait_recv()
        self.op_b = self.copy(self.up, 64, 64, self.dn, 7, 5)
        self.side_up_b = self.copy(self.up, 64, 64, self.sib, 8, 8)

    def near(self):
        self.dn_b.wait_recv()
        self.side_dn_b = self.copy(self.dn, 64, 64, self.sib, 9, 9)
        self.up_a.wait_recv()
        self.side_up_a = self.copy(self.up, 0, 64, self.sib, 10, 10)

    def far(self):
        self.op_a.wait_recv()
        self.side_op_a = self.copy(self.op, 0, 64, self.sib, 11, 11)
        self.op_b.wait_recv()
        self.side_op_b = self.copy(self.op, 64, 64, self.sib, 12, 12)

    def finish(self):
        for copy in self.used:
            copy.wait_send()


def head_sum():
    row = lax.broadcasted_iota(jnp.int32, (1024, 128), 0) // 64
    col = lax.broadcasted_iota(jnp.int32, (1024, 128), 1)
    return (row == col).astype(F32).astype(BF)


def head_spread():
    row = lax.broadcasted_iota(jnp.int32, (128, 1024), 0)
    col = lax.broadcasted_iota(jnp.int32, (128, 1024), 1) // 64
    return (row == col).astype(F32).astype(BF)


NX, NZ = 4, 8
HALF = (slice(0, 512), slice(512, 1024))


def middle(kv, query, bg, mix):
    hsum = head_sum()
    spread = head_spread()

    def part(i, _):
        at = pl.multiple_of(i * 128, 128)
        rows = [pl.ds(at + e * 256, 128) for e in range(3)]
        qf = query[pl.ds(at, 128), :].astype(F32)
        back = bg[pl.ds(at, 128), :]
        products = [(qf * kv[r, :1024].astype(F32)).astype(BF) for r in rows]
        products += [(back * kv[r, 1024:].astype(F32)).astype(BF) for r in rows]
        sums = nn(jnp.concatenate(products, axis=0), hsum)
        score = [sums[e * 128 : e * 128 + 128] * SCALE for e in range(3)]
        along = [sums[e * 128 + 384 : e * 128 + 512] for e in range(3)]
        top = jnp.maximum(jnp.maximum(score[0], score[1]), score[2])
        term = [jnp.exp(s - top) for s in score]
        total = term[0] + term[1] + term[2]
        weight = [t / total for t in term]
        mean = weight[0] * along[0] + weight[1] * along[1] + weight[2] * along[2]
        heads = [w.astype(BF) for w in weight]
        heads += [(w * (s - mean) * SCALE).astype(BF) for w, s in zip(weight, along)]
        mixed = jnp.zeros((128, 1024), F32)
        for e in range(3):
            wide = nn(heads[e], spread)
            mixed += wide * kv[rows[e], 1024:].astype(F32)
            grad = nn(heads[3 + e], spread)
            kv[rows[e], :1024] = (grad * qf).astype(BF)
            kv[rows[e], 1024:] = (wide * back).astype(BF)
        mix[pl.ds(at, 128), :] = mixed.astype(BF)
        return 0

    lax.fori_loop(0, 2, part, 0)


DMA = pltpu.SemaphoreType.DMA
SCRATCH = {
    "grid_v": ((112, 256), BF), "emb_v": ((128, 1024), BF), "src_v": ((16, 128), jnp.int32),
    "len_v": ((1, 128), jnp.int32), "wkv_v": ((112, 2048), BF), "pgain_v": ((1, 1024), F32),
    "wqkv_v": ((1024, 384), BF), "dgain_v": ((1, 1024), F32), "hid": ((128, 1024), F32),
    "full": ((1024, 1024), BF), "wfull": ((1024, 1024), BF), "q": ((1024, 128), BF),
    "kvx": ((1536, 256), BF), "att": ((1024, 128), BF), "afull": ((128, 1024), BF),
    "unit": ((128, 1024), F32), "inv": ((128, 128), F32), "send_v": ((32, 32), jnp.int32),
    "mine": ((NZ, 8, 128), jnp.int32), "dfc_v": ((100, 256), BF), "dsrc_v": ((3, 256), jnp.int32),
    "wq_v": ((112, 1024), BF), "wf_v": ((100, 1024), BF), "u_v": ((1024, 2048), BF),
    "zbuf": ((NZ, 128, 1024), BF), "tab": ((NZ, 8, 128), jnp.int32), "xs": ((8, 128, 1024), BF),
    "arrived": ((8, 128, 1024), BF), "xe": ((768, 1024), BF), "kv": ((768, 2048), BF), "query": ((256, 1024), BF),
    "bg": ((256, 1024), F32), "mix": ((256, 1024), BF), "rg": ((768, 1024), BF),
    "bs": ((8, 128, 1024), BF), "rback": ((8, 128, 1024), BF), "outs": ((2, 4, 128, 1024), BF),
    "ins": ((2, 4, 128, 1024), BF),
}
SEMS = {
    "load": 18, "nsend": 13, "nrecv": 13, "wsend": 13, "wrecv": 13, "hsend": 4, "hrecv": 4, "asend": 8,
    "arecv": 8, "tsend": 8, "trecv": 8, "zsend": 16, "zrecv": 16, "xsend": 64, "xrecv": 64, "bsend": 64,
    "brecv": 64, "qsend": 16, "qrecv": 16,
}
INPUTS = (
    "grid_h", "emb_h", "src_h", "len_h", "wkv_h", "pgain_h", "wqkv_h", "wout_h", "dgain_h", "u_h", "wq_h",
    "wf_h", "send_h", "dsrc_h", "dfc_h",
)


class Refs:
    def __init__(self, refs):
        for name, ref in zip(INPUTS + ("est_o", "vert_o") + tuple(SCRATCH) + tuple(SEMS), refs):
            setattr(self, name, ref)


def start_loads(r, h):
    own = pl.ds(pl.multiple_of(h * 128, 128), 128)
    pairs = [
        (r.wout_h, r.wfull.at[own, :]), (r.send_h, r.send_v), (r.grid_h, r.grid_v), (r.emb_h, r.emb_v),
        (r.src_h, r.src_v), (r.len_h, r.len_v), (r.wkv_h, r.wkv_v), (r.pgain_h, r.pgain_v),
        (r.wqkv_h.at[0], r.wqkv_v.at[:, 0:128]), (r.wqkv_h.at[1], r.wqkv_v.at[:, 128:256]),
        (r.wqkv_h.at[2], r.wqkv_v.at[:, 256:384]), (r.dgain_h, r.dgain_v), (r.dfc_h, r.dfc_v),
        (r.dsrc_h, r.dsrc_v), (r.wq_h, r.wq_v), (r.wf_h, r.wf_v), (r.u_h, r.u_v),
    ]
    loads = [pltpu.make_async_copy(s, d, r.load.at[i]) for i, (s, d) in enumerate(pairs)]
    for copy in loads:
        copy.start()
    return loads


def kernel(*refs):
    r = Refs(refs)
    g = lax.axis_index("grp")
    h = lax.axis_index("head")
    groups = lax.axis_size("grp")
    right, left = (g + 1) % groups, (g + groups - 1) % groups
    x, z = g // NZ, g % NZ
    nexts = [(z + 1) % NZ, (z + NZ - 1) % NZ]
    loads = start_loads(r, h)
    barrier = pltpu.get_barrier_semaphore()
    for i in range(1, 8):
        pl.semaphore_signal(barrier, inc=1, device_id={"head": (h + i) % 8}, device_id_type=MESH)
    for k in range(1, NZ):
        pl.semaphore_signal(barrier, inc=1, device_id={"grp": x * NZ + (z + k) % NZ}, device_id_type=MESH)
    for k in range(1, NX):
        pl.semaphore_signal(barrier, inc=1, device_id={"grp": (x + k) % NX * NZ + z}, device_id_type=MESH)
    for other in (right, left):
        pl.semaphore_signal(barrier, inc=1, device_id={"grp": other}, device_id_type=MESH)
    loads[1].wait()
    table = jnp.concatenate([r.send_v[8 * k : 8 * k + 8, :] for k in range(NX)], axis=1)
    for k in range(NZ):
        r.mine[k] = jnp.broadcast_to(table[k : k + 1, :], (8, 128))

    def remote(source, target, send, recv, xx, zz):
        copy = pltpu.make_async_remote_copy(
            src_ref=source, dst_ref=target, send_sem=send, recv_sem=recv,
            device_id={"grp": xx * NZ + zz}, device_id_type=MESH,
        )
        copy.start()
        return copy

    for copy in loads[2:8]:
        copy.wait()
    encode(r.grid_v, r.emb_v, r.src_v, r.len_v, r.wkv_v, r.hid)
    unit, _ = norm_rows(r.hid[...])
    r.full[pl.ds(pl.multiple_of(h * 128, 128), 128), :] = (unit * r.pgain_v[...]).astype(BF)
    pl.semaphore_wait(barrier, 7 + NZ + NX - 2 + 2)
    rows = Ring(r.full, r.nsend, r.nrecv)
    rows.begin()
    r.tab[pl.ds(z, 1)] = r.mine[pl.ds(z, 1)]
    tables = [
        remote(r.mine.at[(z + k) % NZ], r.tab.at[z], r.tsend.at[k], r.trecv.at[k], x, (z + k) % NZ)
        for k in range(1, NZ)
    ]
    loads[0].wait()
    weights = Ring(r.wfull, r.wsend, r.wrecv)
    for copy in loads[8:16]:
        copy.wait()

    def halo(start, land, sem, to):
        return pltpu.make_async_remote_copy(
            src_ref=r.kvx.at[pl.ds(start, 128), :], dst_ref=r.kvx.at[pl.ds(land, 128), :],
            send_sem=r.hsend.at[sem], recv_sem=r.hrecv.at[sem],
            device_id={"grp": to}, device_id_type=MESH,
        )

    def project(block):
        at = pl.multiple_of(block * 128, 128)
        triple = nn(r.full[pl.ds(at, 128), :], r.wqkv_v[...]).astype(BF)
        r.q[pl.ds(at, 128), :] = (triple[:, :128].astype(F32) * SCALE).astype(BF)
        r.kvx[pl.ds(at + 256, 128), :] = triple[:, 128:]

        @pl.when(block >= 6)
        def _():
            halo(at + 256, at - 768, block - 6, right).start()

        @pl.when(block < 2)
        def _():
            halo(at + 256, at + 1280, block + 2, left).start()

    flip = rows.flip
    project(h)
    rows.side.wait_recv()
    rows.forward()
    project(rows.sib)
    rows.near()
    weights.begin()
    project(rows.dn)
    project(rows.up)
    rows.side_dn_a.wait_recv()
    rows.side_dn_b.wait_recv()
    project(rows.dn + flip)
    rows.side_up_a.wait_recv()
    rows.side_up_b.wait_recv()
    project(rows.up + flip)
    rows.far()
    project(rows.op)
    rows.side_op_a.wait_recv()
    rows.side_op_b.wait_recv()
    project(rows.op + flip)

    halos = [
        halo(1024, 0, 0, right), halo(1152, 128, 1, right), halo(256, 1280, 2, left), halo(384, 1408, 3, left),
    ]
    weights.forward()

    def give(start, column, to, land):
        return pltpu.make_async_remote_copy(
            src_ref=r.att.at[pl.ds(start, 128), :], dst_ref=r.afull.at[:, pl.ds(column, 128)],
            send_sem=r.asend.at[to], recv_sem=r.arecv.at[land],
            device_id={"head": to}, device_id_type=MESH,
        )

    mine = pl.multiple_of(h * 128, 128)
    for blk in (1, 2, 0, 3):
        if blk == 0:
            weights.near()
            for copy in halos:
                copy.wait_recv()
        low = jnp.where(g == 0, 256, 0) if blk == 0 else 0
        high = jnp.where(g == groups - 1, 512, 768) if blk == 3 else 768
        attend(r.q, r.kvx, r.att, blk, low, high)
        for to in (2 * blk, 2 * blk + 1):

            @pl.when(to != h)
            def _():
                give(to * 128, mine, to, h).start()

    weights.far()
    r.afull[:, pl.ds(mine, 128)] = r.att[pl.ds(mine, 128), :]
    r.query[...] = tn(r.grid_v[...], r.wq_v[...]).astype(BF)
    r.bg[...] = tn(r.dfc_v[...], r.wf_v[...])
    three = jnp.concatenate([r.dsrc_v[...], jnp.zeros((5, 256), jnp.int32)], axis=0)
    edges = three.astype(F32).T.astype(jnp.int32)
    for copy in (
        weights.side, weights.side_dn_a, weights.side_dn_b, weights.side_up_a, weights.side_up_b,
        weights.side_op_a, weights.side_op_b,
    ):
        copy.wait_recv()
    for other in range(8):

        @pl.when(other != h)
        def _():
            give(0, other * 128, other, other).wait()

    unit, inverse = norm_rows(r.hid[...] + nn(r.afull[...], r.wfull[...]))
    r.zbuf[z] = (unit * r.dgain_v[...]).astype(BF)
    sent = list(tables) + halos
    ring = {}

    def pass_on(way, d, chunk):
        block = (z + d) % NZ if way else (z + NZ - d) % NZ
        view = r.zbuf.at[block, :, pl.ds(512 * chunk, 512)]
        sem = way * 8 + d * 2 + chunk
        ring[way, d, chunk] = remote(view, view, r.zsend.at[sem], r.zrecv.at[sem], x, nexts[way])
        sent.append(ring[way, d, chunk])

    hops = ((0, 0), (1, 1), (0, 1), (1, 0))
    for way, chunk in hops:
        pass_on(way, 0, chunk)
    r.unit[...] = unit
    r.inv[...] = jnp.broadcast_to(inverse, (128, 128))

    def where(index):
        if index == 0:
            return z
        return (z + (NZ - (index + 1) // 2 if index % 2 else index // 2)) % NZ

    def chosen(zz):
        node = lax.broadcasted_iota(jnp.int32, (128, 128), 0)
        return (node == r.tab[zz][0:1, :]).astype(F32).astype(BF)

    crossing = {}
    land = pl.ds(pl.multiple_of(x * 32, 32), 32)

    def select(index, half):
        zz = where(index)
        cols = pl.ds(512 * half, 512)
        r.xs[index, :, HALF[half]] = tn(chosen(zz), r.zbuf[zz, :, HALF[half]]).astype(BF)
        for k in range(1, NX):
            xx = (x + k) % NX
            sem = index * 8 + half * NX + k
            crossing[index, half, k] = remote(
                r.xs.at[index, pl.ds(pl.multiple_of(xx * 32, 32), 32), cols], r.arrived.at[index, land, cols],
                r.xsend.at[sem], r.xrecv.at[sem], xx, z,
            )
        r.arrived[index, land, HALF[half]] = r.xs[index, land, HALF[half]]

    def absorb(first, count):
        for index in range(first, first + count):
            for half in range(2):
                for k in range(1, NX):
                    crossing[index, half, k].wait_recv()
        lane = lax.broadcasted_iota(jnp.int32, (1, 128), 1)
        slots = jnp.concatenate(
            [(lane // 32 * NZ + where(first + j)) * 32 + lane % 32 for j in range(count)], axis=1
        )
        picks = jnp.concatenate(
            [(edges[:, e : e + 1] == slots).astype(F32).astype(BF) for e in range(3)], axis=0
        )

        def tile(j, _):
            cols = pl.ds(pl.multiple_of(j * 256, 256), 256)
            block = r.arrived[first : first + count, :, cols].reshape(count * 128, 256)
            value = nn(picks, block).astype(BF)
            r.xe[:, cols] = value if first == 0 else r.xe[:, cols] + value
            return 0

        lax.fori_loop(0, 4, tile, 0)

    for copy in tables:
        copy.wait_recv()
    loads[16].wait()
    select(0, 0)
    select(0, 1)
    for d in range(1, 5):
        for phase in range(2):
            if d == 4 and phase == 1:
                continue
            for way in range(2):
                chunk = way ^ phase
                ring[way, d - 1, chunk].wait_recv()
                if d < 3 or (d == 3 and phase == 0):
                    pass_on(way, d, chunk)
            for way in range(2):
                select(7 if d == 4 else 2 * d - 1 + way, way ^ phase)
            if d == 2 and phase == 1:
                absorb(0, 3)
        if d == 3:
            absorb(3, 2)
    absorb(5, 2)
    absorb(7, 1)

    def unpack(j, _):
        cols = pl.ds(pl.multiple_of(j * 1024, 1024), 1024)
        r.kv[:, cols] = nn(r.xe[...], r.u_v[:, cols]).astype(BF)
        return 0

    lax.fori_loop(0, 2, unpack, 0)
    middle(r.kv, r.query, r.bg, r.mix)

    def unproject(j, _):
        cols = pl.ds(pl.multiple_of(j * 512, 512), 512)
        r.rg[:, cols] = nt(r.kv[...], r.u_v[cols, :]).astype(BF)
        return 0

    returning = {}

    def scatter(half, *indices):
        for index in indices:
            zz = where(index)
            row = lax.broadcasted_iota(jnp.int32, (128, 256), 0)
            slot = (row // 32 * NZ + zz) * 32 + row % 32
            pick = jnp.concatenate(
                [(r.dsrc_v[e : e + 1, :] == slot).astype(F32).astype(BF) for e in range(3)], axis=1
            )
            r.bs[index, :, HALF[half]] = nn(pick, r.rg[:, HALF[half]]).astype(BF)
            cols = pl.ds(512 * half, 512)
            for k in range(1, NX):
                xx = (x + k) % NX
                sem = index * 8 + half * NX + k
                returning[index, half, k] = remote(
                    r.bs.at[index, pl.ds(pl.multiple_of(xx * 32, 32), 32), cols],
                    r.rback.at[index, land, cols], r.bsend.at[sem], r.brecv.at[sem], xx, z,
                )
            r.rback[index, land, HALF[half]] = r.bs[index, land, HALF[half]]

    def partial(index, half):
        for k in range(1, NX):
            returning[index, half, k].wait_recv()
        return nn(chosen(where(index)), r.rback[index, :, HALF[half]])

    flow = {}

    def push(way, i, chunk, value):
        r.outs[way, i, :, HALF[chunk]] = value.astype(BF)
        cols = pl.ds(512 * chunk, 512)
        sem = way * 8 + i * 2 + chunk
        flow[way, i, chunk] = remote(
            r.outs.at[way, i, :, cols], r.ins.at[way, i, :, cols], r.qsend.at[sem], r.qrecv.at[sem],
            x, nexts[way],
        )

    def step(d, phase):
        for way in range(2):
            chunk = way ^ phase
            value = partial(2 * d - way, chunk)
            if d < 3 or phase == 0:
                flow[way, d, chunk].wait_recv()
                value = value + r.ins[way, d, :, HALF[chunk]].astype(F32)
            push(way, d - 1, chunk, value)

    lax.fori_loop(0, 1, unproject, 0)
    scatter(0, 7)
    lax.fori_loop(1, 2, unproject, 0)
    scatter(1, 7)
    scatter(1, 6)
    scatter(0, 5)
    push(0, 3, 0, partial(7, 0))
    push(1, 3, 1, partial(7, 1))
    scatter(0, 6)
    scatter(1, 5)
    scatter(1, 4)
    step(3, 1)
    scatter(0, 3)
    scatter(0, 4)
    scatter(1, 3)
    r.est_o[...] = r.grid_v[0:100, :].astype(F32) + nt(r.wf_v[...], r.mix[...])
    step(3, 0)
    scatter(1, 2)
    scatter(0, 1)
    scatter(0, 2)
    scatter(1, 1)
    step(2, 1)
    scatter(0, 0)
    scatter(1, 0)
    step(2, 0)
    step(1, 1)
    step(1, 0)
    part = jnp.concatenate([partial(0, 0), partial(0, 1)], axis=1)
    for way in range(2):
        for chunk in range(2):
            flow[way, 0, chunk].wait_recv()
    grad = part + r.ins[0, 0].astype(F32) + r.ins[1, 0].astype(F32)
    unit = r.unit[...]
    scaled = grad * r.dgain_v[...]
    first = jnp.mean(scaled, axis=-1, keepdims=True)
    second = jnp.mean(scaled * unit, axis=-1, keepdims=True)
    r.vert_o[...] = r.inv[:, 0:1] * (scaled - first - unit * second)
    rows.finish()
    weights.finish()
    for copy in sent + list(crossing.values()) + list(returning.values()) + list(flow.values()):
        copy.wait_send()


VM = pl.BlockSpec(memory_space=pltpu.VMEM)
OUT = (jax.ShapeDtypeStruct((100, 256), F32), jax.ShapeDtypeStruct((128, 1024), F32))


def hand_over(a_ref, b_ref, c_ref, d_ref):
    c_ref[...] = a_ref[...]
    d_ref[...] = b_ref[...]


def body(
    grid_in, mesh_embed, enc_src, enc_len, enc_kv_weight, proc_gain, qkv_weight, out_weight,
    dec_gain, unpack, wq, wf, dec_send, dec_src, dforecast,
):
    est, vert = pl.pallas_call(
        kernel,
        out_shape=OUT,
        in_specs=[pl.BlockSpec(memory_space=pl.ANY)] * 15,
        out_specs=(VM, VM),
        scratch_shapes=[pltpu.VMEM(*s) for s in SCRATCH.values()] + [DMA((n,)) for n in SEMS.values()],
        compiler_params=pltpu.CompilerParams(
            vmem_limit_bytes=60 * 2**20, collective_id=0, has_side_effects=True
        ),
    )(
        grid_in, mesh_embed, enc_src, enc_len.reshape(1, -1), enc_kv_weight, proc_gain.reshape(1, -1),
        qkv_weight.transpose(1, 0, 2), out_weight, dec_gain.reshape(1, -1), unpack, wq, wf, dec_send,
        dec_src, dforecast,
    )
    return pl.pallas_call(
        hand_over, out_shape=OUT, in_specs=[VM, VM], out_specs=(VM, VM)
    )(est, vert)


def solution(mesh):
    return jax.shard_map(
        body,
        mesh=mesh,
        in_specs=(
            P(None, ("grp", "head")), P(("grp", "head"), None), P(None, ("grp", "head")),
            P(("grp", "head")), P(), P(), P(None, None, "head"), P("head", None), P(), P(), P(), P(),
            P(("grp", "head"), None), P(None, ("grp", "head")), P(None, ("grp", "head")),
        ),
        out_specs=(P(None, ("grp", "head")), P(("grp", "head"), None)),
        check_vma=False,
    )
```

```python
import jax
import jax.numpy as jnp
from jax import lax
from jax.experimental import pallas as pl
from jax.experimental.pallas import tpu as pltpu
from jax.sharding import PartitionSpec as P

F32 = jnp.float32
BF = jnp.bfloat16
EPS = 1e-05
SCALE = 0.125


def nn(a, b):
    return lax.dot_general(a, b, (((1,), (0,)), ((), ())), preferred_element_type=F32)


def nt(a, b):
    return lax.dot_general(a, b, (((1,), (1,)), ((), ())), preferred_element_type=F32)


def tn(a, b):
    return lax.dot_general(a, b, (((0,), (0,)), ((), ())), preferred_element_type=F32)


def half_masks():
    lane = lax.broadcasted_iota(jnp.int32, (1, 128), 1)
    return [(lane < 64).astype(F32).astype(BF), (lane >= 64).astype(F32).astype(BF)]


def norm_rows(rows):
    row_mean = jnp.mean(rows, axis=-1, keepdims=True)
    centred = rows - row_mean
    spread = jnp.mean(centred * centred, axis=-1, keepdims=True)
    inverse = lax.rsqrt(spread + EPS)
    return centred * inverse, inverse


def encode(grid_ref, emb_ref, src_ref, len_ref, wkv_ref, hid_ref):
    points = grid_ref.shape[1]
    nodes = emb_ref.shape[0]
    pid = lax.broadcasted_iota(jnp.int32, (points, nodes), 0)
    count = jnp.zeros((points, nodes), F32)
    lens = len_ref[...]
    for e in range(src_ref.shape[0]):
        row = jnp.where(e < lens, src_ref[e : e + 1, :], -1)
        count += (pid == row).astype(F32)
    dead = jnp.where(count > 0, 0.0, -jnp.inf)
    grid_t = grid_ref[...].T
    masks = half_masks()

    def pair(j, _):
        cols = pl.ds(j * 128, 128)
        vcols = pl.ds(j * 128 + 1024, 128)
        keys = nn(grid_t, wkv_ref[:, cols]).astype(BF)
        values = nn(grid_t, wkv_ref[:, vcols]).astype(BF)
        emb = emb_ref[:, cols]
        weights = []
        for n in range(2):
            score = nt(keys, emb * masks[n]) * SCALE + dead
            top = jnp.max(score, axis=0, keepdims=True)
            term = jnp.exp(score - top) * count
            weights.append((term / jnp.sum(term, axis=0, keepdims=True)).astype(BF))
        mixed = tn(weights[0], values * masks[0]) + tn(weights[1], values * masks[1])
        hid_ref[:, cols] = emb.astype(F32) + mixed
        return 0

    for j in range(emb_ref.shape[1] // 128):
        pair(j, 0)


def attend(q_ref, kv_ref, out_ref, blk, low, high):
    masks = half_masks()
    rows = pl.ds(blk * 256, 256)
    span = pl.ds(blk * 256, 768)
    q = q_ref[rows, :]
    k = kv_ref[span, 0:128]
    v = kv_ref[span, 128:256]
    gap = lax.broadcasted_iota(jnp.int32, (256, 768), 1) - lax.broadcasted_iota(
        jnp.int32, (256, 768), 0
    )
    col = lax.broadcasted_iota(jnp.int32, (256, 768), 1)
    live = (gap >= 0) & (gap <= 512) & (col >= low) & (col < high)
    total = None
    for n in range(2):
        score = jnp.where(live, nt(q * masks[n], k), -jnp.inf)
        top = jnp.max(score, axis=1, keepdims=True)
        term = jnp.exp(score - top)
        part = nn(term.astype(BF), v * masks[n]) / jnp.sum(term, axis=1, keepdims=True)
        total = part if total is None else total + part
    out_ref[rows, :] = total.astype(BF)


MESH = pl.DeviceIdType.MESH


class Ring:
    def __init__(self, full, send, recv):
        h = lax.axis_index("head")
        y, c = h // 2, h % 2
        self.full, self.send, self.recv, self.used = full, send, recv, []
        self.own = h
        self.up = ((y + 1) % 4) * 2 + c
        self.dn = ((y + 3) % 4) * 2 + c
        self.op = ((y + 2) % 4) * 2 + c
        self.flip = 1 - 2 * c
        self.sib = h + self.flip

    def copy(self, block, start, size, to, sem, land):
        view = self.full.at[pl.ds(block * 128 + start, size), :]
        copy = pltpu.make_async_remote_copy(
            src_ref=view, dst_ref=view, send_sem=self.send.at[sem], recv_sem=self.recv.at[land],
            device_id={"head": to}, device_id_type=MESH,
        )
        copy.start()
        self.used.append(copy)
        return copy

    def begin(self):
        own = self.own
        self.dn_a = self.copy(own, 0, 64, self.up, 0, 0)
        self.up_b = self.copy(own, 64, 64, self.dn, 1, 3)
        self.side = self.copy(own, 0, 128, self.sib, 4, 6)
        self.dn_b = self.copy(own, 64, 64, self.up, 2, 1)
        self.up_a = self.copy(own, 0, 64, self.dn, 3, 2)

    def forward(self):
        self.dn_a.wait_recv()
        self.op_a = self.copy(self.dn, 0, 64, self.up, 5, 4)
        self.side_dn_a = self.copy(self.dn, 0, 64, self.sib, 6, 7)
        self.up_b.wait_recv()
        self.op_b = self.copy(self.up, 64, 64, self.dn, 7, 5)
        self.side_up_b = self.copy(self.up, 64, 64, self.sib, 8, 8)

    def near(self):
        self.dn_b.wait_recv()
        self.side_dn_b = self.copy(self.dn, 64, 64, self.sib, 9, 9)
        self.up_a.wait_recv()
        self.side_up_a = self.copy(self.up, 0, 64, self.sib, 10, 10)

    def far(self):
        self.op_a.wait_recv()
        self.side_op_a = self.copy(self.op, 0, 64, self.sib, 11, 11)
        self.op_b.wait_recv()
        self.side_op_b = self.copy(self.op, 64, 64, self.sib, 12, 12)

    def finish(self):
        for copy in self.used:
            copy.wait_send()


def head_sum():
    row = lax.broadcasted_iota(jnp.int32, (1024, 128), 0) // 64
    col = lax.broadcasted_iota(jnp.int32, (1024, 128), 1)
    return (row == col).astype(F32).astype(BF)


def head_spread():
    row = lax.broadcasted_iota(jnp.int32, (128, 1024), 0)
    col = lax.broadcasted_iota(jnp.int32, (128, 1024), 1) // 64
    return (row == col).astype(F32).astype(BF)


NX, NZ = 4, 8
HALF = (slice(0, 512), slice(512, 1024))


def middle(kv, query, bg, mix):
    hsum = head_sum()
    spread = head_spread()

    def part(i, _):
        at = pl.multiple_of(i * 128, 128)
        rows = [pl.ds(at + e * 256, 128) for e in range(3)]
        qf = query[pl.ds(at, 128), :].astype(F32)
        back = bg[pl.ds(at, 128), :]
        products = [(qf * kv[r, :1024].astype(F32)).astype(BF) for r in rows]
        products += [(back * kv[r, 1024:].astype(F32)).astype(BF) for r in rows]
        sums = nn(jnp.concatenate(products, axis=0), hsum)
        score = [sums[e * 128 : e * 128 + 128] * SCALE for e in range(3)]
        along = [sums[e * 128 + 384 : e * 128 + 512] for e in range(3)]
        top = jnp.maximum(jnp.maximum(score[0], score[1]), score[2])
        term = [jnp.exp(s - top) for s in score]
        total = term[0] + term[1] + term[2]
        weight = [t / total for t in term]
        mean = weight[0] * along[0] + weight[1] * along[1] + weight[2] * along[2]
        heads = [w.astype(BF) for w in weight]
        heads += [(w * (s - mean) * SCALE).astype(BF) for w, s in zip(weight, along)]
        mixed = jnp.zeros((128, 1024), F32)
        for e in range(3):
            wide = nn(heads[e], spread)
            mixed += wide * kv[rows[e], 1024:].astype(F32)
            grad = nn(heads[3 + e], spread)
            kv[rows[e], :1024] = (grad * qf).astype(BF)
            kv[rows[e], 1024:] = (wide * back).astype(BF)
        mix[pl.ds(at, 128), :] = mixed.astype(BF)
        return 0

    lax.fori_loop(0, 2, part, 0)


DMA = pltpu.SemaphoreType.DMA
SCRATCH = {
    "grid_v": ((112, 256), BF), "emb_v": ((128, 1024), BF), "src_v": ((16, 128), jnp.int32),
    "len_v": ((1, 128), jnp.int32), "wkv_v": ((112, 2048), BF), "pgain_v": ((1, 1024), F32),
    "wqkv_v": ((1024, 384), BF), "dgain_v": ((1, 1024), F32), "hid": ((128, 1024), F32),
    "full": ((1024, 1024), BF), "wfull": ((1024, 1024), BF), "q": ((1024, 128), BF),
    "kvx": ((1536, 256), BF), "att": ((1024, 128), BF), "afull": ((128, 1024), BF),
    "unit": ((128, 1024), F32), "inv": ((128, 128), F32), "send_v": ((32, 32), jnp.int32),
    "mine": ((NZ, 8, 128), jnp.int32), "dfc_v": ((100, 256), BF), "dsrc_v": ((3, 256), jnp.int32),
    "wq_v": ((112, 1024), BF), "wf_v": ((100, 1024), BF), "u_v": ((1024, 2048), BF),
    "zbuf": ((NZ, 128, 1024), BF), "tab": ((NZ, 8, 128), jnp.int32), "xs": ((8, 128, 1024), BF),
    "arrived": ((8, 128, 1024), BF), "xe": ((768, 1024), BF), "kv": ((768, 2048), BF), "query": ((256, 1024), BF),
    "bg": ((256, 1024), F32), "mix": ((256, 1024), BF), "rg": ((768, 1024), BF),
    "bs": ((8, 128, 1024), BF), "rback": ((8, 128, 1024), BF), "outs": ((2, 4, 128, 1024), BF),
    "ins": ((2, 4, 128, 1024), BF),
}
SEMS = {
    "load": 18, "nsend": 13, "nrecv": 13, "wsend": 13, "wrecv": 13, "hsend": 4, "hrecv": 4, "asend": 8,
    "arecv": 8, "tsend": 8, "trecv": 8, "zsend": 16, "zrecv": 16, "xsend": 64, "xrecv": 64, "bsend": 64,
    "brecv": 64, "qsend": 32, "qrecv": 32,
}
INPUTS = (
    "grid_h", "emb_h", "src_h", "len_h", "wkv_h", "pgain_h", "wqkv_h", "wout_h", "dgain_h", "u_h", "wq_h",
    "wf_h", "send_h", "dsrc_h", "dfc_h",
)


class Refs:
    def __init__(self, refs):
        for name, ref in zip(INPUTS + ("est_o", "vert_o") + tuple(SCRATCH) + tuple(SEMS), refs):
            setattr(self, name, ref)


def start_loads(r, h):
    own = pl.ds(pl.multiple_of(h * 128, 128), 128)
    pairs = [
        (r.wout_h, r.wfull.at[own, :]), (r.send_h, r.send_v), (r.grid_h, r.grid_v), (r.emb_h, r.emb_v),
        (r.src_h, r.src_v), (r.len_h, r.len_v), (r.wkv_h, r.wkv_v), (r.pgain_h, r.pgain_v),
        (r.wqkv_h.at[0], r.wqkv_v.at[:, 0:128]), (r.wqkv_h.at[1], r.wqkv_v.at[:, 128:256]),
        (r.wqkv_h.at[2], r.wqkv_v.at[:, 256:384]), (r.dgain_h, r.dgain_v), (r.dfc_h, r.dfc_v),
        (r.dsrc_h, r.dsrc_v), (r.wq_h, r.wq_v), (r.wf_h, r.wf_v), (r.u_h, r.u_v),
    ]
    loads = [pltpu.make_async_copy(s, d, r.load.at[i]) for i, (s, d) in enumerate(pairs)]
    for copy in loads:
        copy.start()
    return loads


def kernel(*refs):
    r = Refs(refs)
    g = lax.axis_index("grp")
    h = lax.axis_index("head")
    groups = lax.axis_size("grp")
    right, left = (g + 1) % groups, (g + groups - 1) % groups
    x, z = g // NZ, g % NZ
    nexts = [(z + 1) % NZ, (z + NZ - 1) % NZ]
    loads = start_loads(r, h)
    barrier = pltpu.get_barrier_semaphore()
    for i in range(1, 8):
        pl.semaphore_signal(barrier, inc=1, device_id={"head": (h + i) % 8}, device_id_type=MESH)
    for k in range(1, NZ):
        pl.semaphore_signal(barrier, inc=1, device_id={"grp": x * NZ + (z + k) % NZ}, device_id_type=MESH)
    for k in range(1, NX):
        pl.semaphore_signal(barrier, inc=1, device_id={"grp": (x + k) % NX * NZ + z}, device_id_type=MESH)
    for other in (right, left):
        pl.semaphore_signal(barrier, inc=1, device_id={"grp": other}, device_id_type=MESH)
    loads[1].wait()
    table = jnp.concatenate([r.send_v[8 * k : 8 * k + 8, :] for k in range(NX)], axis=1)
    for k in range(NZ):
        r.mine[k] = jnp.broadcast_to(table[k : k + 1, :], (8, 128))

    def remote(source, target, send, recv, xx, zz):
        copy = pltpu.make_async_remote_copy(
            src_ref=source, dst_ref=target, send_sem=send, recv_sem=recv,
            device_id={"grp": xx * NZ + zz}, device_id_type=MESH,
        )
        copy.start()
        return copy

    for copy in loads[2:8]:
        copy.wait()
    encode(r.grid_v, r.emb_v, r.src_v, r.len_v, r.wkv_v, r.hid)
    unit, _ = norm_rows(r.hid[...])
    r.full[pl.ds(pl.multiple_of(h * 128, 128), 128), :] = (unit * r.pgain_v[...]).astype(BF)
    pl.semaphore_wait(barrier, 7 + NZ + NX - 2 + 2)
    rows = Ring(r.full, r.nsend, r.nrecv)
    rows.begin()
    r.tab[pl.ds(z, 1)] = r.mine[pl.ds(z, 1)]
    tables = [
        remote(r.mine.at[(z + k) % NZ], r.tab.at[z], r.tsend.at[k], r.trecv.at[k], x, (z + k) % NZ)
        for k in range(1, NZ)
    ]
    loads[0].wait()
    weights = Ring(r.wfull, r.wsend, r.wrecv)
    for copy in loads[8:16]:
        copy.wait()

    def halo(start, land, sem, to):
        return pltpu.make_async_remote_copy(
            src_ref=r.kvx.at[pl.ds(start, 128), :], dst_ref=r.kvx.at[pl.ds(land, 128), :],
            send_sem=r.hsend.at[sem], recv_sem=r.hrecv.at[sem],
            device_id={"grp": to}, device_id_type=MESH,
        )

    def project(block):
        at = pl.multiple_of(block * 128, 128)
        triple = nn(r.full[pl.ds(at, 128), :], r.wqkv_v[...]).astype(BF)
        r.q[pl.ds(at, 128), :] = (triple[:, :128].astype(F32) * SCALE).astype(BF)
        r.kvx[pl.ds(at + 256, 128), :] = triple[:, 128:]

        @pl.when(block >= 6)
        def _():
            halo(at + 256, at - 768, block - 6, right).start()

        @pl.when(block < 2)
        def _():
            halo(at + 256, at + 1280, block + 2, left).start()

    flip = rows.flip
    project(h)
    rows.side.wait_recv()
    rows.forward()
    project(rows.sib)
    rows.near()
    weights.begin()
    project(rows.dn)
    project(rows.up)
    rows.side_dn_a.wait_recv()
    rows.side_dn_b.wait_recv()
    project(rows.dn + flip)
    rows.side_up_a.wait_recv()
    rows.side_up_b.wait_recv()
    project(rows.up + flip)
    rows.far()
    project(rows.op)
    rows.side_op_a.wait_recv()
    rows.side_op_b.wait_recv()
    project(rows.op + flip)

    halos = [
        halo(1024, 0, 0, right), halo(1152, 128, 1, right), halo(256, 1280, 2, left), halo(384, 1408, 3, left),
    ]
    weights.forward()

    def give(start, column, to, land):
        return pltpu.make_async_remote_copy(
            src_ref=r.att.at[pl.ds(start, 128), :], dst_ref=r.afull.at[:, pl.ds(column, 128)],
            send_sem=r.asend.at[to], recv_sem=r.arecv.at[land],
            device_id={"head": to}, device_id_type=MESH,
        )

    mine = pl.multiple_of(h * 128, 128)
    for blk in (1, 2, 0, 3):
        if blk == 0:
            weights.near()
            for copy in halos:
                copy.wait_recv()
        low = jnp.where(g == 0, 256, 0) if blk == 0 else 0
        high = jnp.where(g == groups - 1, 512, 768) if blk == 3 else 768
        attend(r.q, r.kvx, r.att, blk, low, high)
        for to in (2 * blk, 2 * blk + 1):

            @pl.when(to != h)
            def _():
                give(to * 128, mine, to, h).start()

    weights.far()
    r.afull[:, pl.ds(mine, 128)] = r.att[pl.ds(mine, 128), :]
    r.query[...] = tn(r.grid_v[...], r.wq_v[...]).astype(BF)
    r.bg[...] = tn(r.dfc_v[...], r.wf_v[...])
    three = jnp.concatenate([r.dsrc_v[...], jnp.zeros((5, 256), jnp.int32)], axis=0)
    edges = three.astype(F32).T.astype(jnp.int32)
    for copy in (
        weights.side, weights.side_dn_a, weights.side_dn_b, weights.side_up_a, weights.side_up_b,
        weights.side_op_a, weights.side_op_b,
    ):
        copy.wait_recv()
    for other in range(8):

        @pl.when(other != h)
        def _():
            give(0, other * 128, other, other).wait()

    unit, inverse = norm_rows(r.hid[...] + nn(r.afull[...], r.wfull[...]))
    r.zbuf[z] = (unit * r.dgain_v[...]).astype(BF)
    sent = list(tables) + halos
    ring = {}

    def pass_on(way, d, chunk):
        block = (z + d) % NZ if way else (z + NZ - d) % NZ
        view = r.zbuf.at[block, :, pl.ds(512 * chunk, 512)]
        sem = way * 8 + d * 2 + chunk
        ring[way, d, chunk] = remote(view, view, r.zsend.at[sem], r.zrecv.at[sem], x, nexts[way])
        sent.append(ring[way, d, chunk])

    hops = ((0, 0), (1, 1), (0, 1), (1, 0))
    for way, chunk in hops:
        pass_on(way, 0, chunk)
    r.unit[...] = unit
    r.inv[...] = jnp.broadcast_to(inverse, (128, 128))

    def where(index):
        if index == 0:
            return z
        return (z + (NZ - (index + 1) // 2 if index % 2 else index // 2)) % NZ

    def chosen(zz):
        node = lax.broadcasted_iota(jnp.int32, (128, 128), 0)
        return (node == r.tab[zz][0:1, :]).astype(F32).astype(BF)

    crossing = {}
    land = pl.ds(pl.multiple_of(x * 32, 32), 32)

    def select(index, half):
        zz = where(index)
        cols = pl.ds(512 * half, 512)
        r.xs[index, :, HALF[half]] = tn(chosen(zz), r.zbuf[zz, :, HALF[half]]).astype(BF)
        for k in range(1, NX):
            xx = (x + k) % NX
            sem = index * 8 + half * NX + k
            crossing[index, half, k] = remote(
                r.xs.at[index, pl.ds(pl.multiple_of(xx * 32, 32), 32), cols], r.arrived.at[index, land, cols],
                r.xsend.at[sem], r.xrecv.at[sem], xx, z,
            )
        r.arrived[index, land, HALF[half]] = r.xs[index, land, HALF[half]]

    def absorb(first, count):
        for index in range(first, first + count):
            for half in range(2):
                for k in range(1, NX):
                    crossing[index, half, k].wait_recv()
        lane = lax.broadcasted_iota(jnp.int32, (1, 128), 1)
        slots = jnp.concatenate(
            [(lane // 32 * NZ + where(first + j)) * 32 + lane % 32 for j in range(count)], axis=1
        )
        picks = jnp.concatenate(
            [(edges[:, e : e + 1] == slots).astype(F32).astype(BF) for e in range(3)], axis=0
        )

        def tile(j, _):
            cols = pl.ds(pl.multiple_of(j * 256, 256), 256)
            block = r.arrived[first : first + count, :, cols].reshape(count * 128, 256)
            value = nn(picks, block).astype(BF)
            r.xe[:, cols] = value if first == 0 else r.xe[:, cols] + value
            return 0

        lax.fori_loop(0, 4, tile, 0)

    for copy in tables:
        copy.wait_recv()
    loads[16].wait()
    select(0, 0)
    select(0, 1)
    for d in range(1, 5):
        for phase in range(2):
            if d == 4 and phase == 1:
                continue
            for way in range(2):
                chunk = way ^ phase
                ring[way, d - 1, chunk].wait_recv()
                if d < 3 or (d == 3 and phase == 0):
                    pass_on(way, d, chunk)
            for way in range(2):
                select(7 if d == 4 else 2 * d - 1 + way, way ^ phase)
            if d == 2 and phase == 1:
                absorb(0, 3)
        if d == 3:
            absorb(3, 2)
    absorb(5, 2)
    absorb(7, 1)

    def unpack(j, _):
        cols = pl.ds(pl.multiple_of(j * 1024, 1024), 1024)
        r.kv[:, cols] = nn(r.xe[...], r.u_v[:, cols]).astype(BF)
        return 0

    lax.fori_loop(0, 2, unpack, 0)
    middle(r.kv, r.query, r.bg, r.mix)

    def unproject(j, _):
        cols = pl.ds(pl.multiple_of(j * 512, 512), 512)
        r.rg[:, cols] = nt(r.kv[...], r.u_v[cols, :]).astype(BF)
        return 0

    returning = {}

    def scatter(half, *indices):
        for index in indices:
            zz = where(index)
            row = lax.broadcasted_iota(jnp.int32, (128, 256), 0)
            slot = (row // 32 * NZ + zz) * 32 + row % 32
            pick = jnp.concatenate(
                [(r.dsrc_v[e : e + 1, :] == slot).astype(F32).astype(BF) for e in range(3)], axis=1
            )
            r.bs[index, :, HALF[half]] = nn(pick, r.rg[:, HALF[half]]).astype(BF)
            cols = pl.ds(512 * half, 512)
            for k in range(1, NX):
                xx = (x + k) % NX
                sem = index * 8 + half * NX + k
                returning[index, half, k] = remote(
                    r.bs.at[index, pl.ds(pl.multiple_of(xx * 32, 32), 32), cols],
                    r.rback.at[index, land, cols], r.bsend.at[sem], r.brecv.at[sem], xx, z,
                )
            r.rback[index, land, HALF[half]] = r.bs[index, land, HALF[half]]

    def partial(index, half):
        for k in range(1, NX):
            returning[index, half, k].wait_recv()
        return nn(chosen(where(index)), r.rback[index, :, HALF[half]])

    flow = {}

    def push(way, i, chunk, value, wait):
        for sub in range(2):
            cols = pl.ds(512 * chunk + 256 * sub, 256)
            part = value[:, 256 * sub : 256 * sub + 256]
            if wait:
                flow[way, i + 1, chunk, sub].wait_recv()
                part = part + r.ins[way, i + 1, :, cols].astype(F32)
            r.outs[way, i, :, cols] = part.astype(BF)
            sem = way * 16 + i * 4 + chunk * 2 + sub
            flow[way, i, chunk, sub] = remote(
                r.outs.at[way, i, :, cols], r.ins.at[way, i, :, cols], r.qsend.at[sem], r.qrecv.at[sem],
                x, nexts[way],
            )

    def step(d, phase):
        for way in range(2):
            chunk = way ^ phase
            push(way, d - 1, chunk, partial(2 * d - way, chunk), d < 3 or phase == 0)

    lax.fori_loop(0, 1, unproject, 0)
    scatter(0, 7)
    lax.fori_loop(1, 2, unproject, 0)
    scatter(1, 7)
    scatter(1, 6)
    scatter(0, 5)
    push(0, 3, 0, partial(7, 0), False)
    push(1, 3, 1, partial(7, 1), False)
    scatter(0, 6)
    scatter(1, 5)
    scatter(1, 4)
    step(3, 1)
    scatter(0, 3)
    scatter(0, 4)
    scatter(1, 3)
    r.est_o[...] = r.grid_v[0:100, :].astype(F32) + nt(r.wf_v[...], r.mix[...])
    step(3, 0)
    scatter(1, 2)
    scatter(0, 1)
    scatter(0, 2)
    scatter(1, 1)
    step(2, 1)
    scatter(0, 0)
    scatter(1, 0)
    step(2, 0)
    step(1, 1)
    step(1, 0)
    part = jnp.concatenate([partial(0, 0), partial(0, 1)], axis=1)
    for way in range(2):
        for chunk in range(4):
            flow[way, 0, chunk // 2, chunk % 2].wait_recv()
    grad = part + r.ins[0, 0].astype(F32) + r.ins[1, 0].astype(F32)
    unit = r.unit[...]
    scaled = grad * r.dgain_v[...]
    first = jnp.mean(scaled, axis=-1, keepdims=True)
    second = jnp.mean(scaled * unit, axis=-1, keepdims=True)
    r.vert_o[...] = r.inv[:, 0:1] * (scaled - first - unit * second)
    rows.finish()
    weights.finish()
    for copy in sent + list(crossing.values()) + list(returning.values()) + list(flow.values()):
        copy.wait_send()


VM = pl.BlockSpec(memory_space=pltpu.VMEM)
OUT = (jax.ShapeDtypeStruct((100, 256), F32), jax.ShapeDtypeStruct((128, 1024), F32))


def hand_over(a_ref, b_ref, c_ref, d_ref):
    c_ref[...] = a_ref[...]
    d_ref[...] = b_ref[...]


def body(
    grid_in, mesh_embed, enc_src, enc_len, enc_kv_weight, proc_gain, qkv_weight, out_weight,
    dec_gain, unpack, wq, wf, dec_send, dec_src, dforecast,
):
    est, vert = pl.pallas_call(
        kernel,
        out_shape=OUT,
        in_specs=[pl.BlockSpec(memory_space=pl.ANY)] * 15,
        out_specs=(VM, VM),
        scratch_shapes=[pltpu.VMEM(*s) for s in SCRATCH.values()] + [DMA((n,)) for n in SEMS.values()],
        compiler_params=pltpu.CompilerParams(
            vmem_limit_bytes=60 * 2**20, collective_id=0, has_side_effects=True
        ),
    )(
        grid_in, mesh_embed, enc_src, enc_len.reshape(1, -1), enc_kv_weight, proc_gain.reshape(1, -1),
        qkv_weight.transpose(1, 0, 2), out_weight, dec_gain.reshape(1, -1), unpack, wq, wf, dec_send,
        dec_src, dforecast,
    )
    return pl.pallas_call(
        hand_over, out_shape=OUT, in_specs=[VM, VM], out_specs=(VM, VM)
    )(est, vert)


def solution(mesh):
    return jax.shard_map(
        body,
        mesh=mesh,
        in_specs=(
            P(None, ("grp", "head")), P(("grp", "head"), None), P(None, ("grp", "head")),
            P(("grp", "head")), P(), P(), P(None, None, "head"), P("head", None), P(), P(), P(), P(),
            P(("grp", "head"), None), P(None, ("grp", "head")), P(None, ("grp", "head")),
        ),
        out_specs=(P(None, ("grp", "head")), P(("grp", "head"), None)),
        check_vma=False,
    )
```

```python
import jax
import jax.numpy as jnp
from jax import lax
from jax.experimental import pallas as pl
from jax.experimental.pallas import tpu as pltpu
from jax.sharding import PartitionSpec as P

F32 = jnp.float32
BF = jnp.bfloat16
EPS = 1e-05
SCALE = 0.125


def nn(a, b):
    return lax.dot_general(a, b, (((1,), (0,)), ((), ())), preferred_element_type=F32)


def nt(a, b):
    return lax.dot_general(a, b, (((1,), (1,)), ((), ())), preferred_element_type=F32)


def tn(a, b):
    return lax.dot_general(a, b, (((0,), (0,)), ((), ())), preferred_element_type=F32)


def half_masks():
    lane = lax.broadcasted_iota(jnp.int32, (1, 128), 1)
    return [(lane < 64).astype(F32).astype(BF), (lane >= 64).astype(F32).astype(BF)]


def norm_rows(rows):
    row_mean = jnp.mean(rows, axis=-1, keepdims=True)
    centred = rows - row_mean
    spread = jnp.mean(centred * centred, axis=-1, keepdims=True)
    inverse = lax.rsqrt(spread + EPS)
    return centred * inverse, inverse


def encode(grid_ref, emb_ref, src_ref, len_ref, wkv_ref, hid_ref):
    points = grid_ref.shape[1]
    nodes = emb_ref.shape[0]
    pid = lax.broadcasted_iota(jnp.int32, (points, nodes), 0)
    count = jnp.zeros((points, nodes), F32)
    lens = len_ref[...]
    for e in range(src_ref.shape[0]):
        row = jnp.where(e < lens, src_ref[e : e + 1, :], -1)
        count += (pid == row).astype(F32)
    dead = jnp.where(count > 0, 0.0, -jnp.inf)
    grid_t = grid_ref[...].T
    masks = half_masks()

    def pair(j, _):
        cols = pl.ds(j * 128, 128)
        vcols = pl.ds(j * 128 + 1024, 128)
        keys = nn(grid_t, wkv_ref[:, cols]).astype(BF)
        values = nn(grid_t, wkv_ref[:, vcols]).astype(BF)
        emb = emb_ref[:, cols]
        weights = []
        for n in range(2):
            score = nt(keys, emb * masks[n]) * SCALE + dead
            top = jnp.max(score, axis=0, keepdims=True)
            term = jnp.exp(score - top) * count
            weights.append((term / jnp.sum(term, axis=0, keepdims=True)).astype(BF))
        mixed = tn(weights[0], values * masks[0]) + tn(weights[1], values * masks[1])
        hid_ref[:, cols] = emb.astype(F32) + mixed
        return 0

    for j in range(emb_ref.shape[1] // 128):
        pair(j, 0)


def attend(q_ref, kv_ref, out_ref, blk, low, high):
    masks = half_masks()
    rows = pl.ds(blk * 256, 256)
    span = pl.ds(blk * 256, 768)
    q = q_ref[rows, :]
    k = kv_ref[span, 0:128]
    v = kv_ref[span, 128:256]
    gap = lax.broadcasted_iota(jnp.int32, (256, 768), 1) - lax.broadcasted_iota(
        jnp.int32, (256, 768), 0
    )
    col = lax.broadcasted_iota(jnp.int32, (256, 768), 1)
    live = (gap >= 0) & (gap <= 512) & (col >= low) & (col < high)
    total = None
    for n in range(2):
        score = jnp.where(live, nt(q * masks[n], k), -jnp.inf)
        top = jnp.max(score, axis=1, keepdims=True)
        term = jnp.exp(score - top)
        part = nn(term.astype(BF), v * masks[n]) / jnp.sum(term, axis=1, keepdims=True)
        total = part if total is None else total + part
    out_ref[rows, :] = total.astype(BF)


MESH = pl.DeviceIdType.MESH


class Ring:
    def __init__(self, full, send, recv):
        h = lax.axis_index("head")
        y, c = h // 2, h % 2
        self.full, self.send, self.recv, self.used = full, send, recv, []
        self.own = h
        self.up = ((y + 1) % 4) * 2 + c
        self.dn = ((y + 3) % 4) * 2 + c
        self.op = ((y + 2) % 4) * 2 + c
        self.flip = 1 - 2 * c
        self.sib = h + self.flip

    def copy(self, block, start, size, to, sem, land):
        view = self.full.at[pl.ds(block * 128 + start, size), :]
        copy = pltpu.make_async_remote_copy(
            src_ref=view, dst_ref=view, send_sem=self.send.at[sem], recv_sem=self.recv.at[land],
            device_id={"head": to}, device_id_type=MESH,
        )
        copy.start()
        self.used.append(copy)
        return copy

    def begin(self):
        own = self.own
        self.dn_a = self.copy(own, 0, 64, self.up, 0, 0)
        self.up_b = self.copy(own, 64, 64, self.dn, 1, 3)
        self.side = self.copy(own, 0, 128, self.sib, 4, 6)
        self.dn_b = self.copy(own, 64, 64, self.up, 2, 1)
        self.up_a = self.copy(own, 0, 64, self.dn, 3, 2)

    def forward(self):
        self.dn_a.wait_recv()
        self.op_a = self.copy(self.dn, 0, 64, self.up, 5, 4)
        self.side_dn_a = self.copy(self.dn, 0, 64, self.sib, 6, 7)
        self.up_b.wait_recv()
        self.op_b = self.copy(self.up, 64, 64, self.dn, 7, 5)
        self.side_up_b = self.copy(self.up, 64, 64, self.sib, 8, 8)

    def near(self):
        self.dn_b.wait_recv()
        self.side_dn_b = self.copy(self.dn, 64, 64, self.sib, 9, 9)
        self.up_a.wait_recv()
        self.side_up_a = self.copy(self.up, 0, 64, self.sib, 10, 10)

    def far(self):
        self.op_a.wait_recv()
        self.side_op_a = self.copy(self.op, 0, 64, self.sib, 11, 11)
        self.op_b.wait_recv()
        self.side_op_b = self.copy(self.op, 64, 64, self.sib, 12, 12)

    def finish(self):
        for copy in self.used:
            copy.wait_send()


def head_sum():
    row = lax.broadcasted_iota(jnp.int32, (1024, 128), 0) // 64
    col = lax.broadcasted_iota(jnp.int32, (1024, 128), 1)
    return (row == col).astype(F32).astype(BF)


def head_spread():
    row = lax.broadcasted_iota(jnp.int32, (128, 1024), 0)
    col = lax.broadcasted_iota(jnp.int32, (128, 1024), 1) // 64
    return (row == col).astype(F32).astype(BF)


NX, NZ = 4, 8
HALF = (slice(0, 512), slice(512, 1024))


def middle(kv, query, bg, mix):
    hsum = head_sum()
    spread = head_spread()

    def part(i, _):
        at = pl.multiple_of(i * 128, 128)
        rows = [pl.ds(at + e * 256, 128) for e in range(3)]
        qf = query[pl.ds(at, 128), :].astype(F32)
        back = bg[pl.ds(at, 128), :]
        products = [(qf * kv[r, :1024].astype(F32)).astype(BF) for r in rows]
        products += [(back * kv[r, 1024:].astype(F32)).astype(BF) for r in rows]
        sums = nn(jnp.concatenate(products, axis=0), hsum)
        score = [sums[e * 128 : e * 128 + 128] * SCALE for e in range(3)]
        along = [sums[e * 128 + 384 : e * 128 + 512] for e in range(3)]
        top = jnp.maximum(jnp.maximum(score[0], score[1]), score[2])
        term = [jnp.exp(s - top) for s in score]
        total = term[0] + term[1] + term[2]
        weight = [t / total for t in term]
        mean = weight[0] * along[0] + weight[1] * along[1] + weight[2] * along[2]
        heads = [w.astype(BF) for w in weight]
        heads += [(w * (s - mean) * SCALE).astype(BF) for w, s in zip(weight, along)]
        mixed = jnp.zeros((128, 1024), F32)
        for e in range(3):
            wide = nn(heads[e], spread)
            mixed += wide * kv[rows[e], 1024:].astype(F32)
            grad = nn(heads[3 + e], spread)
            kv[rows[e], :1024] = (grad * qf).astype(BF)
            kv[rows[e], 1024:] = (wide * back).astype(BF)
        mix[pl.ds(at, 128), :] = mixed.astype(BF)
        return 0

    lax.fori_loop(0, 2, part, 0)


DMA = pltpu.SemaphoreType.DMA
SCRATCH = {
    "grid_v": ((112, 256), BF), "emb_v": ((128, 1024), BF), "src_v": ((16, 128), jnp.int32),
    "len_v": ((1, 128), jnp.int32), "wkv_v": ((112, 2048), BF), "pgain_v": ((1, 1024), F32),
    "wqkv_v": ((1024, 384), BF), "dgain_v": ((1, 1024), F32), "hid": ((128, 1024), F32),
    "full": ((1024, 1024), BF), "wfull": ((1024, 1024), BF), "q": ((1024, 128), BF),
    "kvx": ((1536, 256), BF), "att": ((1024, 128), BF), "afull": ((128, 1024), BF),
    "unit": ((128, 1024), F32), "inv": ((128, 128), F32), "send_v": ((32, 32), jnp.int32),
    "mine": ((NZ, 8, 128), jnp.int32), "dfc_v": ((100, 256), BF), "dsrc_v": ((3, 256), jnp.int32),
    "wq_v": ((112, 1024), BF), "wf_v": ((100, 1024), BF), "u_v": ((1024, 2048), BF),
    "zbuf": ((NZ, 128, 1024), BF), "tab": ((NZ, 8, 128), jnp.int32), "xs": ((8, 128, 1024), BF),
    "arrived": ((8, 128, 1024), BF), "xe": ((768, 1024), BF), "kv": ((768, 2048), BF), "query": ((256, 1024), BF),
    "bg": ((256, 1024), F32), "mix": ((256, 1024), BF), "rg": ((768, 1024), BF),
    "bs": ((8, 128, 1024), BF), "rback": ((8, 128, 1024), BF), "outs": ((2, 4, 128, 1024), BF),
    "ins": ((2, 4, 128, 1024), BF),
}
SEMS = {
    "load": 18, "nsend": 13, "nrecv": 13, "wsend": 13, "wrecv": 13, "hsend": 4, "hrecv": 4, "asend": 8,
    "arecv": 8, "tsend": 8, "trecv": 8, "zsend": 16, "zrecv": 16, "xsend": 64, "xrecv": 64, "bsend": 64,
    "brecv": 64, "qsend": 32, "qrecv": 32,
}
INPUTS = (
    "grid_h", "emb_h", "src_h", "len_h", "wkv_h", "pgain_h", "wqkv_h", "wout_h", "dgain_h", "u_h", "wq_h",
    "wf_h", "send_h", "dsrc_h", "dfc_h",
)


class Refs:
    def __init__(self, refs):
        for name, ref in zip(INPUTS + ("est_o", "vert_o") + tuple(SCRATCH) + tuple(SEMS), refs):
            setattr(self, name, ref)


def start_loads(r, h):
    own = pl.ds(pl.multiple_of(h * 128, 128), 128)
    pairs = [
        (r.wout_h, r.wfull.at[own, :]), (r.send_h, r.send_v), (r.grid_h, r.grid_v), (r.emb_h, r.emb_v),
        (r.src_h, r.src_v), (r.len_h, r.len_v), (r.wkv_h, r.wkv_v), (r.pgain_h, r.pgain_v),
        (r.wqkv_h.at[0], r.wqkv_v.at[:, 0:128]), (r.wqkv_h.at[1], r.wqkv_v.at[:, 128:256]),
        (r.wqkv_h.at[2], r.wqkv_v.at[:, 256:384]), (r.dgain_h, r.dgain_v), (r.dfc_h, r.dfc_v),
        (r.dsrc_h, r.dsrc_v), (r.wq_h, r.wq_v), (r.wf_h, r.wf_v), (r.u_h, r.u_v),
    ]
    loads = [pltpu.make_async_copy(s, d, r.load.at[i]) for i, (s, d) in enumerate(pairs)]
    for copy in loads[1:8]:
        copy.start()
    return loads


def kernel(*refs):
    r = Refs(refs)
    g = lax.axis_index("grp")
    h = lax.axis_index("head")
    groups = lax.axis_size("grp")
    right, left = (g + 1) % groups, (g + groups - 1) % groups
    x, z = g // NZ, g % NZ
    nexts = [(z + 1) % NZ, (z + NZ - 1) % NZ]
    loads = start_loads(r, h)
    barrier = pltpu.get_barrier_semaphore()
    for i in range(1, 8):
        pl.semaphore_signal(barrier, inc=1, device_id={"head": (h + i) % 8}, device_id_type=MESH)
    for k in range(1, NZ):
        pl.semaphore_signal(barrier, inc=1, device_id={"grp": x * NZ + (z + k) % NZ}, device_id_type=MESH)
    for k in range(1, NX):
        pl.semaphore_signal(barrier, inc=1, device_id={"grp": (x + k) % NX * NZ + z}, device_id_type=MESH)
    for other in (right, left):
        pl.semaphore_signal(barrier, inc=1, device_id={"grp": other}, device_id_type=MESH)
    loads[1].wait()
    table = jnp.concatenate([r.send_v[8 * k : 8 * k + 8, :] for k in range(NX)], axis=1)
    for k in range(NZ):
        r.mine[k] = jnp.broadcast_to(table[k : k + 1, :], (8, 128))

    def remote(source, target, send, recv, xx, zz):
        copy = pltpu.make_async_remote_copy(
            src_ref=source, dst_ref=target, send_sem=send, recv_sem=recv,
            device_id={"grp": xx * NZ + zz}, device_id_type=MESH,
        )
        copy.start()
        return copy

    for copy in loads[2:8]:
        copy.wait()
    for copy in loads[8:] + loads[:1]:
        copy.start()
    encode(r.grid_v, r.emb_v, r.src_v, r.len_v, r.wkv_v, r.hid)
    unit, _ = norm_rows(r.hid[...])
    r.full[pl.ds(pl.multiple_of(h * 128, 128), 128), :] = (unit * r.pgain_v[...]).astype(BF)
    pl.semaphore_wait(barrier, 7 + NZ + NX - 2 + 2)
    rows = Ring(r.full, r.nsend, r.nrecv)
    rows.begin()
    r.tab[pl.ds(z, 1)] = r.mine[pl.ds(z, 1)]
    tables = [
        remote(r.mine.at[(z + k) % NZ], r.tab.at[z], r.tsend.at[k], r.trecv.at[k], x, (z + k) % NZ)
        for k in range(1, NZ)
    ]
    loads[0].wait()
    weights = Ring(r.wfull, r.wsend, r.wrecv)
    for copy in loads[8:16]:
        copy.wait()

    def halo(start, land, sem, to):
        return pltpu.make_async_remote_copy(
            src_ref=r.kvx.at[pl.ds(start, 128), :], dst_ref=r.kvx.at[pl.ds(land, 128), :],
            send_sem=r.hsend.at[sem], recv_sem=r.hrecv.at[sem],
            device_id={"grp": to}, device_id_type=MESH,
        )

    def project(block):
        at = pl.multiple_of(block * 128, 128)
        triple = nn(r.full[pl.ds(at, 128), :], r.wqkv_v[...]).astype(BF)
        r.q[pl.ds(at, 128), :] = (triple[:, :128].astype(F32) * SCALE).astype(BF)
        r.kvx[pl.ds(at + 256, 128), :] = triple[:, 128:]

        @pl.when(block >= 6)
        def _():
            halo(at + 256, at - 768, block - 6, right).start()

        @pl.when(block < 2)
        def _():
            halo(at + 256, at + 1280, block + 2, left).start()

    flip = rows.flip
    project(h)
    rows.side.wait_recv()
    rows.forward()
    project(rows.sib)
    rows.near()
    weights.begin()
    project(rows.dn)
    project(rows.up)
    rows.side_dn_a.wait_recv()
    rows.side_dn_b.wait_recv()
    project(rows.dn + flip)
    rows.side_up_a.wait_recv()
    rows.side_up_b.wait_recv()
    project(rows.up + flip)
    rows.far()
    project(rows.op)
    rows.side_op_a.wait_recv()
    rows.side_op_b.wait_recv()
    project(rows.op + flip)

    halos = [
        halo(1024, 0, 0, right), halo(1152, 128, 1, right), halo(256, 1280, 2, left), halo(384, 1408, 3, left),
    ]
    weights.forward()

    def give(start, column, to, land):
        return pltpu.make_async_remote_copy(
            src_ref=r.att.at[pl.ds(start, 128), :], dst_ref=r.afull.at[:, pl.ds(column, 128)],
            send_sem=r.asend.at[to], recv_sem=r.arecv.at[land],
            device_id={"head": to}, device_id_type=MESH,
        )

    mine = pl.multiple_of(h * 128, 128)
    for blk in (1, 2, 0, 3):
        if blk == 0:
            weights.near()
            for copy in halos:
                copy.wait_recv()
        low = jnp.where(g == 0, 256, 0) if blk == 0 else 0
        high = jnp.where(g == groups - 1, 512, 768) if blk == 3 else 768
        attend(r.q, r.kvx, r.att, blk, low, high)
        for to in (2 * blk, 2 * blk + 1):

            @pl.when(to != h)
            def _():
                give(to * 128, mine, to, h).start()

    weights.far()
    r.afull[:, pl.ds(mine, 128)] = r.att[pl.ds(mine, 128), :]
    r.query[...] = tn(r.grid_v[...], r.wq_v[...]).astype(BF)
    r.bg[...] = tn(r.dfc_v[...], r.wf_v[...])
    three = jnp.concatenate([r.dsrc_v[...], jnp.zeros((5, 256), jnp.int32)], axis=0)
    edges = three.astype(F32).T.astype(jnp.int32)
    for copy in (
        weights.side, weights.side_dn_a, weights.side_dn_b, weights.side_up_a, weights.side_up_b,
        weights.side_op_a, weights.side_op_b,
    ):
        copy.wait_recv()
    for other in range(8):

        @pl.when(other != h)
        def _():
            give(0, other * 128, other, other).wait()

    unit, inverse = norm_rows(r.hid[...] + nn(r.afull[...], r.wfull[...]))
    r.zbuf[z] = (unit * r.dgain_v[...]).astype(BF)
    sent = list(tables) + halos
    ring = {}

    def pass_on(way, d, chunk):
        block = (z + d) % NZ if way else (z + NZ - d) % NZ
        view = r.zbuf.at[block, :, pl.ds(512 * chunk, 512)]
        sem = way * 8 + d * 2 + chunk
        ring[way, d, chunk] = remote(view, view, r.zsend.at[sem], r.zrecv.at[sem], x, nexts[way])
        sent.append(ring[way, d, chunk])

    hops = ((0, 0), (1, 1), (0, 1), (1, 0))
    for way, chunk in hops:
        pass_on(way, 0, chunk)

    def where(index):
        if index == 0:
            return z
        return (z + (NZ - (index + 1) // 2 if index % 2 else index // 2)) % NZ

    def chosen(zz):
        node = lax.broadcasted_iota(jnp.int32, (128, 128), 0)
        return (node == r.tab[zz][0:1, :]).astype(F32).astype(BF)

    crossing = {}
    land = pl.ds(pl.multiple_of(x * 32, 32), 32)

    def select(index, half):
        zz = where(index)
        cols = pl.ds(512 * half, 512)
        r.xs[index, :, HALF[half]] = tn(chosen(zz), r.zbuf[zz, :, HALF[half]]).astype(BF)
        for k in (2, 1, 3):
            xx = (x + k) % NX
            sem = index * 8 + half * NX + k
            crossing[index, half, k] = remote(
                r.xs.at[index, pl.ds(pl.multiple_of(xx * 32, 32), 32), cols], r.arrived.at[index, land, cols],
                r.xsend.at[sem], r.xrecv.at[sem], xx, z,
            )
        r.arrived[index, land, HALF[half]] = r.xs[index, land, HALF[half]]

    def absorb(first, count):
        for index in range(first, first + count):
            for half in range(2):
                for k in range(1, NX):
                    crossing[index, half, k].wait_recv()
        lane = lax.broadcasted_iota(jnp.int32, (1, 128), 1)
        slots = jnp.concatenate(
            [(lane // 32 * NZ + where(first + j)) * 32 + lane % 32 for j in range(count)], axis=1
        )
        picks = jnp.concatenate(
            [(edges[:, e : e + 1] == slots).astype(F32).astype(BF) for e in range(3)], axis=0
        )

        def tile(j, _):
            cols = pl.ds(pl.multiple_of(j * 256, 256), 256)
            block = r.arrived[first : first + count, :, cols].reshape(count * 128, 256)
            value = nn(picks, block).astype(BF)
            r.xe[:, cols] = value if first == 0 else r.xe[:, cols] + value
            return 0

        lax.fori_loop(0, 4, tile, 0)

    for copy in tables:
        copy.wait_recv()
    loads[16].wait()
    select(0, 0)
    select(0, 1)
    r.unit[...] = unit
    r.inv[...] = jnp.broadcast_to(inverse, (128, 128))
    for d in range(1, 5):
        for phase in range(2):
            if d == 4 and phase == 1:
                continue
            for way in range(2):
                chunk = way ^ phase
                ring[way, d - 1, chunk].wait_recv()
                if d < 3 or (d == 3 and phase == 0):
                    pass_on(way, d, chunk)
            for way in range(2):
                select(7 if d == 4 else 2 * d - 1 + way, way ^ phase)
            if d == 2 and phase == 1:
                absorb(0, 3)
        if d == 3:
            absorb(3, 2)
    absorb(5, 2)
    absorb(7, 1)

    def unpack(j, _):
        cols = pl.ds(pl.multiple_of(j * 1024, 1024), 1024)
        r.kv[:, cols] = nn(r.xe[...], r.u_v[:, cols]).astype(BF)
        return 0

    lax.fori_loop(0, 2, unpack, 0)
    middle(r.kv, r.query, r.bg, r.mix)

    def unproject(j, _):
        cols = pl.ds(pl.multiple_of(j * 512, 512), 512)
        r.rg[:, cols] = nt(r.kv[...], r.u_v[cols, :]).astype(BF)
        return 0

    returning = {}

    def scatter(half, *indices):
        for index in indices:
            zz = where(index)
            row = lax.broadcasted_iota(jnp.int32, (128, 256), 0)
            slot = (row // 32 * NZ + zz) * 32 + row % 32
            pick = jnp.concatenate(
                [(r.dsrc_v[e : e + 1, :] == slot).astype(F32).astype(BF) for e in range(3)], axis=1
            )
            r.bs[index, :, HALF[half]] = nn(pick, r.rg[:, HALF[half]]).astype(BF)
            cols = pl.ds(512 * half, 512)
            for k in (2, 1, 3):
                xx = (x + k) % NX
                sem = index * 8 + half * NX + k
                returning[index, half, k] = remote(
                    r.bs.at[index, pl.ds(pl.multiple_of(xx * 32, 32), 32), cols],
                    r.rback.at[index, land, cols], r.bsend.at[sem], r.brecv.at[sem], xx, z,
                )
            r.rback[index, land, HALF[half]] = r.bs[index, land, HALF[half]]

    def partial(index, half):
        for k in range(1, NX):
            returning[index, half, k].wait_recv()
        return nn(chosen(where(index)), r.rback[index, :, HALF[half]])

    flow = {}

    def push(way, i, chunk, value, wait):
        for sub in range(2):
            cols = pl.ds(512 * chunk + 256 * sub, 256)
            part = value[:, 256 * sub : 256 * sub + 256]
            if wait:
                flow[way, i + 1, chunk, sub].wait_recv()
                part = part + r.ins[way, i + 1, :, cols].astype(F32)
            r.outs[way, i, :, cols] = part.astype(BF)
            sem = way * 16 + i * 4 + chunk * 2 + sub
            flow[way, i, chunk, sub] = remote(
                r.outs.at[way, i, :, cols], r.ins.at[way, i, :, cols], r.qsend.at[sem], r.qrecv.at[sem],
                x, nexts[way],
            )

    def step(d, phase):
        for way in range(2):
            chunk = way ^ phase
            push(way, d - 1, chunk, partial(2 * d - way, chunk), d < 3 or phase == 0)

    lax.fori_loop(0, 1, unproject, 0)
    scatter(0, 7)
    lax.fori_loop(1, 2, unproject, 0)
    scatter(1, 7)
    scatter(1, 6)
    scatter(0, 5)
    push(0, 3, 0, partial(7, 0), False)
    push(1, 3, 1, partial(7, 1), False)
    scatter(0, 6)
    scatter(1, 5)
    scatter(1, 4)
    step(3, 1)
    scatter(0, 3)
    scatter(0, 4)
    scatter(1, 3)
    r.est_o[...] = r.grid_v[0:100, :].astype(F32) + nt(r.wf_v[...], r.mix[...])
    step(3, 0)
    scatter(1, 2)
    scatter(0, 1)
    scatter(0, 2)
    scatter(1, 1)
    step(2, 1)
    scatter(0, 0)
    scatter(1, 0)
    step(2, 0)
    step(1, 1)
    step(1, 0)
    part = jnp.concatenate([partial(0, 0), partial(0, 1)], axis=1)
    for way in range(2):
        for chunk in range(4):
            flow[way, 0, chunk // 2, chunk % 2].wait_recv()
    grad = part + r.ins[0, 0].astype(F32) + r.ins[1, 0].astype(F32)
    unit = r.unit[...]
    scaled = grad * r.dgain_v[...]
    first = jnp.mean(scaled, axis=-1, keepdims=True)
    second = jnp.mean(scaled * unit, axis=-1, keepdims=True)
    r.vert_o[...] = r.inv[:, 0:1] * (scaled - first - unit * second)
    rows.finish()
    weights.finish()
    for copy in sent + list(crossing.values()) + list(returning.values()) + list(flow.values()):
        copy.wait_send()


VM = pl.BlockSpec(memory_space=pltpu.VMEM)
OUT = (jax.ShapeDtypeStruct((100, 256), F32), jax.ShapeDtypeStruct((128, 1024), F32))


def hand_over(a_ref, b_ref, c_ref, d_ref):
    c_ref[...] = a_ref[...]
    d_ref[...] = b_ref[...]


def body(
    grid_in, mesh_embed, enc_src, enc_len, enc_kv_weight, proc_gain, qkv_weight, out_weight,
    dec_gain, unpack, wq, wf, dec_send, dec_src, dforecast,
):
    est, vert = pl.pallas_call(
        kernel,
        out_shape=OUT,
        in_specs=[pl.BlockSpec(memory_space=pl.ANY)] * 15,
        out_specs=(VM, VM),
        scratch_shapes=[pltpu.VMEM(*s) for s in SCRATCH.values()] + [DMA((n,)) for n in SEMS.values()],
        compiler_params=pltpu.CompilerParams(
            vmem_limit_bytes=60 * 2**20, collective_id=0, has_side_effects=True
        ),
    )(
        grid_in, mesh_embed, enc_src, enc_len.reshape(1, -1), enc_kv_weight, proc_gain.reshape(1, -1),
        qkv_weight.transpose(1, 0, 2), out_weight, dec_gain.reshape(1, -1), unpack, wq, wf, dec_send,
        dec_src, dforecast,
    )
    return pl.pallas_call(
        hand_over, out_shape=OUT, in_specs=[VM, VM], out_specs=(VM, VM)
    )(est, vert)


def solution(mesh):
    return jax.shard_map(
        body,
        mesh=mesh,
        in_specs=(
            P(None, ("grp", "head")), P(("grp", "head"), None), P(None, ("grp", "head")),
            P(("grp", "head")), P(), P(), P(None, None, "head"), P("head", None), P(), P(), P(), P(),
            P(("grp", "head"), None), P(None, ("grp", "head")), P(None, ("grp", "head")),
        ),
        out_specs=(P(None, ("grp", "head")), P(("grp", "head"), None)),
        check_vma=False,
    )
```

```python
import jax
import jax.numpy as jnp
from jax import lax
from jax.experimental import pallas as pl
from jax.experimental.pallas import tpu as pltpu
from jax.sharding import PartitionSpec as P

F32 = jnp.float32
BF = jnp.bfloat16
EPS = 1e-05
SCALE = 0.125


def nn(a, b):
    return lax.dot_general(a, b, (((1,), (0,)), ((), ())), preferred_element_type=F32)


def nt(a, b):
    return lax.dot_general(a, b, (((1,), (1,)), ((), ())), preferred_element_type=F32)


def tn(a, b):
    return lax.dot_general(a, b, (((0,), (0,)), ((), ())), preferred_element_type=F32)


def half_masks():
    lane = lax.broadcasted_iota(jnp.int32, (1, 128), 1)
    return [(lane < 64).astype(F32).astype(BF), (lane >= 64).astype(F32).astype(BF)]


def norm_rows(rows):
    row_mean = jnp.mean(rows, axis=-1, keepdims=True)
    centred = rows - row_mean
    spread = jnp.mean(centred * centred, axis=-1, keepdims=True)
    inverse = lax.rsqrt(spread + EPS)
    return centred * inverse, inverse


def encode(grid_ref, emb_ref, src_ref, len_ref, wkv_ref, hid_ref):
    points = grid_ref.shape[1]
    nodes = emb_ref.shape[0]
    pid = lax.broadcasted_iota(jnp.int32, (points, nodes), 0)
    count = jnp.zeros((points, nodes), F32)
    lens = len_ref[...]
    for e in range(src_ref.shape[0]):
        row = jnp.where(e < lens, src_ref[e : e + 1, :], -1)
        count += (pid == row).astype(F32)
    dead = jnp.where(count > 0, 0.0, -jnp.inf)
    grid_t = grid_ref[...].T
    masks = half_masks()

    def pair(j, _):
        cols = pl.ds(j * 128, 128)
        vcols = pl.ds(j * 128 + 1024, 128)
        keys = nn(grid_t, wkv_ref[:, cols]).astype(BF)
        values = nn(grid_t, wkv_ref[:, vcols]).astype(BF)
        emb = emb_ref[:, cols]
        weights = []
        for n in range(2):
            score = nt(keys, emb * masks[n]) * SCALE + dead
            top = jnp.max(score, axis=0, keepdims=True)
            term = jnp.exp(score - top) * count
            weights.append((term / jnp.sum(term, axis=0, keepdims=True)).astype(BF))
        mixed = tn(weights[0], values * masks[0]) + tn(weights[1], values * masks[1])
        hid_ref[:, cols] = emb.astype(F32) + mixed
        return 0

    for j in range(emb_ref.shape[1] // 128):
        pair(j, 0)


def attend(q_ref, kv_ref, out_ref, blk, low, high):
    masks = half_masks()
    rows = pl.ds(blk * 256, 256)
    span = pl.ds(blk * 256, 768)
    q = q_ref[rows, :]
    k = kv_ref[span, 0:128]
    v = kv_ref[span, 128:256]
    gap = lax.broadcasted_iota(jnp.int32, (256, 256), 1) - lax.broadcasted_iota(
        jnp.int32, (256, 256), 0
    )
    early, late = gap >= low, gap <= high
    total = None
    for n in range(2):
        score = nt(q * masks[n], k)
        score = jnp.concatenate(
            [
                jnp.where(early, score[:, :256], -jnp.inf),
                score[:, 256:512],
                jnp.where(late, score[:, 512:], -jnp.inf),
            ],
            axis=1,
        )
        top = jnp.max(score, axis=1, keepdims=True)
        term = jnp.exp(score - top)
        part = nn(term.astype(BF), v * masks[n]) / jnp.sum(term, axis=1, keepdims=True)
        total = part if total is None else total + part
    out_ref[rows, :] = total.astype(BF)


MESH = pl.DeviceIdType.MESH


class Ring:
    def __init__(self, full, send, recv):
        h = lax.axis_index("head")
        y, c = h // 2, h % 2
        self.full, self.send, self.recv, self.used = full, send, recv, []
        self.own = h
        self.up = ((y + 1) % 4) * 2 + c
        self.dn = ((y + 3) % 4) * 2 + c
        self.op = ((y + 2) % 4) * 2 + c
        self.flip = 1 - 2 * c
        self.sib = h + self.flip

    def copy(self, block, start, size, to, sem, land):
        view = self.full.at[pl.ds(block * 128 + start, size), :]
        copy = pltpu.make_async_remote_copy(
            src_ref=view, dst_ref=view, send_sem=self.send.at[sem], recv_sem=self.recv.at[land],
            device_id={"head": to}, device_id_type=MESH,
        )
        copy.start()
        self.used.append(copy)
        return copy

    def begin(self):
        own = self.own
        self.dn_a = self.copy(own, 0, 64, self.up, 0, 0)
        self.up_b = self.copy(own, 64, 64, self.dn, 1, 3)
        self.side = self.copy(own, 0, 128, self.sib, 4, 6)
        self.dn_b = self.copy(own, 64, 64, self.up, 2, 1)
        self.up_a = self.copy(own, 0, 64, self.dn, 3, 2)

    def forward(self):
        self.dn_a.wait_recv()
        self.op_a = self.copy(self.dn, 0, 64, self.up, 5, 4)
        self.side_dn_a = self.copy(self.dn, 0, 64, self.sib, 6, 7)
        self.up_b.wait_recv()
        self.op_b = self.copy(self.up, 64, 64, self.dn, 7, 5)
        self.side_up_b = self.copy(self.up, 64, 64, self.sib, 8, 8)

    def near(self):
        self.dn_b.wait_recv()
        self.side_dn_b = self.copy(self.dn, 64, 64, self.sib, 9, 9)
        self.up_a.wait_recv()
        self.side_up_a = self.copy(self.up, 0, 64, self.sib, 10, 10)

    def far(self):
        self.op_a.wait_recv()
        self.side_op_a = self.copy(self.op, 0, 64, self.sib, 11, 11)
        self.op_b.wait_recv()
        self.side_op_b = self.copy(self.op, 64, 64, self.sib, 12, 12)

    def finish(self):
        for copy in self.used:
            copy.wait_send()


def head_sum():
    row = lax.broadcasted_iota(jnp.int32, (1024, 128), 0) // 64
    col = lax.broadcasted_iota(jnp.int32, (1024, 128), 1)
    return (row == col).astype(F32).astype(BF)


def head_spread():
    row = lax.broadcasted_iota(jnp.int32, (128, 1024), 0)
    col = lax.broadcasted_iota(jnp.int32, (128, 1024), 1) // 64
    return (row == col).astype(F32).astype(BF)


NX, NZ = 4, 8
HALF = (slice(0, 512), slice(512, 1024))


def middle(kv, query, bg, mix):
    hsum = head_sum()
    spread = head_spread()

    def part(i, _):
        at = pl.multiple_of(i * 128, 128)
        rows = [pl.ds(at + e * 256, 128) for e in range(3)]
        qf = query[pl.ds(at, 128), :].astype(F32)
        back = bg[pl.ds(at, 128), :]
        products = [(qf * kv[r, :1024].astype(F32)).astype(BF) for r in rows]
        products += [(back * kv[r, 1024:].astype(F32)).astype(BF) for r in rows]
        sums = nn(jnp.concatenate(products, axis=0), hsum)
        score = [sums[e * 128 : e * 128 + 128] * SCALE for e in range(3)]
        along = [sums[e * 128 + 384 : e * 128 + 512] for e in range(3)]
        top = jnp.maximum(jnp.maximum(score[0], score[1]), score[2])
        term = [jnp.exp(s - top) for s in score]
        total = term[0] + term[1] + term[2]
        weight = [t / total for t in term]
        mean = weight[0] * along[0] + weight[1] * along[1] + weight[2] * along[2]
        heads = [w.astype(BF) for w in weight]
        heads += [(w * (s - mean) * SCALE).astype(BF) for w, s in zip(weight, along)]
        mixed = jnp.zeros((128, 1024), F32)
        for e in range(3):
            wide = nn(heads[e], spread)
            mixed += wide * kv[rows[e], 1024:].astype(F32)
            grad = nn(heads[3 + e], spread)
            kv[rows[e], :1024] = (grad * qf).astype(BF)
            kv[rows[e], 1024:] = (wide * back).astype(BF)
        mix[pl.ds(at, 128), :] = mixed.astype(BF)
        return 0

    lax.fori_loop(0, 2, part, 0)


DMA = pltpu.SemaphoreType.DMA
SCRATCH = {
    "grid_v": ((112, 256), BF), "emb_v": ((128, 1024), BF), "src_v": ((16, 128), jnp.int32),
    "len_v": ((1, 128), jnp.int32), "wkv_v": ((112, 2048), BF), "pgain_v": ((1, 1024), F32),
    "wqkv_v": ((1024, 384), BF), "dgain_v": ((1, 1024), F32), "hid": ((128, 1024), F32),
    "full": ((1024, 1024), BF), "wfull": ((1024, 1024), BF), "q": ((1024, 128), BF),
    "kvx": ((1536, 256), BF), "att": ((1024, 128), BF), "afull": ((128, 1024), BF),
    "unit": ((128, 1024), F32), "inv": ((128, 128), F32), "send_v": ((32, 32), jnp.int32),
    "mine": ((NZ, 8, 128), jnp.int32), "dfc_v": ((100, 256), BF), "dsrc_v": ((3, 256), jnp.int32),
    "wq_v": ((112, 1024), BF), "wf_v": ((100, 1024), BF), "u_v": ((1024, 2048), BF),
    "zbuf": ((NZ, 128, 1024), BF), "tab": ((NZ, 8, 128), jnp.int32), "xs": ((8, 128, 1024), BF),
    "arrived": ((8, 128, 1024), BF), "xe": ((768, 1024), BF), "kv": ((768, 2048), BF), "query": ((256, 1024), BF),
    "bg": ((256, 1024), F32), "mix": ((256, 1024), BF), "rg": ((768, 1024), BF),
    "bs": ((8, 128, 1024), BF), "rback": ((8, 128, 1024), BF), "outs": ((2, 4, 128, 1024), BF),
    "ins": ((2, 4, 128, 1024), BF),
}
SEMS = {
    "load": 18, "nsend": 13, "nrecv": 13, "wsend": 13, "wrecv": 13, "hsend": 4, "hrecv": 4, "asend": 8,
    "arecv": 8, "tsend": 8, "trecv": 8, "zsend": 16, "zrecv": 16, "xsend": 64, "xrecv": 64, "bsend": 64,
    "brecv": 64, "qsend": 32, "qrecv": 32,
}
INPUTS = (
    "grid_h", "emb_h", "src_h", "len_h", "wkv_h", "pgain_h", "wqkv_h", "wout_h", "dgain_h", "u_h", "wq_h",
    "wf_h", "send_h", "dsrc_h", "dfc_h",
)


class Refs:
    def __init__(self, refs):
        for name, ref in zip(INPUTS + ("est_o", "vert_o") + tuple(SCRATCH) + tuple(SEMS), refs):
            setattr(self, name, ref)


def start_loads(r, h):
    own = pl.ds(pl.multiple_of(h * 128, 128), 128)
    pairs = [
        (r.wout_h, r.wfull.at[own, :]), (r.send_h, r.send_v), (r.grid_h, r.grid_v), (r.emb_h, r.emb_v),
        (r.src_h, r.src_v), (r.len_h, r.len_v), (r.wkv_h, r.wkv_v), (r.pgain_h, r.pgain_v),
        (r.wqkv_h.at[0], r.wqkv_v.at[:, 0:128]), (r.wqkv_h.at[1], r.wqkv_v.at[:, 128:256]),
        (r.wqkv_h.at[2], r.wqkv_v.at[:, 256:384]), (r.dgain_h, r.dgain_v), (r.dfc_h, r.dfc_v),
        (r.dsrc_h, r.dsrc_v), (r.wq_h, r.wq_v), (r.wf_h, r.wf_v), (r.u_h, r.u_v),
    ]
    loads = [pltpu.make_async_copy(s, d, r.load.at[i]) for i, (s, d) in enumerate(pairs)]
    for copy in loads[1:8]:
        copy.start()
    return loads


def kernel(*refs):
    r = Refs(refs)
    g = lax.axis_index("grp")
    h = lax.axis_index("head")
    groups = lax.axis_size("grp")
    right, left = (g + 1) % groups, (g + groups - 1) % groups
    x, z = g // NZ, g % NZ
    nexts = [(z + 1) % NZ, (z + NZ - 1) % NZ]
    loads = start_loads(r, h)
    barrier = pltpu.get_barrier_semaphore()
    for i in range(1, 8):
        pl.semaphore_signal(barrier, inc=1, device_id={"head": (h + i) % 8}, device_id_type=MESH)
    for k in range(1, NZ):
        pl.semaphore_signal(barrier, inc=1, device_id={"grp": x * NZ + (z + k) % NZ}, device_id_type=MESH)
    for k in range(1, NX):
        pl.semaphore_signal(barrier, inc=1, device_id={"grp": (x + k) % NX * NZ + z}, device_id_type=MESH)
    for other in (right, left):
        pl.semaphore_signal(barrier, inc=1, device_id={"grp": other}, device_id_type=MESH)
    loads[1].wait()
    table = jnp.concatenate([r.send_v[8 * k : 8 * k + 8, :] for k in range(NX)], axis=1)
    for k in range(NZ):
        r.mine[k] = jnp.broadcast_to(table[k : k + 1, :], (8, 128))

    def remote(source, target, send, recv, xx, zz):
        copy = pltpu.make_async_remote_copy(
            src_ref=source, dst_ref=target, send_sem=send, recv_sem=recv,
            device_id={"grp": xx * NZ + zz}, device_id_type=MESH,
        )
        copy.start()
        return copy

    for copy in loads[2:8]:
        copy.wait()
    for copy in loads[8:] + loads[:1]:
        copy.start()
    encode(r.grid_v, r.emb_v, r.src_v, r.len_v, r.wkv_v, r.hid)
    unit, _ = norm_rows(r.hid[...])
    r.full[pl.ds(pl.multiple_of(h * 128, 128), 128), :] = (unit * r.pgain_v[...]).astype(BF)
    pl.semaphore_wait(barrier, 7 + NZ + NX - 2 + 2)
    rows = Ring(r.full, r.nsend, r.nrecv)
    rows.begin()
    r.tab[pl.ds(z, 1)] = r.mine[pl.ds(z, 1)]
    tables = [
        remote(r.mine.at[(z + k) % NZ], r.tab.at[z], r.tsend.at[k], r.trecv.at[k], x, (z + k) % NZ)
        for k in range(1, NZ)
    ]
    loads[0].wait()
    weights = Ring(r.wfull, r.wsend, r.wrecv)
    for copy in loads[8:16]:
        copy.wait()

    def halo(start, land, sem, to):
        return pltpu.make_async_remote_copy(
            src_ref=r.kvx.at[pl.ds(start, 128), :], dst_ref=r.kvx.at[pl.ds(land, 128), :],
            send_sem=r.hsend.at[sem], recv_sem=r.hrecv.at[sem],
            device_id={"grp": to}, device_id_type=MESH,
        )

    def project(block):
        at = pl.multiple_of(block * 128, 128)
        triple = nn(r.full[pl.ds(at, 128), :], r.wqkv_v[...]).astype(BF)
        r.q[pl.ds(at, 128), :] = (triple[:, :128].astype(F32) * SCALE).astype(BF)
        r.kvx[pl.ds(at + 256, 128), :] = triple[:, 128:]

        @pl.when(block >= 6)
        def _():
            halo(at + 256, at - 768, block - 6, right).start()

        @pl.when(block < 2)
        def _():
            halo(at + 256, at + 1280, block + 2, left).start()

    flip = rows.flip
    project(h)
    rows.side.wait_recv()
    rows.forward()
    project(rows.sib)
    rows.near()
    weights.begin()
    project(rows.dn)
    project(rows.up)
    rows.side_dn_a.wait_recv()
    rows.side_dn_b.wait_recv()
    project(rows.dn + flip)
    rows.side_up_a.wait_recv()
    rows.side_up_b.wait_recv()
    project(rows.up + flip)
    rows.far()
    project(rows.op)
    rows.side_op_a.wait_recv()
    rows.side_op_b.wait_recv()
    project(rows.op + flip)

    halos = [
        halo(1024, 0, 0, right), halo(1152, 128, 1, right), halo(256, 1280, 2, left), halo(384, 1408, 3, left),
    ]
    weights.forward()

    def give(start, column, to, land):
        return pltpu.make_async_remote_copy(
            src_ref=r.att.at[pl.ds(start, 128), :], dst_ref=r.afull.at[:, pl.ds(column, 128)],
            send_sem=r.asend.at[to], recv_sem=r.arecv.at[land],
            device_id={"head": to}, device_id_type=MESH,
        )

    mine = pl.multiple_of(h * 128, 128)
    for blk in (1, 2, 0, 3):
        if blk == 0:
            weights.near()
            for copy in halos:
                copy.wait_recv()
        low = jnp.where(g == 0, 256, 0) if blk == 0 else 0
        high = jnp.where(g == groups - 1, -256, 0) if blk == 3 else 0
        attend(r.q, r.kvx, r.att, blk, low, high)
        for to in (2 * blk, 2 * blk + 1):

            @pl.when(to != h)
            def _():
                give(to * 128, mine, to, h).start()

    weights.far()
    r.afull[:, pl.ds(mine, 128)] = r.att[pl.ds(mine, 128), :]
    r.query[...] = tn(r.grid_v[...], r.wq_v[...]).astype(BF)
    r.bg[...] = tn(r.dfc_v[...], r.wf_v[...])
    three = jnp.concatenate([r.dsrc_v[...], jnp.zeros((5, 256), jnp.int32)], axis=0)
    edges = three.astype(F32).T.astype(jnp.int32)
    for copy in (
        weights.side, weights.side_dn_a, weights.side_dn_b, weights.side_up_a, weights.side_up_b,
        weights.side_op_a, weights.side_op_b,
    ):
        copy.wait_recv()
    for other in range(8):

        @pl.when(other != h)
        def _():
            give(0, other * 128, other, other).wait()

    unit, inverse = norm_rows(r.hid[...] + nn(r.afull[...], r.wfull[...]))
    r.zbuf[z] = (unit * r.dgain_v[...]).astype(BF)
    sent = list(tables) + halos
    ring = {}

    def pass_on(way, d, chunk):
        block = (z + d) % NZ if way else (z + NZ - d) % NZ
        view = r.zbuf.at[block, :, pl.ds(512 * chunk, 512)]
        sem = way * 8 + d * 2 + chunk
        ring[way, d, chunk] = remote(view, view, r.zsend.at[sem], r.zrecv.at[sem], x, nexts[way])
        sent.append(ring[way, d, chunk])

    hops = ((0, 0), (1, 1), (0, 1), (1, 0))
    for way, chunk in hops:
        pass_on(way, 0, chunk)

    def where(index):
        if index == 0:
            return z
        return (z + (NZ - (index + 1) // 2 if index % 2 else index // 2)) % NZ

    def chosen(zz):
        node = lax.broadcasted_iota(jnp.int32, (128, 128), 0)
        return (node == r.tab[zz][0:1, :]).astype(F32).astype(BF)

    crossing = {}
    land = pl.ds(pl.multiple_of(x * 32, 32), 32)

    def select(index, half):
        zz = where(index)
        cols = pl.ds(512 * half, 512)
        r.xs[index, :, HALF[half]] = tn(chosen(zz), r.zbuf[zz, :, HALF[half]]).astype(BF)
        for k in (2, 1, 3):
            xx = (x + k) % NX
            sem = index * 8 + half * NX + k
            crossing[index, half, k] = remote(
                r.xs.at[index, pl.ds(pl.multiple_of(xx * 32, 32), 32), cols], r.arrived.at[index, land, cols],
                r.xsend.at[sem], r.xrecv.at[sem], xx, z,
            )
        r.arrived[index, land, HALF[half]] = r.xs[index, land, HALF[half]]

    def absorb(first, count):
        for index in range(first, first + count):
            for half in range(2):
                for k in range(1, NX):
                    crossing[index, half, k].wait_recv()
        lane = lax.broadcasted_iota(jnp.int32, (1, 128), 1)
        slots = jnp.concatenate(
            [(lane // 32 * NZ + where(first + j)) * 32 + lane % 32 for j in range(count)], axis=1
        )
        picks = jnp.concatenate(
            [(edges[:, e : e + 1] == slots).astype(F32).astype(BF) for e in range(3)], axis=0
        )

        def tile(j, _):
            cols = pl.ds(pl.multiple_of(j * 256, 256), 256)
            block = r.arrived[first : first + count, :, cols].reshape(count * 128, 256)
            value = nn(picks, block).astype(BF)
            r.xe[:, cols] = value if first == 0 else r.xe[:, cols] + value
            return 0

        lax.fori_loop(0, 4, tile, 0)

    for copy in tables:
        copy.wait_recv()
    loads[16].wait()
    select(0, 0)
    select(0, 1)
    r.unit[...] = unit
    r.inv[...] = jnp.broadcast_to(inverse, (128, 128))
    for d in range(1, 5):
        for phase in range(2):
            if d == 4 and phase == 1:
                continue
            for way in range(2):
                chunk = way ^ phase
                ring[way, d - 1, chunk].wait_recv()
                if d < 3 or (d == 3 and phase == 0):
                    pass_on(way, d, chunk)
            for way in range(2):
                select(7 if d == 4 else 2 * d - 1 + way, way ^ phase)
            if d == 2 and phase == 1:
                absorb(0, 3)
        if d == 3:
            absorb(3, 2)
    absorb(5, 2)
    absorb(7, 1)

    def unpack(j, _):
        cols = pl.ds(pl.multiple_of(j * 1024, 1024), 1024)
        r.kv[:, cols] = nn(r.xe[...], r.u_v[:, cols]).astype(BF)
        return 0

    lax.fori_loop(0, 2, unpack, 0)
    middle(r.kv, r.query, r.bg, r.mix)

    def unproject(j, _):
        cols = pl.ds(pl.multiple_of(j * 512, 512), 512)
        r.rg[:, cols] = nt(r.kv[...], r.u_v[cols, :]).astype(BF)
        return 0

    returning = {}

    def scatter(half, *indices):
        for index in indices:
            zz = where(index)
            row = lax.broadcasted_iota(jnp.int32, (128, 256), 0)
            slot = (row // 32 * NZ + zz) * 32 + row % 32
            pick = jnp.concatenate(
                [(r.dsrc_v[e : e + 1, :] == slot).astype(F32).astype(BF) for e in range(3)], axis=1
            )
            r.bs[index, :, HALF[half]] = nn(pick, r.rg[:, HALF[half]]).astype(BF)
            cols = pl.ds(512 * half, 512)
            for k in (2, 1, 3):
                xx = (x + k) % NX
                sem = index * 8 + half * NX + k
                returning[index, half, k] = remote(
                    r.bs.at[index, pl.ds(pl.multiple_of(xx * 32, 32), 32), cols],
                    r.rback.at[index, land, cols], r.bsend.at[sem], r.brecv.at[sem], xx, z,
                )
            r.rback[index, land, HALF[half]] = r.bs[index, land, HALF[half]]

    def partial(index, half):
        for k in range(1, NX):
            returning[index, half, k].wait_recv()
        return nn(chosen(where(index)), r.rback[index, :, HALF[half]])

    flow = {}

    def push(way, i, chunk, value, wait):
        for sub in range(2):
            cols = pl.ds(512 * chunk + 256 * sub, 256)
            part = value[:, 256 * sub : 256 * sub + 256]
            if wait:
                flow[way, i + 1, chunk, sub].wait_recv()
                part = part + r.ins[way, i + 1, :, cols].astype(F32)
            r.outs[way, i, :, cols] = part.astype(BF)
            sem = way * 16 + i * 4 + chunk * 2 + sub
            flow[way, i, chunk, sub] = remote(
                r.outs.at[way, i, :, cols], r.ins.at[way, i, :, cols], r.qsend.at[sem], r.qrecv.at[sem],
                x, nexts[way],
            )

    def step(d, phase):
        for way in range(2):
            chunk = way ^ phase
            push(way, d - 1, chunk, partial(2 * d - way, chunk), d < 3 or phase == 0)

    lax.fori_loop(0, 1, unproject, 0)
    scatter(0, 7)
    lax.fori_loop(1, 2, unproject, 0)
    scatter(1, 7)
    scatter(1, 6)
    scatter(0, 5)
    push(0, 3, 0, partial(7, 0), False)
    push(1, 3, 1, partial(7, 1), False)
    scatter(0, 6)
    scatter(1, 5)
    scatter(1, 4)
    step(3, 1)
    scatter(0, 3)
    scatter(0, 4)
    scatter(1, 3)
    r.est_o[...] = r.grid_v[0:100, :].astype(F32) + nt(r.wf_v[...], r.mix[...])
    step(3, 0)
    scatter(1, 2)
    scatter(0, 1)
    scatter(0, 2)
    scatter(1, 1)
    step(2, 1)
    scatter(0, 0)
    scatter(1, 0)
    step(2, 0)
    step(1, 1)
    step(1, 0)
    part = jnp.concatenate([partial(0, 0), partial(0, 1)], axis=1)
    for way in range(2):
        for chunk in range(4):
            flow[way, 0, chunk // 2, chunk % 2].wait_recv()
    grad = part + r.ins[0, 0].astype(F32) + r.ins[1, 0].astype(F32)
    unit = r.unit[...]
    scaled = grad * r.dgain_v[...]
    first = jnp.mean(scaled, axis=-1, keepdims=True)
    second = jnp.mean(scaled * unit, axis=-1, keepdims=True)
    r.vert_o[...] = r.inv[:, 0:1] * (scaled - first - unit * second)
    rows.finish()
    weights.finish()
    for copy in sent + list(crossing.values()) + list(returning.values()) + list(flow.values()):
        copy.wait_send()


VM = pl.BlockSpec(memory_space=pltpu.VMEM)
OUT = (jax.ShapeDtypeStruct((100, 256), F32), jax.ShapeDtypeStruct((128, 1024), F32))


def hand_over(a_ref, b_ref, c_ref, d_ref):
    c_ref[...] = a_ref[...]
    d_ref[...] = b_ref[...]


def body(
    grid_in, mesh_embed, enc_src, enc_len, enc_kv_weight, proc_gain, qkv_weight, out_weight,
    dec_gain, unpack, wq, wf, dec_send, dec_src, dforecast,
):
    est, vert = pl.pallas_call(
        kernel,
        out_shape=OUT,
        in_specs=[pl.BlockSpec(memory_space=pl.ANY)] * 15,
        out_specs=(VM, VM),
        scratch_shapes=[pltpu.VMEM(*s) for s in SCRATCH.values()] + [DMA((n,)) for n in SEMS.values()],
        compiler_params=pltpu.CompilerParams(
            vmem_limit_bytes=60 * 2**20, collective_id=0, has_side_effects=True
        ),
    )(
        grid_in, mesh_embed, enc_src, enc_len.reshape(1, -1), enc_kv_weight, proc_gain.reshape(1, -1),
        qkv_weight.transpose(1, 0, 2), out_weight, dec_gain.reshape(1, -1), unpack, wq, wf, dec_send,
        dec_src, dforecast,
    )
    return pl.pallas_call(
        hand_over, out_shape=OUT, in_specs=[VM, VM], out_specs=(VM, VM)
    )(est, vert)


def solution(mesh):
    return jax.shard_map(
        body,
        mesh=mesh,
        in_specs=(
            P(None, ("grp", "head")), P(("grp", "head"), None), P(None, ("grp", "head")),
            P(("grp", "head")), P(), P(), P(None, None, "head"), P("head", None), P(), P(), P(), P(),
            P(("grp", "head"), None), P(None, ("grp", "head")), P(None, ("grp", "head")),
        ),
        out_specs=(P(None, ("grp", "head")), P(("grp", "head"), None)),
        check_vma=False,
    )
```
